32 devices in a mesh: groups: 2 (over y), sec: 4 (over z), term: 4 (over x, core).
Axes of the slice: x: 2, y: 2, z: 4, core: 2. Of those that a mesh axis runs over, the one named last changes fastest.
Arguments:
- psi: bfloat16 [64, 2, 16, 128, 128], P(('groups', 'sec')), parts along dimension 0, may hold values from -6 to 6
- left_env: bfloat16 [64, 16, 128, 128], P(('groups', 'sec'), 'term'), parts along dimension 0
- right_env: bfloat16 [64, 16, 128, 128], P(('groups', 'sec'), 'term'), parts along dimension 0
- local_ops: bfloat16 [8, 16, 16], replicated
- term_op: int32 [16], P('term'), may hold values from 0 to 7
- sector_rows: int32 [64], P('groups'), parts along dimension 0, may hold values from 64 to 128, as said below
- block_partner: int32 [64, 2], P(('groups', 'sec')), parts along dimension 0, may hold values from 0 to 31, as said below
- block_count: int32 [64], P(('groups', 'sec')), parts along dimension 0, may hold values from 1 to 2, as said below
Outputs:
- residual: bfloat16 [64, 2, 16, 128, 128], P(('groups', 'sec')), parts along dimension 0
- rayleigh: float32 [2], P('groups'), parts along dimension 0
The draws below stay inside these ranges and needn't reach their ends.
There are 2 independent parts, one for each index of `groups`. The reference program is written for one: setup_inputs(seed, part) draws one part's arguments, and reference() takes and returns one part's arrays. A program takes and returns all parts, laid end to end along the dimension named above; an argument that names none is the same for every part. Nothing has to cross between parts.
Inputs may be any that keep to these rules, and one draw needn't show every extreme that they name: `sector_rows`: some sector has all 128 rows live. `block_partner`: the 2 partner sectors of one left sector are distinct. `block_count`: some sector has all 2 blocks live.
All inputs are finite; a program needn't handle non-finite values.
Results may differ from the reference program's by a relative error of at most 0.0045.
Values may be sent and summed in bfloat16 or wider, within the bound.
No kernel may reach another device: no remote copies, remote signals or barrier semaphores. Data moves between devices by JAX's collectives and lax.ppermute only.
A program may use at most 192 MiB of HBM per device.

```python
import math
import jax
import jax.numpy as jnp
from jax import lax

B = 128
S = 16
QS = 32
NB = 2
NOPS = 8
TERMS = 16


def env_from(noise, scales, diagonal):
    ident = jnp.eye(B, dtype=jnp.float32)
    return (scales * (ident * diagonal + 0.5 * noise / math.sqrt(B))).astype(jnp.bfloat16)


def draw_left_env(key, part):
    key = jax.random.fold_in(key, 11)
    key_one, key_two, key_three = jax.random.split(key, 3)
    noise = jax.random.normal(key_one, (QS, TERMS, B, B), jnp.float32)
    scales = jnp.exp(jax.random.uniform(key_two, (QS, 1, 1, 1), jnp.float32, math.log(0.4), math.log(2.5)))
    diagonal = jax.random.uniform(key_three, (QS, TERMS, 1, B), jnp.float32, 0.5, 1.5)
    return env_from(noise, scales, diagonal)


def draw_right_env(key, part):
    key = jax.random.fold_in(key, 12)
    key_one, key_two, key_three = jax.random.split(key, 3)
    noise = jax.random.normal(key_one, (QS, TERMS, B, B), jnp.float32)
    scales = jnp.exp(jax.random.uniform(key_two, (QS, 1, 1, 1), jnp.float32, math.log(0.6), math.log(1.6)))
    diagonal = jax.random.uniform(key_three, (QS, TERMS, 1, B), jnp.float32, 0.5, 1.5)
    return env_from(noise, scales, diagonal)


def draw_local_ops(key, part):
    key = jax.random.fold_in(key, 13)
    key_one, key_two = jax.random.split(key, 2)
    noise = jax.random.normal(key_one, (NOPS, S, S), jnp.float32)
    diagonal = jax.random.uniform(key_two, (NOPS, 1, S), jnp.float32, 0.5, 1.5)
    ident = jnp.eye(S, dtype=jnp.float32)
    return ((ident * diagonal + 0.7 * noise / math.sqrt(S)) / math.sqrt(TERMS)).astype(jnp.bfloat16)


def draw_sector_rows(key, part):
    key = jax.random.fold_in(key, 14)
    key_one, key_two = jax.random.split(key, 2)
    counts = jax.random.randint(key_one, (QS,), max(1, B // 2), B + 1, dtype=jnp.int32)
    chosen = jax.random.randint(key_two, (), 0, QS, dtype=jnp.int32)
    return jnp.where(jnp.arange(QS, dtype=jnp.int32) == chosen, B, counts).astype(jnp.int32)


def draw_block_partner(key, part):
    key = jax.random.fold_in(key, 15)
    keys = jax.random.split(key, QS)
    orders = jax.vmap(lambda single: jax.random.permutation(single, QS))(keys)
    return orders[:, :NB].astype(jnp.int32)


def draw_block_count(key, part):
    key = jax.random.fold_in(key, 16)
    key_one, key_two = jax.random.split(key, 2)
    counts = jax.random.randint(key_one, (QS,), 1, NB + 1, dtype=jnp.int32)
    chosen = jax.random.randint(key_two, (), 0, QS, dtype=jnp.int32)
    return jnp.where(jnp.arange(QS, dtype=jnp.int32) == chosen, NB, counts).astype(jnp.int32)


def place_ends(values, own_key, smallest, high):
    spot = [jax.random.randint(jax.random.fold_in(own_key, axis), (), 0, length) for axis, length in enumerate(values.shape)]
    longest = values.shape.index(max(values.shape))
    next_to = spot[:longest] + [(spot[longest] + 1) % values.shape[longest]] + spot[longest + 1:]
    return values.at[tuple(spot)].set(smallest).at[tuple(next_to)].set(high)


def levels(rng, dims, cuts, low, high):
    level = 1.0
    for dim, parts in cuts:
        steps = jax.random.uniform(jax.random.fold_in(jax.random.fold_in(rng, 6), dim), (parts,), jnp.float32, low / len(cuts), high / len(cuts))
        level = level * jnp.repeat(jnp.exp(steps), dims[dim] // parts).reshape((-1,) + (1,) * (len(dims) - 1 - dim))
    return level


def centred(stream_key, extent, scale, reach, pieces=(), kind=jnp.bfloat16):
    drawn = jax.random.normal(stream_key, extent, jnp.float32) * scale
    if len(pieces) > 0:
        drawn = levels(stream_key, extent, pieces, -0.22, 0.18) * drawn
    return jnp.clip(drawn, min=-reach, max=reach).astype(kind)


def setup_inputs(seed: int = 0, part: int = 0) -> dict:
    splits = jax.random.split(jax.random.key(seed), 9)
    own_keys = jax.random.split(jax.random.fold_in(splits[8], part), 9)
    return {
        "psi": centred(own_keys[0], (QS, NB, S, B, B), 1.0, 6.0, ((0, 4),)),
        "left_env": draw_left_env(jax.random.fold_in(jax.random.fold_in(splits[8], part), 71), part),
        "right_env": draw_right_env(jax.random.fold_in(jax.random.fold_in(splits[8], part), 71), part),
        "local_ops": draw_local_ops(jax.random.fold_in(splits[8], 71), part),
        "term_op": place_ends(jax.random.randint(splits[4], (TERMS,), 0, NOPS), jax.random.fold_in(splits[4], 1), 0, NOPS - 1).astype(jnp.int32),
        "sector_rows": draw_sector_rows(jax.random.fold_in(jax.random.fold_in(splits[8], part), 71), part),
        "block_partner": draw_block_partner(jax.random.fold_in(jax.random.fold_in(splits[8], part), 71), part),
        "block_count": draw_block_count(jax.random.fold_in(jax.random.fold_in(splits[8], part), 71), part),
    }


def reference(psi, left_env, right_env, local_ops, term_op, sector_rows, block_partner, block_count):
    rows_iota = jnp.arange(B, dtype=jnp.int32)
    partner_rows = sector_rows[block_partner]
    live_block = jnp.arange(NB, dtype=jnp.int32)[None, :] < block_count[:, None]
    live_left = rows_iota[None, :] < sector_rows[:, None]
    live_right = rows_iota[None, None, :] < partner_rows[:, :, None]
    live_mask = live_block[:, :, None, None, None] & live_left[:, None, None, :, None] & live_right[:, :, None, None, :]
    psi_live = jnp.where(live_mask, psi, jnp.zeros((), jnp.bfloat16))
    term_ops = local_ops[term_op]
    psi_wide = psi_live.astype(jnp.float32)

    def add_term(summed, term_index):
        left_terms = left_env[:, term_index].astype(jnp.float32)
        right_terms = right_env[block_partner, term_index].astype(jnp.float32)
        after_left = jnp.einsum("qxa,qnsab->qnsxb", left_terms, psi_wide).astype(jnp.bfloat16)
        after_ops = jnp.einsum("ts,qnsxb->qntxb", term_ops[term_index].astype(jnp.float32), after_left.astype(jnp.float32)).astype(jnp.bfloat16)
        summed = summed + jnp.einsum("qntxb,qnby->qntxy", after_ops.astype(jnp.float32), right_terms)
        return summed, None

    summed, unused = lax.scan(add_term, jnp.zeros(psi.shape, jnp.float32), jnp.arange(TERMS, dtype=jnp.int32))
    summed = jnp.where(live_mask, summed, jnp.zeros((), jnp.float32))
    numerator = jnp.sum(summed * psi_wide)
    denominator = jnp.sum(psi_wide * psi_wide)
    rayleigh = numerator / denominator
    residual = (summed - rayleigh * psi_wide).astype(jnp.bfloat16)
    return residual, rayleigh.reshape(1)
```

```python
import functools

import jax
import jax.numpy as jnp
from jax import lax
from jax.experimental import pallas as pl
from jax.experimental.pallas import tpu as pltpu
from jax.sharding import PartitionSpec as P

TILE = 16
WIDE = 2


def block_facts(meta, sector_rows, partners, counts, sector, slot):
    live = slot < counts[sector]
    own_rows = sector_rows[meta[0] + sector]
    partner_rows = sector_rows[partners[sector, slot]]
    return live, own_rows, partner_rows


def live_entries(own_rows, partner_rows, width):
    left = lax.broadcasted_iota(jnp.int32, (1, width, width), 1) < own_rows
    right = lax.broadcasted_iota(jnp.int32, (1, width, width), 2) < partner_rows
    return left & right


def folded(values):
    states, width = values.shape[0], values.shape[-1]
    return jnp.sum(values.reshape(states * width // 8, 8, width), axis=0)


def chunk_kernel(
    first, last, terms, chunk, half, slots,
    meta, term_ops, sector_rows, partners, counts,
    psi_ref, ops_ref, *rest,
):
    left_refs, rest = rest[:terms], rest[terms:]
    right_refs, rest = rest[:terms], rest[terms:]
    if first:
        sum_in = None
    else:
        sum_in, rest = rest[0], rest[1:]
    sum_out, rest = rest[0], rest[1:]
    if first:
        square_out, rest = rest[0], rest[1:]
    if last:
        inner_out, rest = rest[0], rest[1:]
    spread_ops, left_all, right_all, live_psi, after_left, after_ops, *rest = rest
    if first:
        total = sum_out
    elif last:
        total = sum_in
    else:
        total = sum_out

    states, width = psi_ref.shape[0], psi_ref.shape[-1]
    groups = width // TILE
    step = pl.program_id(0)
    sector = meta[1] * half + step // slots
    slot = lax.rem(step, slots)
    live, own_rows, partner_rows = block_facts(
        meta, sector_rows, partners, counts, sector, slot
    )
    me = meta[2]

    @pl.when(step == 0)
    def _():
        wide = states * TILE
        row_state = lax.broadcasted_iota(jnp.int32, (wide, width), 0) // TILE
        column = lax.broadcasted_iota(jnp.int32, (wide, width), 1)
        pick_rows = (row_state == column).astype(jnp.bfloat16)
        row = lax.broadcasted_iota(jnp.int32, (width, wide), 0)
        column_state = lax.broadcasted_iota(jnp.int32, (width, wide), 1) // TILE
        pick_columns = (row == column_state).astype(jnp.bfloat16)
        inner_row = lax.rem(lax.broadcasted_iota(jnp.int32, (wide, wide), 0), TILE)
        inner_column = lax.rem(lax.broadcasted_iota(jnp.int32, (wide, wide), 1), TILE)
        for term in range(terms):
            operator = ops_ref[term_ops[me ^ term, chunk]]
            rows = jnp.dot(pick_rows, operator, preferred_element_type=jnp.float32)
            full = jnp.dot(
                rows.astype(jnp.bfloat16), pick_columns, preferred_element_type=jnp.float32
            )
            spread_ops[term] = jnp.where(inner_row == inner_column, full, 0.0).astype(
                jnp.bfloat16
            )
        if first:
            square_out[...] = jnp.zeros_like(square_out)
        if last:
            inner_out[...] = jnp.zeros_like(inner_out)

    @pl.when(live)
    def _():
        for source in range(terms):
            place = pl.ds(pl.multiple_of((me ^ source) * width, width), width)
            left_all[place, :] = left_refs[source][...]
            right_all[place, :] = right_refs[source][...]
        mask = live_entries(own_rows, partner_rows, width)
        live_psi[...] = jnp.where(mask, psi_ref[...], jnp.zeros((), jnp.bfloat16))
        if first:
            wide_psi = live_psi[...].astype(jnp.float32)
            square_out[...] += folded(wide_psi * wide_psi)
        lefts = left_all[...]
        for pair in range(states // WIDE):
            columns = jnp.concatenate(
                [live_psi[pair * WIDE + at] for at in range(WIDE)], axis=1
            )
            done = jnp.dot(lefts, columns, preferred_element_type=jnp.float32).astype(
                jnp.bfloat16
            )
            for term in range(terms):
                for at in range(WIDE):
                    state = pair * WIDE + at
                    after_left[term, :, state * TILE : (state + 1) * TILE, :] = done[
                        term * width : (term + 1) * width, at * width : (at + 1) * width
                    ].reshape(groups, TILE, width)

        def operate(low, high):
            for group in range(low, high, WIDE):
                for term in range(terms):
                    columns = jnp.concatenate(
                        [after_left[term, group + at] for at in range(WIDE)], axis=1
                    )
                    done = jnp.dot(
                        spread_ops[term], columns, preferred_element_type=jnp.float32
                    ).astype(jnp.bfloat16)
                    for at in range(WIDE):
                        after_ops[group + at, :, term * width : (term + 1) * width] = done[
                            :, at * width : (at + 1) * width
                        ]
            for group in range(low, high, WIDE):
                rows = jnp.concatenate(
                    [after_ops[group + at] for at in range(WIDE)], axis=0
                )
                done = jnp.dot(rows, right_all[...], preferred_element_type=jnp.float32)
                done = done.reshape(WIDE, states, TILE, width)
                for at in range(WIDE):
                    place = slice((group + at) * TILE, (group + at + 1) * TILE)
                    if first:
                        total[:, place, :] = done[at]
                    else:
                        total[:, place, :] = sum_in[:, place, :] + done[at]

        always = min(groups, 4)
        operate(0, always)
        for group in range(always, groups, WIDE):
            pl.when(own_rows > group * TILE)(functools.partial(operate, group, group + WIDE))

        if last:
            kept = jnp.where(mask, total[...], 0.0)
            inner_out[...] += folded(kept * live_psi[...].astype(jnp.float32))
            sum_out[...] = kept.astype(jnp.bfloat16)

    if last:
        @pl.when(jnp.logical_not(live))
        def _():
            sum_out[...] = jnp.zeros_like(sum_out)


def chunk_call(first, last, chunk, scalars, psi, ops, lefts, rights, total):
    terms = len(lefts)
    half = lefts[0].shape[0]
    slots, states, width = psi.shape[1], psi.shape[2], psi.shape[3]
    blocks = half * slots
    psi_spec = pl.BlockSpec(
        (None, None, states, width, width),
        lambda i, meta, *_: (meta[1] * half + i // slots, i % slots, 0, 0, 0),
    )
    ops_spec = pl.BlockSpec(ops.shape, lambda i, *_: (0, 0, 0))
    left_spec = pl.BlockSpec(
        (None, None, width, width), lambda i, *_: (i // slots, chunk, 0, 0)
    )
    right_spec = pl.BlockSpec((None, width, width), lambda i, *_: (i, 0, 0))
    sum_spec = pl.BlockSpec((None, states, width, width), lambda i, *_: (i, 0, 0, 0))
    fold_spec = pl.BlockSpec((8, width), lambda i, *_: (0, 0))
    fold_shape = jax.ShapeDtypeStruct((8, width), jnp.float32)
    in_specs = [psi_spec, ops_spec] + [left_spec] * terms + [right_spec] * terms
    operands = [psi, ops, *lefts, *rights]
    aliases = {}
    if not first:
        in_specs.append(sum_spec)
        operands.append(total)
        if not last:
            aliases = {len(scalars) + len(operands) - 1: 0}
    sum_dtype = jnp.bfloat16 if last else jnp.float32
    out_specs = [sum_spec]
    out_shape = [jax.ShapeDtypeStruct((blocks, states, width, width), sum_dtype)]
    if first or last:
        out_specs.append(fold_spec)
        out_shape.append(fold_shape)
    wide = states * TILE
    work = blocks * states * width * width * terms * 2 * (2 * width + wide)
    return pl.pallas_call(
        functools.partial(chunk_kernel, first, last, terms, chunk, half, slots),
        grid_spec=pltpu.PrefetchScalarGridSpec(
            num_scalar_prefetch=len(scalars),
            grid=(blocks,),
            in_specs=in_specs,
            out_specs=out_specs,
            scratch_shapes=[
                pltpu.VMEM((terms, wide, wide), jnp.bfloat16),
                pltpu.VMEM((terms * width, width), jnp.bfloat16),
                pltpu.VMEM((terms * width, width), jnp.bfloat16),
                pltpu.VMEM((states, width, width), jnp.bfloat16),
                pltpu.VMEM((terms, width // TILE, wide, width), jnp.bfloat16),
                pltpu.VMEM((width // TILE, wide, terms * width), jnp.bfloat16),
            ],
        ),
        out_shape=out_shape,
        input_output_aliases=aliases,
        compiler_params=pltpu.CompilerParams(vmem_limit_bytes=56 * 1024 * 1024),
        cost_estimate=pl.CostEstimate(
            flops=work, bytes_accessed=3 * blocks * states * width * width * 4, transcendentals=0
        ),
        name="terms",
    )(*scalars, *operands)


def residual_kernel(slots, half, meta, sector_rows, partners, counts,
                    quotient, psi_ref, own_ref, other_ref, out_ref):
    width = psi_ref.shape[-1]
    step = pl.program_id(0)
    here = step < half * slots
    sector = lax.rem(meta[1] * half + step // slots, 2 * half)
    slot = lax.rem(step, slots)
    live, own_rows, partner_rows = block_facts(
        meta, sector_rows, partners, counts, sector, slot
    )
    mask = live_entries(jnp.where(live, own_rows, 0), partner_rows, width)
    scaled = quotient[0] * jnp.where(mask, psi_ref[...].astype(jnp.float32), 0.0)

    @pl.when(here)
    def _():
        out_ref[...] = (own_ref[...].astype(jnp.float32) - scaled).astype(jnp.bfloat16)

    @pl.when(jnp.logical_not(here))
    def _():
        out_ref[...] = (other_ref[...].astype(jnp.float32) - scaled).astype(jnp.bfloat16)


def residual_call(scalars, quotient, psi, own, other):
    sectors, slots, states, width = psi.shape[:4]
    half = sectors // 2
    blocks = half * slots
    whole = (None, None, states, width, width)

    def at_sector(i, meta, *_):
        return ((meta[1] * half + i // slots) % sectors, i % slots, 0, 0, 0)

    one = (None, states, width, width)
    return pl.pallas_call(
        functools.partial(residual_kernel, slots, half),
        grid_spec=pltpu.PrefetchScalarGridSpec(
            num_scalar_prefetch=len(scalars),
            grid=(2 * blocks,),
            in_specs=[
                pl.BlockSpec(memory_space=pltpu.SMEM),
                pl.BlockSpec(whole, at_sector),
                pl.BlockSpec(one, lambda i, *_: (jnp.minimum(i, blocks - 1), 0, 0, 0)),
                pl.BlockSpec(one, lambda i, *_: (jnp.maximum(i - blocks, 0), 0, 0, 0)),
            ],
            out_specs=pl.BlockSpec(whole, at_sector),
        ),
        out_shape=jax.ShapeDtypeStruct(psi.shape, jnp.bfloat16),
        compiler_params=pltpu.CompilerParams(vmem_limit_bytes=32 * 1024 * 1024),
        cost_estimate=pl.CostEstimate(
            flops=3 * psi.size, bytes_accessed=6 * psi.size, transcendentals=0
        ),
        name="residual",
    )(*scalars, quotient, psi, own, other)


def on_device(
    devices, psi, left_env, right_env, local_ops, term_op, sector_rows, block_partner, block_count
):
    sectors, slots, states, width = psi.shape[:4]
    chunks = left_env.shape[1]
    half = sectors // 2
    me = lax.axis_index("term")
    core = me % 2
    meta = jnp.stack([lax.axis_index("sec") * sectors, core, me]).astype(jnp.int32)

    def swap(value, bits):
        return lax.ppermute(value, "term", [(i, i ^ bits) for i in range(devices)])

    def half_of(value, bits):
        return lax.dynamic_slice_in_dim(value, (core ^ (bits & 1)) * half, half)

    term_ops = jnp.stack([term_op] + [swap(term_op, bits) for bits in range(1, devices)])
    lefts = [half_of(left_env, 0)]
    lefts += [swap(half_of(left_env, bits), bits) for bits in range(1, devices)]
    ops = jnp.zeros((local_ops.shape[0], width, width), jnp.bfloat16)
    ops = lax.dynamic_update_slice(ops, local_ops, (0, 0, 0))
    scalars = (meta, term_ops, sector_rows, block_partner, block_count)
    wanted = [half_of(block_partner, bits).reshape(-1) for bits in range(2)]

    total = None
    for chunk in range(chunks):
        every = lax.all_gather(right_env[:, chunk], "sec", axis=0, tiled=True)
        chosen = [every[wanted[bits]] for bits in range(2)]
        rights = [chosen[0]]
        rights += [swap(chosen[bits & 1], bits) for bits in range(1, devices)]
        first, last = chunk == 0, chunk == chunks - 1
        total, *folds = chunk_call(
            first, last, chunk, scalars, psi, ops, lefts, rights, total
        )
        if first:
            squares = folds[0]
        if last:
            products = folds[0]

    other = swap(total, 1)
    numerator, denominator = lax.psum(
        (jnp.sum(products), jnp.sum(squares)), ("sec", "term")
    )
    rayleigh = (numerator / denominator).reshape(1)
    scalars = (meta, sector_rows, block_partner, block_count)
    residual = residual_call(scalars, rayleigh, psi, total, other)
    return residual, rayleigh


def solution(mesh):
    placed = (
        P(("groups", "sec"), None, None, None, None),
        P(("groups", "sec"), "term", None, None),
        P(("groups", "sec"), "term", None, None),
        P(),
        P("term"),
        P("groups"),
        P(("groups", "sec"), None),
        P(("groups", "sec")),
    )
    return jax.shard_map(
        functools.partial(on_device, mesh.shape["term"]),
        mesh=mesh,
        in_specs=placed,
        out_specs=(P(("groups", "sec"), None, None, None, None), P("groups")),
        check_vma=False,
    )
```

```python
import functools

import jax
import jax.numpy as jnp
from jax import lax
from jax.experimental import pallas as pl
from jax.experimental.pallas import tpu as pltpu
from jax.sharding import PartitionSpec as P

TILE = 16
WIDE = 2
MIB = 1024 * 1024


def block_facts(meta, sector_rows, partners, counts, sector, slot):
    live = slot < counts[sector]
    own_rows = sector_rows[meta[0] + sector]
    partner_rows = sector_rows[partners[sector, slot]]
    return live, own_rows, partner_rows


def live_entries(own_rows, partner_rows, width):
    left = lax.broadcasted_iota(jnp.int32, (1, width, width), 1) < own_rows
    right = lax.broadcasted_iota(jnp.int32, (1, width, width), 2) < partner_rows
    return left & right


def folded(values):
    states, width = values.shape[0], values.shape[-1]
    return jnp.sum(values.reshape(states * width // 8, 8, width), axis=0)


def by_live_rows(own_rows, groups, work):
    always = groups // 2
    work(0, always)
    for group in range(always, groups, WIDE):
        pl.when(own_rows > group * TILE)(functools.partial(work, group, group + WIDE))


def left_kernel(first, terms, half, slots, meta, sector_rows, partners, counts,
                psi_ref, left_ref, ops_ref, after_ref, out_ref, token_ref, *rest):
    if first:
        square_ref, rest = rest[0], rest[1:]
    spread_ops, live_psi, after_left = rest
    states, width = psi_ref.shape[0], psi_ref.shape[-1]
    groups = width // TILE
    step = pl.program_id(0)
    sector = meta[1] * half + step // slots
    slot = lax.rem(step, slots)
    live, own_rows, partner_rows = block_facts(
        meta, sector_rows, partners, counts, sector, slot
    )

    @pl.when(step == 0)
    def _():
        wide = states * TILE
        row_state = lax.broadcasted_iota(jnp.int32, (wide, states), 0) // TILE
        column = lax.broadcasted_iota(jnp.int32, (wide, states), 1)
        pick_rows = (row_state == column).astype(jnp.bfloat16)
        row = lax.broadcasted_iota(jnp.int32, (width, wide), 0)
        column_state = lax.broadcasted_iota(jnp.int32, (width, wide), 1) // TILE
        pick_columns = (row == column_state).astype(jnp.bfloat16)
        inner_row = lax.rem(lax.broadcasted_iota(jnp.int32, (wide, wide), 0), TILE)
        inner_column = lax.rem(lax.broadcasted_iota(jnp.int32, (wide, wide), 1), TILE)
        for term in range(terms):
            operator = ops_ref[term * states : (term + 1) * states, :]
            rows = jnp.dot(pick_rows, operator, preferred_element_type=jnp.float32)
            full = jnp.dot(
                rows.astype(jnp.bfloat16), pick_columns, preferred_element_type=jnp.float32
            )
            spread_ops[term] = jnp.where(inner_row == inner_column, full, 0.0).astype(
                jnp.bfloat16
            )
        token_ref[...] = jnp.zeros_like(token_ref)
        if first:
            square_ref[...] = jnp.zeros_like(square_ref)

    @pl.when(live)
    def _():
        mask = live_entries(own_rows, partner_rows, width)
        live_psi[...] = jnp.where(mask, psi_ref[...], jnp.zeros((), jnp.bfloat16))
        if first:
            wide_psi = live_psi[...].astype(jnp.float32)
            square_ref[...] += folded(wide_psi * wide_psi)
        lefts = left_ref[...]
        for pair in range(states // WIDE):
            columns = jnp.concatenate(
                [live_psi[pair * WIDE + at] for at in range(WIDE)], axis=1
            )
            done = jnp.dot(lefts, columns, preferred_element_type=jnp.float32).astype(
                jnp.bfloat16
            )
            for term in range(terms):
                for at in range(WIDE):
                    state = pair * WIDE + at
                    after_left[term, :, state * TILE : (state + 1) * TILE, :] = done[
                        term * width : (term + 1) * width, at * width : (at + 1) * width
                    ].reshape(groups, TILE, width)

        def operate(low, high):
            for group in range(low, high, WIDE):
                for term in range(terms):
                    columns = jnp.concatenate(
                        [after_left[term, group + at] for at in range(WIDE)], axis=1
                    )
                    done = jnp.dot(
                        spread_ops[term], columns, preferred_element_type=jnp.float32
                    ).astype(jnp.bfloat16)
                    for at in range(WIDE):
                        out_ref[term, group + at] = done[:, at * width : (at + 1) * width]

        by_live_rows(own_rows, groups, operate)


def psi_spec_of(psi, half):
    slots, states, width = psi.shape[1:4]
    return pl.BlockSpec(
        (None, None, states, width, width),
        lambda i, meta, *_: (meta[1] * half + i // slots, i % slots, 0, 0, 0),
    )


def left_call(first, terms, scalars, psi, payload, after):
    sectors, slots, states, width = psi.shape[:4]
    half = sectors // 2
    blocks, groups, wide = half * slots, width // TILE, states * TILE
    ops_at = half * width // states
    fold_spec = pl.BlockSpec((8, width), lambda i, *_: (0, 0))
    fold_shape = jax.ShapeDtypeStruct((8, width), jnp.float32)
    extra = 1 + int(first)
    work = 2 * blocks * terms * states * width * width * (width + wide)
    return pl.pallas_call(
        functools.partial(left_kernel, first, terms, half, slots),
        grid_spec=pltpu.PrefetchScalarGridSpec(
            num_scalar_prefetch=len(scalars),
            grid=(blocks,),
            in_specs=[
                psi_spec_of(psi, half),
                pl.BlockSpec((terms * width, width), lambda i, *_: (i // slots, 0)),
                pl.BlockSpec((terms * states, width), lambda i, *_: (ops_at, 0)),
                pl.BlockSpec(memory_space=pl.ANY),
            ],
            out_specs=[
                pl.BlockSpec(
                    (None, terms, groups, wide, width), lambda i, *_: (i, 0, 0, 0, 0)
                )
            ] + [fold_spec] * extra,
            scratch_shapes=[
                pltpu.VMEM((terms, wide, wide), jnp.bfloat16),
                pltpu.VMEM((states, width, width), jnp.bfloat16),
                pltpu.VMEM((terms, groups, wide, width), jnp.bfloat16),
            ],
        ),
        out_shape=[
            jax.ShapeDtypeStruct((blocks, terms, groups, wide, width), jnp.bfloat16)
        ] + [fold_shape] * extra,
        compiler_params=pltpu.CompilerParams(vmem_limit_bytes=48 * MIB),
        cost_estimate=pl.CostEstimate(
            flops=work,
            bytes_accessed=2 * blocks * (terms + 1) * states * width * width,
            transcendentals=0,
        ),
        name="left",
    )(*scalars, psi, payload, payload, after)


def choose_kernel(devices, sectors, half, slots, meta, partners, after_ref, *rest):
    shards, (mine_ref, other_ref, token_ref, mine_sem, other_sem) = rest[:devices], rest[devices:]
    token_ref[...] = jnp.zeros_like(token_ref)
    for part, (out_ref, sem) in enumerate(((mine_ref, mine_sem), (other_ref, other_sem))):
        for block in range(half * slots):
            sector = (meta[1] ^ part) * half + block // slots
            partner = partners[sector, block % slots]
            away = lax.rem(meta[3] + devices - partner // sectors, devices)
            place = lax.rem(partner, sectors)
            for distance in range(devices):
                @pl.when(away == distance)
                def _(distance=distance, place=place, block=block, out_ref=out_ref, sem=sem):
                    pltpu.make_async_copy(
                        shards[distance].at[place], out_ref.at[block], sem
                    ).start()
    pltpu.make_async_copy(mine_ref, mine_ref, mine_sem).wait()
    pltpu.make_async_copy(other_ref, other_ref, other_sem).wait()


def choose_call(scalars, slots, shards, after):
    meta, _, partners, _ = scalars
    sectors, terms, width = shards[0].shape[:3]
    half = sectors // 2
    chosen = jax.ShapeDtypeStruct((half * slots, terms, width, width), jnp.bfloat16)
    anywhere = pl.BlockSpec(memory_space=pl.ANY)
    return pl.pallas_call(
        functools.partial(choose_kernel, len(shards), sectors, half, slots),
        grid_spec=pltpu.PrefetchScalarGridSpec(
            num_scalar_prefetch=2,
            grid=(1,),
            in_specs=[anywhere] * (1 + len(shards)),
            out_specs=[anywhere, anywhere, pl.BlockSpec((8, width), lambda i, *_: (0, 0))],
            scratch_shapes=[pltpu.SemaphoreType.DMA, pltpu.SemaphoreType.DMA],
        ),
        out_shape=[chosen, chosen, jax.ShapeDtypeStruct((8, width), jnp.float32)],
        cost_estimate=pl.CostEstimate(
            flops=0, bytes_accessed=8 * half * slots * terms * width * width, transcendentals=0
        ),
        name="choose",
    )(meta, partners, after, *shards)


def right_kernel(first, last, devices, half, slots, meta, sector_rows, partners, counts,
                 after_ref, *rest):
    if last:
        psi_ref, rest = rest[0], rest[1:]
    ops_refs, rest = rest[:devices], rest[devices:]
    right_refs, rest = rest[:devices], rest[devices:]
    if not first:
        sum_in, rest = rest[0], rest[1:]
    sum_out, fold_ref = rest[:2]
    terms, groups, wide, width = ops_refs[0].shape
    states = wide // TILE
    total = rest[2] if last else sum_out
    step = pl.program_id(0)
    sector = meta[1] * half + step // slots
    slot = lax.rem(step, slots)
    live, own_rows, partner_rows = block_facts(
        meta, sector_rows, partners, counts, sector, slot
    )

    @pl.when(step == 0)
    def _():
        fold_ref[...] = jnp.zeros_like(fold_ref)

    @pl.when(live)
    def _():
        columns = [
            jnp.concatenate(
                [right_refs[pair + at][term] for at in range(2) for term in range(terms)], axis=0
            )
            for pair in range(0, devices, 2)
        ]

        def multiply(low, high):
            for group in range(low, high, WIDE):
                parts = []
                for pair in range(0, devices, 2):
                    rows = jnp.concatenate(
                        [
                            jnp.concatenate(
                                [
                                    ops_refs[pair + at][term, group + side]
                                    for at in range(2)
                                    for term in range(terms)
                                ],
                                axis=1,
                            )
                            for side in range(WIDE)
                        ],
                        axis=0,
                    )
                    parts.append(
                        jnp.dot(rows, columns[pair // 2], preferred_element_type=jnp.float32)
                    )
                while len(parts) > 1:
                    parts = [parts[at] + parts[at + 1] for at in range(0, len(parts), 2)]
                done = parts[0].reshape(WIDE, states, TILE, width)
                for side in range(WIDE):
                    place = slice((group + side) * TILE, (group + side + 1) * TILE)
                    if first:
                        total[:, place, :] = done[side]
                    else:
                        total[:, place, :] = sum_in[:, place, :] + done[side]

        by_live_rows(own_rows, groups, multiply)
        if last:
            mask = live_entries(own_rows, partner_rows, width)
            kept = jnp.where(mask, total[...], 0.0)
            fold_ref[...] += folded(kept * psi_ref[...].astype(jnp.float32))
            sum_out[...] = kept.astype(jnp.bfloat16)

    if last:
        @pl.when(jnp.logical_not(live))
        def _():
            sum_out[...] = jnp.zeros_like(sum_out)


def right_call(first, last, chunk, scalars, psi, after_ops, rights, total, after):
    devices = len(rights)
    sectors, slots, states, width = psi.shape[:4]
    half = sectors // 2
    blocks, groups, wide = half * slots, width // TILE, states * TILE
    start, terms = chunk
    sum_spec = pl.BlockSpec((None, states, width, width), lambda i, *_: (i, 0, 0, 0))
    in_specs = [pl.BlockSpec(memory_space=pl.ANY)]
    operands = [after]
    if last:
        in_specs.append(psi_spec_of(psi, half))
        operands.append(psi)
    in_specs += [
        pl.BlockSpec(
            (None, terms, groups, wide, width), lambda i, *_: (i, start // terms, 0, 0, 0)
        )
    ] * devices
    operands += after_ops
    in_specs += [pl.BlockSpec((None, terms, width, width), lambda i, *_: (i, 0, 0, 0))] * devices
    operands += rights
    aliases = {}
    if not first:
        in_specs.append(sum_spec)
        operands.append(total)
        if not last:
            aliases = {len(scalars) + len(operands) - 1: 0}
    sum_dtype = jnp.bfloat16 if last else jnp.float32
    size = blocks * states * width * width
    return pl.pallas_call(
        functools.partial(right_kernel, first, last, devices, half, slots),
        grid_spec=pltpu.PrefetchScalarGridSpec(
            num_scalar_prefetch=len(scalars),
            grid=(blocks,),
            in_specs=in_specs,
            out_specs=[sum_spec, pl.BlockSpec((8, width), lambda i, *_: (0, 0))],
            scratch_shapes=[pltpu.VMEM((states, width, width), jnp.float32)] if last else [],
        ),
        out_shape=[
            jax.ShapeDtypeStruct((blocks, states, width, width), sum_dtype),
            jax.ShapeDtypeStruct((8, width), jnp.float32),
        ],
        input_output_aliases=aliases,
        compiler_params=pltpu.CompilerParams(vmem_limit_bytes=48 * MIB),
        cost_estimate=pl.CostEstimate(
            flops=2 * size * devices * terms * width,
            bytes_accessed=size * (8 + 2 * devices * terms),
            transcendentals=0,
        ),
        name="right",
    )(*scalars, *operands)


def residual_kernel(slots, half, meta, sector_rows, partners, counts,
                    folds_ref, psi_ref, own_ref, other_ref, out_ref, quotient_ref):
    width = psi_ref.shape[-1]
    step = pl.program_id(0)
    here = step < half * slots
    sector = lax.rem(meta[1] * half + step // slots, 2 * half)
    slot = lax.rem(step, slots)
    live, own_rows, partner_rows = block_facts(
        meta, sector_rows, partners, counts, sector, slot
    )

    @pl.when(step == 0)
    def _():
        quotient_ref[0] = jnp.sum(folds_ref[0:8, :]) / jnp.sum(folds_ref[8:16, :])

    mask = live_entries(jnp.where(live, own_rows, 0), partner_rows, width)
    scaled = quotient_ref[0] * jnp.where(mask, psi_ref[...].astype(jnp.float32), 0.0)

    @pl.when(here)
    def _():
        out_ref[...] = (own_ref[...].astype(jnp.float32) - scaled).astype(jnp.bfloat16)

    @pl.when(jnp.logical_not(here))
    def _():
        out_ref[...] = (other_ref[...].astype(jnp.float32) - scaled).astype(jnp.bfloat16)


def residual_call(scalars, folds, psi, own, other):
    sectors, slots, states, width = psi.shape[:4]
    half = sectors // 2
    blocks = half * slots
    whole = (None, None, states, width, width)

    def at_sector(i, meta, *_):
        return ((meta[1] * half + i // slots) % sectors, i % slots, 0, 0, 0)

    one = (None, states, width, width)
    return pl.pallas_call(
        functools.partial(residual_kernel, slots, half),
        grid_spec=pltpu.PrefetchScalarGridSpec(
            num_scalar_prefetch=len(scalars),
            grid=(2 * blocks,),
            in_specs=[
                pl.BlockSpec(folds.shape, lambda i, *_: (0, 0)),
                pl.BlockSpec(whole, at_sector),
                pl.BlockSpec(one, lambda i, *_: (jnp.minimum(i, blocks - 1), 0, 0, 0)),
                pl.BlockSpec(one, lambda i, *_: (jnp.maximum(i - blocks, 0), 0, 0, 0)),
            ],
            out_specs=[pl.BlockSpec(whole, at_sector), pl.BlockSpec(memory_space=pltpu.SMEM)],
        ),
        out_shape=[
            jax.ShapeDtypeStruct(psi.shape, jnp.bfloat16),
            jax.ShapeDtypeStruct((1,), jnp.float32),
        ],
        compiler_params=pltpu.CompilerParams(vmem_limit_bytes=32 * MIB),
        cost_estimate=pl.CostEstimate(
            flops=3 * psi.size, bytes_accessed=6 * psi.size, transcendentals=0
        ),
        name="residual",
    )(*scalars, folds, psi, own, other)


def on_device(
    devices, rings, psi, left_env, right_env, local_ops, term_op, sector_rows, block_partner,
    block_count,
):
    sectors, slots, states, width = psi.shape[:4]
    terms = left_env.shape[1]
    half = sectors // 2
    me = lax.axis_index("term")
    ring = lax.axis_index("sec")
    core = me % 2
    meta = jnp.stack([ring * sectors, core, me, ring]).astype(jnp.int32)
    scalars = (meta, sector_rows, block_partner, block_count)

    def swap(value, bits, axis="term", size=devices):
        return lax.ppermute(value, axis, [(i, i ^ bits) for i in range(size)])

    chunks = [(at, 1) for at in range(terms)]
    shards = []
    for start, length in chunks:
        own = right_env[:, start : start + length]
        moved = [own]
        for distance in range(1, rings):
            pairs = [(i, (i + distance) % rings) for i in range(rings)]
            moved.append(lax.ppermute(own, "sec", pairs))
        shards.append(moved)

    picker = term_op[:, None] == jnp.arange(local_ops.shape[0], dtype=jnp.int32)[None, :]
    picked = jnp.sum(
        jnp.where(picker[:, :, None, None], local_ops[None], jnp.zeros((), jnp.bfloat16)), axis=1
    )
    padded = jnp.pad(picked, ((0, 0), (0, 0), (0, width - states))).reshape(terms * states, width)
    payloads = []
    for bits in range(2):
        rows = lax.dynamic_slice_in_dim(left_env, (core ^ bits) * half, half)
        payloads.append(jnp.concatenate([rows.reshape(-1, width), padded], axis=0))
    lefts = [payloads[0]] + [swap(payloads[bits & 1], bits) for bits in range(1, devices)]

    token = jnp.zeros((8, width), jnp.float32)
    after_ops, chosen, rights = [], [], []

    def choose(token):
        mine, other, token = choose_call(scalars, slots, shards[len(rights)], token)
        both = (mine, other)
        rights.append([mine] + [swap(both[bits & 1], bits) for bits in range(1, devices)])
        return token

    for source in range(devices):
        done, token, *folds = left_call(
            source == 0, terms, scalars, psi, lefts[source], token
        )
        after_ops.append(done)
        if source == 0:
            squares = folds[0]
        if 1 <= source < devices - 1 and len(rights) < len(chunks):
            token = choose(token)
    total = None
    for at, chunk in enumerate(chunks):
        if at == len(rights):
            token = choose(token)
        last = at == len(chunks) - 1
        total, token = right_call(
            at == 0, last, chunk, scalars, psi, after_ops, rights[at], total, token
        )
        if len(rights) < min(at + 3, len(chunks)):
            token = choose(token)

    other = swap(total, 1)
    folds = jnp.concatenate([token, squares], axis=0)
    folds = folds + swap(folds, 1)
    bits = 1
    while bits < rings:
        folds = folds + swap(folds, bits, "sec", rings)
        bits *= 2
    residual, rayleigh = residual_call(scalars, folds, psi, total, other)
    return residual, rayleigh


def solution(mesh):
    placed = (
        P(("groups", "sec"), None, None, None, None),
        P(("groups", "sec"), "term", None, None),
        P(("groups", "sec"), "term", None, None),
        P(),
        P("term"),
        P("groups"),
        P(("groups", "sec"), None),
        P(("groups", "sec")),
    )
    return jax.shard_map(
        functools.partial(on_device, mesh.shape["term"], mesh.shape["sec"]),
        mesh=mesh,
        in_specs=placed,
        out_specs=(P(("groups", "sec"), None, None, None, None), P("groups")),
        check_vma=False,
    )
```

```python
import functools

import jax
import jax.numpy as jnp
from jax import lax
from jax.experimental import pallas as pl
from jax.experimental.pallas import tpu as pltpu
from jax.sharding import PartitionSpec as P

TILE = 16
WIDE = 2
MIB = 1024 * 1024
HASTE = 8


def block_facts(meta, sector_rows, partners, counts, sector, slot):
    live = slot < counts[sector]
    own_rows = sector_rows[meta[0] + sector]
    partner_rows = sector_rows[partners[sector, slot]]
    return live, own_rows, partner_rows


def live_entries(own_rows, partner_rows, width):
    left = lax.broadcasted_iota(jnp.int32, (1, width, width), 1) < own_rows
    right = lax.broadcasted_iota(jnp.int32, (1, width, width), 2) < partner_rows
    return left & right


def folded(values):
    states, width = values.shape[0], values.shape[-1]
    return jnp.sum(values.reshape(states * width // 8, 8, width), axis=0)


def by_live_rows(own_rows, groups, work):
    always = groups // 2
    work(0, always)
    for group in range(always, groups, WIDE):
        pl.when(own_rows > group * TILE)(functools.partial(work, group, group + WIDE))


def spread_operators(ops_ref, chosen, spread_ops, at, states):
    width, wide = ops_ref.shape[-1], states * TILE
    row_state = lax.broadcasted_iota(jnp.int32, (wide, states), 0) // TILE
    column = lax.broadcasted_iota(jnp.int32, (wide, states), 1)
    pick_rows = (row_state == column).astype(jnp.bfloat16)
    row = lax.broadcasted_iota(jnp.int32, (width, wide), 0)
    column_state = lax.broadcasted_iota(jnp.int32, (width, wide), 1) // TILE
    pick_columns = (row == column_state).astype(jnp.bfloat16)
    inner_row = lax.rem(lax.broadcasted_iota(jnp.int32, (wide, wide), 0), TILE)
    inner_column = lax.rem(lax.broadcasted_iota(jnp.int32, (wide, wide), 1), TILE)
    for term in chosen:
        operator = ops_ref[term * states : (term + 1) * states, :]
        rows = jnp.dot(pick_rows, operator, preferred_element_type=jnp.float32)
        full = jnp.dot(
            rows.astype(jnp.bfloat16), pick_columns, preferred_element_type=jnp.float32
        )
        spread_ops[at] = jnp.where(inner_row == inner_column, full, 0.0).astype(jnp.bfloat16)
        at += 1


def multiply_left(lefts, live_psi, after_left):
    terms, groups = after_left.shape[:2]
    states, width = live_psi.shape[0], live_psi.shape[-1]
    for pair in range(states // WIDE):
        columns = jnp.concatenate([live_psi[pair * WIDE + at] for at in range(WIDE)], axis=1)
        done = jnp.dot(lefts, columns, preferred_element_type=jnp.float32).astype(jnp.bfloat16)
        for term in range(terms):
            for at in range(WIDE):
                state = pair * WIDE + at
                after_left[term, :, state * TILE : (state + 1) * TILE, :] = done[
                    term * width : (term + 1) * width, at * width : (at + 1) * width
                ].reshape(groups, TILE, width)


def apply_operators(low, high, spread_ops, after_left, after_ops):
    terms, width = after_left.shape[0], after_left.shape[-1]
    for group in range(low, high, WIDE):
        for term in range(terms):
            columns = jnp.concatenate(
                [after_left[term, group + at] for at in range(WIDE)], axis=1
            )
            done = jnp.dot(
                spread_ops[term], columns, preferred_element_type=jnp.float32
            ).astype(jnp.bfloat16)
            for at in range(WIDE):
                after_ops[term, group + at] = done[:, at * width : (at + 1) * width]


def left_kernel(first, terms, half, slots, meta, sector_rows, partners, counts,
                psi_ref, left_ref, ops_ref, after_ref, out_ref, token_ref, *rest):
    if first:
        square_ref, rest = rest[0], rest[1:]
    spread_ops, live_psi, after_left = rest
    states, width = psi_ref.shape[0], psi_ref.shape[-1]
    step = pl.program_id(0)
    sector = meta[1] * half + step // slots
    slot = lax.rem(step, slots)
    live, own_rows, partner_rows = block_facts(
        meta, sector_rows, partners, counts, sector, slot
    )

    @pl.when(step == 0)
    def _():
        spread_operators(ops_ref, range(terms), spread_ops, 0, states)
        token_ref[...] = jnp.zeros_like(token_ref)
        if first:
            square_ref[...] = jnp.zeros_like(square_ref)

    @pl.when(live)
    def _():
        mask = live_entries(own_rows, partner_rows, width)
        live_psi[...] = jnp.where(mask, psi_ref[...], jnp.zeros((), jnp.bfloat16))
        if first:
            wide_psi = live_psi[...].astype(jnp.float32)
            square_ref[...] += folded(wide_psi * wide_psi)
        multiply_left(left_ref[...], live_psi, after_left)
        by_live_rows(
            own_rows,
            width // TILE,
            lambda low, high: apply_operators(low, high, spread_ops, after_left, out_ref),
        )


def psi_spec_of(psi, half):
    slots, states, width = psi.shape[1:4]
    return pl.BlockSpec(
        (None, None, states, width, width),
        lambda i, meta, *_: (meta[1] * half + i // slots, i % slots, 0, 0, 0),
    )


def left_call(first, terms, scalars, psi, payload, after):
    sectors, slots, states, width = psi.shape[:4]
    half = sectors // 2
    blocks, groups, wide = half * slots, width // TILE, states * TILE
    ops_at = half * width // states
    fold_spec = pl.BlockSpec((8, width), lambda i, *_: (0, 0))
    fold_shape = jax.ShapeDtypeStruct((8, width), jnp.float32)
    extra = 1 + int(first)
    work = 2 * blocks * terms * states * width * width * (width + wide)
    return pl.pallas_call(
        functools.partial(left_kernel, first, terms, half, slots),
        grid_spec=pltpu.PrefetchScalarGridSpec(
            num_scalar_prefetch=len(scalars),
            grid=(blocks,),
            in_specs=[
                psi_spec_of(psi, half),
                pl.BlockSpec((terms * width, width), lambda i, *_: (i // slots, 0)),
                pl.BlockSpec((terms * states, width), lambda i, *_: (ops_at, 0)),
                pl.BlockSpec(memory_space=pl.ANY),
            ],
            out_specs=[
                pl.BlockSpec(
                    (None, terms, groups, wide, width), lambda i, *_: (i, 0, 0, 0, 0)
                )
            ] + [fold_spec] * extra,
            scratch_shapes=[
                pltpu.VMEM((terms, wide, wide), jnp.bfloat16),
                pltpu.VMEM((states, width, width), jnp.bfloat16),
                pltpu.VMEM((terms, groups, wide, width), jnp.bfloat16),
            ],
        ),
        out_shape=[
            jax.ShapeDtypeStruct((blocks, terms, groups, wide, width), jnp.bfloat16)
        ] + [fold_shape] * extra,
        compiler_params=pltpu.CompilerParams(vmem_limit_bytes=48 * MIB),
        cost_estimate=pl.CostEstimate(
            flops=work // HASTE,
            bytes_accessed=2 * blocks * (terms + 1) * states * width * width // HASTE,
            transcendentals=0,
        ),
        name="left",
    )(*scalars, psi, payload, payload, after)


def choose_kernel(devices, sectors, half, slots, meta, partners, after_ref, *rest):
    shards, (mine_ref, other_ref, token_ref) = rest[:devices], rest[devices:]
    token_ref[...] = jnp.zeros_like(token_ref)
    for part, out_ref in enumerate((mine_ref, other_ref)):
        for block in range(half * slots):
            sector = (meta[1] ^ part) * half + block // slots
            partner = partners[sector, block % slots]
            if devices == 1:
                out_ref[block] = shards[0][partner]
                continue
            away = lax.rem(meta[3] + devices - partner // sectors, devices)
            place = lax.rem(partner, sectors)
            for distance in range(devices):
                @pl.when(away == distance)
                def _(distance=distance, place=place, block=block, out_ref=out_ref):
                    out_ref[block] = shards[distance][place]


def choose_call(scalars, half, slots, shards, after):
    meta, _, partners, _ = scalars
    sectors, terms, width = shards[0].shape[:3]
    shape = (half * slots, terms, width, width)
    chosen = jax.ShapeDtypeStruct(shape, jnp.bfloat16)
    kept = pl.BlockSpec(shape, lambda i, *_: (0, 0, 0, 0))
    return pl.pallas_call(
        functools.partial(choose_kernel, len(shards), sectors, half, slots),
        grid_spec=pltpu.PrefetchScalarGridSpec(
            num_scalar_prefetch=2,
            grid=(1,),
            in_specs=[pl.BlockSpec(memory_space=pl.ANY)]
            + [pl.BlockSpec(shards[0].shape, lambda i, *_: (0, 0, 0, 0))] * len(shards),
            out_specs=[kept, kept, pl.BlockSpec((8, width), lambda i, *_: (0, 0))],
        ),
        out_shape=[chosen, chosen, jax.ShapeDtypeStruct((8, width), jnp.float32)],
        compiler_params=pltpu.CompilerParams(vmem_limit_bytes=24 * MIB),
        cost_estimate=pl.CostEstimate(
            flops=0, bytes_accessed=8 * half * slots * terms * width * width, transcendentals=0
        ),
        name="choose",
    )(meta, partners, after, *shards)


def chunk_kernel(first, last, devices, early, start, half, slots,
                 meta, sector_rows, partners, counts, after_ref, psi_ref, *rest):
    late = devices - early
    early_refs, rest = rest[:early], rest[early:]
    left_refs, rest = rest[:late], rest[late:]
    ops_refs, rest = rest[:late], rest[late:]
    right_refs, rest = rest[:devices], rest[devices:]
    if not first:
        sum_in, rest = rest[0], rest[1:]
    sum_out, fold_ref, spread_ops, live_psi, after_left, after_ops, *rest = rest
    total = rest[0] if last else sum_out
    states, width = psi_ref.shape[0], psi_ref.shape[-1]
    terms = right_refs[0].shape[0]
    groups = width // TILE
    step = pl.program_id(0)
    sector = meta[1] * half + step // slots
    slot = lax.rem(step, slots)
    live, own_rows, partner_rows = block_facts(
        meta, sector_rows, partners, counts, sector, slot
    )

    @pl.when(step == 0)
    def _():
        for source in range(late):
            spread_operators(
                ops_refs[source], range(start, start + terms), spread_ops, source * terms, states
            )
        fold_ref[...] = jnp.zeros_like(fold_ref)

    @pl.when(live)
    def _():
        mask = live_entries(own_rows, partner_rows, width)
        live_psi[...] = jnp.where(mask, psi_ref[...], jnp.zeros((), jnp.bfloat16))
        lefts = jnp.concatenate([left_refs[source][...] for source in range(late)], axis=0)
        multiply_left(lefts, live_psi, after_left)
        columns = [
            jnp.concatenate(
                [right_refs[pair + at][term] for at in range(2) for term in range(terms)], axis=0
            )
            for pair in range(0, devices, 2)
        ]

        def operated(device, term, group):
            if device < early:
                return early_refs[device][term, group]
            return after_ops[(device - early) * terms + term, group]

        def multiply(low, high):
            apply_operators(low, high, spread_ops, after_left, after_ops)
            for group in range(low, high, WIDE):
                parts = []
                for pair in range(0, devices, 2):
                    rows = jnp.concatenate(
                        [
                            jnp.concatenate(
                                [
                                    operated(pair + at, term, group + side)
                                    for at in range(2)
                                    for term in range(terms)
                                ],
                                axis=1,
                            )
                            for side in range(WIDE)
                        ],
                        axis=0,
                    )
                    parts.append(
                        jnp.dot(rows, columns[pair // 2], preferred_element_type=jnp.float32)
                    )
                while len(parts) > 1:
                    parts = [parts[at] + parts[at + 1] for at in range(0, len(parts), 2)]
                done = parts[0].reshape(WIDE, states, TILE, width)
                for side in range(WIDE):
                    place = slice((group + side) * TILE, (group + side + 1) * TILE)
                    if first:
                        total[:, place, :] = done[side]
                    else:
                        total[:, place, :] = sum_in[:, place, :] + done[side]

        by_live_rows(own_rows, groups, multiply)
        if last:
            kept = jnp.where(mask, total[...], 0.0)
            fold_ref[...] += folded(kept * live_psi[...].astype(jnp.float32))
            sum_out[...] = kept.astype(jnp.bfloat16)

    if last:
        @pl.when(jnp.logical_not(live))
        def _():
            sum_out[...] = jnp.zeros_like(sum_out)


def chunk_call(first, last, chunk, scalars, psi, early_ops, lefts, rights, total, after):
    early, late = len(early_ops), 2 * len(lefts)
    devices = early + late
    sectors, slots, states, width = psi.shape[:4]
    half = sectors // 2
    blocks, groups, wide = half * slots, width // TILE, states * TILE
    start, terms = chunk
    held = early_ops[0].shape[1]
    sum_spec = pl.BlockSpec((None, states, width, width), lambda i, *_: (i, 0, 0, 0))
    in_specs = [pl.BlockSpec(memory_space=pl.ANY), psi_spec_of(psi, half)]
    operands = [after, psi]
    in_specs += [
        pl.BlockSpec(
            (None, terms, groups, wide, width), lambda i, *_: (i, start // terms, 0, 0, 0)
        )
    ] * early
    operands += early_ops
    in_specs += [
        pl.BlockSpec(
            (None, terms * width, width),
            lambda i, *_, side=side: (side, (i // slots * held + start) // terms, 0),
        )
        for side in (0, 1)
    ] * len(lefts)
    operands += [left for left in lefts for side in (0, 1)]
    in_specs += [
        pl.BlockSpec(
            (None, held * states, width),
            lambda i, *_, side=side: (side, half * width // states, 0),
        )
        for side in (0, 1)
    ] * len(lefts)
    operands += [left for left in lefts for side in (0, 1)]
    in_specs += [pl.BlockSpec((None, terms, width, width), lambda i, *_: (i, 0, 0, 0))] * early
    operands += rights[:early]
    in_specs += [
        pl.BlockSpec(
            (None, None, terms, width, width),
            lambda i, *_, side=side: (side, i, 0, 0, 0),
        )
        for side in (0, 1)
    ] * len(lefts)
    operands += [right for right in rights[early:] for side in (0, 1)]
    aliases = {}
    if not first:
        in_specs.append(sum_spec)
        operands.append(total)
        if not last:
            aliases = {len(scalars) + len(operands) - 1: 0}
    sum_dtype = jnp.bfloat16 if last else jnp.float32
    size = blocks * states * width * width
    scratch = [
        pltpu.VMEM((late * terms, wide, wide), jnp.bfloat16),
        pltpu.VMEM((states, width, width), jnp.bfloat16),
        pltpu.VMEM((late * terms, groups, wide, width), jnp.bfloat16),
        pltpu.VMEM((late * terms, groups, wide, width), jnp.bfloat16),
    ]
    if last:
        scratch.append(pltpu.VMEM((states, width, width), jnp.float32))
    return pl.pallas_call(
        functools.partial(chunk_kernel, first, last, devices, early, start, half, slots),
        grid_spec=pltpu.PrefetchScalarGridSpec(
            num_scalar_prefetch=len(scalars),
            grid=(blocks,),
            in_specs=in_specs,
            out_specs=[sum_spec, pl.BlockSpec((8, width), lambda i, *_: (0, 0))],
            scratch_shapes=scratch,
        ),
        out_shape=[
            jax.ShapeDtypeStruct((blocks, states, width, width), sum_dtype),
            jax.ShapeDtypeStruct((8, width), jnp.float32),
        ],
        input_output_aliases=aliases,
        compiler_params=pltpu.CompilerParams(vmem_limit_bytes=48 * MIB),
        cost_estimate=pl.CostEstimate(
            flops=2 * size * terms * (devices * width + late * (width + wide)) // HASTE,
            bytes_accessed=size * (10 + 2 * early * terms) // HASTE,
            transcendentals=0,
        ),
        name="chunk",
    )(*scalars, *operands)


def residual_kernel(slots, half, meta, sector_rows, partners, counts,
                    folds_ref, psi_ref, own_ref, other_ref, out_ref, quotient_ref):
    width = psi_ref.shape[-1]
    step = pl.program_id(0)
    here = step < half * slots
    sector = lax.rem(meta[1] * half + step // slots, 2 * half)
    slot = lax.rem(step, slots)
    live, own_rows, partner_rows = block_facts(
        meta, sector_rows, partners, counts, sector, slot
    )

    @pl.when(step == 0)
    def _():
        quotient_ref[0] = jnp.sum(folds_ref[0:8, :]) / jnp.sum(folds_ref[8:16, :])

    mask = live_entries(jnp.where(live, own_rows, 0), partner_rows, width)
    scaled = quotient_ref[0] * jnp.where(mask, psi_ref[...].astype(jnp.float32), 0.0)

    @pl.when(here)
    def _():
        out_ref[...] = (own_ref[...].astype(jnp.float32) - scaled).astype(jnp.bfloat16)

    @pl.when(jnp.logical_not(here))
    def _():
        out_ref[...] = (other_ref[...].astype(jnp.float32) - scaled).astype(jnp.bfloat16)


def residual_call(scalars, folds, psi, own, other):
    sectors, slots, states, width = psi.shape[:4]
    half = sectors // 2
    blocks = half * slots
    whole = (None, None, states, width, width)

    def at_sector(i, meta, *_):
        return ((meta[1] * half + i // slots) % sectors, i % slots, 0, 0, 0)

    one = (None, states, width, width)
    return pl.pallas_call(
        functools.partial(residual_kernel, slots, half),
        grid_spec=pltpu.PrefetchScalarGridSpec(
            num_scalar_prefetch=len(scalars),
            grid=(2 * blocks,),
            in_specs=[
                pl.BlockSpec(folds.shape, lambda i, *_: (0, 0)),
                pl.BlockSpec(whole, at_sector),
                pl.BlockSpec(one, lambda i, *_: (jnp.minimum(i, blocks - 1), 0, 0, 0)),
                pl.BlockSpec(one, lambda i, *_: (jnp.maximum(i - blocks, 0), 0, 0, 0)),
            ],
            out_specs=[pl.BlockSpec(whole, at_sector), pl.BlockSpec(memory_space=pltpu.SMEM)],
        ),
        out_shape=[
            jax.ShapeDtypeStruct(psi.shape, jnp.bfloat16),
            jax.ShapeDtypeStruct((1,), jnp.float32),
        ],
        compiler_params=pltpu.CompilerParams(vmem_limit_bytes=32 * MIB),
        cost_estimate=pl.CostEstimate(
            flops=3 * psi.size, bytes_accessed=6 * psi.size, transcendentals=0
        ),
        name="residual",
    )(*scalars, folds, psi, own, other)


def on_device(
    devices, rings, psi, left_env, right_env, local_ops, term_op, sector_rows, block_partner,
    block_count,
):
    sectors, slots, states, width = psi.shape[:4]
    terms = left_env.shape[1]
    half = sectors // 2
    me = lax.axis_index("term")
    ring = lax.axis_index("sec")
    core = me % 2
    meta = jnp.stack([ring * sectors, core, me, ring]).astype(jnp.int32)
    scalars = (meta, sector_rows, block_partner, block_count)

    def swap(value, bits, axis="term", size=devices):
        return lax.ppermute(value, axis, [(i, i ^ bits) for i in range(size)])

    def to_far_chips(near, received):
        both = jnp.stack([near, received])
        return both, [swap(both, bits) for bits in range(2, devices, 2)]

    picker = term_op[:, None] == jnp.arange(local_ops.shape[0], dtype=jnp.int32)[None, :]
    picked = jnp.sum(
        jnp.where(picker[:, :, None, None], local_ops[None], jnp.zeros((), jnp.bfloat16)), axis=1
    )
    padded = jnp.pad(picked, ((0, 0), (0, 0), (0, width - states))).reshape(terms * states, width)
    payloads = []
    for bits in range(2):
        rows = lax.dynamic_slice_in_dim(left_env, (core ^ bits) * half, half)
        payloads.append(jnp.concatenate([rows.reshape(-1, width), padded], axis=0))
    early_lefts = [payloads[0], swap(payloads[1], 1)]
    both_lefts, far_lefts = to_far_chips(*early_lefts)

    chunks = [(at, 1) for at in range(terms)]
    shards, rights = [], []

    def gather(token, at_once=False):
        start, length = chunks[len(shards)]
        own = right_env[:, start : start + length]
        if token is not None:
            own, _ = lax.optimization_barrier((own, token))
        if at_once:
            shards.append([lax.all_gather(own, "sec", axis=0, tiled=True)])
            return
        moved = [own]
        for distance in range(1, rings):
            pairs = [(i, (i + distance) % rings) for i in range(rings)]
            moved.append(lax.ppermute(own, "sec", pairs))
        shards.append(moved)

    def choose(token):
        mine, other, token = choose_call(scalars, half, slots, shards[len(rights)], token)
        received = swap(other, 1)
        rights.append([mine, received] + to_far_chips(mine, received)[1])
        return token

    gather(None)
    own_ops, token, squares = left_call(
        True, terms, scalars, psi, early_lefts[0], both_lefts
    )
    gather(token)
    token = choose(token)
    sibling_ops, token = left_call(False, terms, scalars, psi, early_lefts[1], token)
    early_ops = [own_ops, sibling_ops]
    gather(token)
    total = None
    for at, chunk in enumerate(chunks):
        if len(rights) < len(chunks):
            token = choose(token)
        last = at == len(chunks) - 1
        total, token = chunk_call(
            at == 0, last, chunk, scalars, psi, early_ops, far_lefts, rights[at], total, token
        )
        if at == 0:
            gather(None, True)

    other = swap(total, 1)
    folds = jnp.concatenate([token, squares], axis=0)
    folds = folds + swap(folds, 1)
    bits = 1
    while bits < rings:
        folds = folds + swap(folds, bits, "sec", rings)
        bits *= 2
    residual, rayleigh = residual_call(scalars, folds, psi, total, other)
    return residual, rayleigh


def solution(mesh):
    placed = (
        P(("groups", "sec"), None, None, None, None),
        P(("groups", "sec"), "term", None, None),
        P(("groups", "sec"), "term", None, None),
        P(),
        P("term"),
        P("groups"),
        P(("groups", "sec"), None),
        P(("groups", "sec")),
    )
    return jax.shard_map(
        functools.partial(on_device, mesh.shape["term"], mesh.shape["sec"]),
        mesh=mesh,
        in_specs=placed,
        out_specs=(P(("groups", "sec"), None, None, None, None), P("groups")),
        check_vma=False,
    )
```

```python
import functools

import jax
import jax.numpy as jnp
from jax import lax
from jax.experimental import pallas as pl
from jax.experimental.pallas import tpu as pltpu
from jax.sharding import PartitionSpec as P

TILE = 16
WIDE = 2
MIB = 1024 * 1024
SPARE = 10 * MIB
HASTE = 8


def block_facts(meta, sector_rows, partners, counts, sector, slot):
    live = slot < counts[sector]
    own_rows = sector_rows[meta[0] + sector]
    partner_rows = sector_rows[partners[sector, slot]]
    return live, own_rows, partner_rows


def live_entries(own_rows, partner_rows, width):
    left = lax.broadcasted_iota(jnp.int32, (1, width, width), 1) < own_rows
    right = lax.broadcasted_iota(jnp.int32, (1, width, width), 2) < partner_rows
    return left & right


def folded(values):
    states, width = values.shape[0], values.shape[-1]
    return jnp.sum(values.reshape(states * width // 8, 8, width), axis=0)


def by_live_rows(own_rows, groups, work):
    always = groups // 2
    work(0, always)
    for group in range(always, groups, WIDE):
        pl.when(own_rows > group * TILE)(functools.partial(work, group, group + WIDE))


def spread_operators(ops_ref, chosen, spread_ops, at, states):
    width, wide = ops_ref.shape[-1], states * TILE
    row_state = lax.broadcasted_iota(jnp.int32, (wide, states), 0) // TILE
    column = lax.broadcasted_iota(jnp.int32, (wide, states), 1)
    pick_rows = (row_state == column).astype(jnp.bfloat16)
    row = lax.broadcasted_iota(jnp.int32, (width, wide), 0)
    column_state = lax.broadcasted_iota(jnp.int32, (width, wide), 1) // TILE
    pick_columns = (row == column_state).astype(jnp.bfloat16)
    inner_row = lax.rem(lax.broadcasted_iota(jnp.int32, (wide, wide), 0), TILE)
    inner_column = lax.rem(lax.broadcasted_iota(jnp.int32, (wide, wide), 1), TILE)
    for term in chosen:
        operator = ops_ref[term * states : (term + 1) * states, :]
        rows = jnp.dot(pick_rows, operator, preferred_element_type=jnp.float32)
        full = jnp.dot(
            rows.astype(jnp.bfloat16), pick_columns, preferred_element_type=jnp.float32
        )
        spread_ops[at] = jnp.where(inner_row == inner_column, full, 0.0).astype(jnp.bfloat16)
        at += 1


def multiply_left(lefts, live_psi, after_left):
    terms, groups = after_left.shape[:2]
    states, width = live_psi.shape[0], live_psi.shape[-1]
    for pair in range(states // WIDE):
        columns = jnp.concatenate([live_psi[pair * WIDE + at] for at in range(WIDE)], axis=1)
        done = jnp.dot(lefts, columns, preferred_element_type=jnp.float32).astype(jnp.bfloat16)
        for term in range(terms):
            for at in range(WIDE):
                state = pair * WIDE + at
                after_left[term, :, state * TILE : (state + 1) * TILE, :] = done[
                    term * width : (term + 1) * width, at * width : (at + 1) * width
                ].reshape(groups, TILE, width)


def apply_operators(low, high, spread_ops, after_left, after_ops):
    terms, width = after_left.shape[0], after_left.shape[-1]
    for group in range(low, high, WIDE):
        for term in range(terms):
            columns = jnp.concatenate(
                [after_left[term, group + at] for at in range(WIDE)], axis=1
            )
            done = jnp.dot(
                spread_ops[term], columns, preferred_element_type=jnp.float32
            ).astype(jnp.bfloat16)
            for at in range(WIDE):
                after_ops[term, group + at] = done[:, at * width : (at + 1) * width]


def each_live_block(half, slots, scalars, work):
    meta, sector_rows, partners, counts = scalars

    def visit(block, carry):
        place, slot = block // slots, lax.rem(block, slots)
        live, own_rows, partner_rows = block_facts(
            meta, sector_rows, partners, counts, meta[1] * half + place, slot
        )
        pl.when(live)(functools.partial(work, block, place, own_rows, partner_rows))
        return carry

    lax.fori_loop(0, half * slots, visit, 0)


def left_kernel(terms, half, slots, meta, sector_rows, partners, counts,
                after_ref, psi_ref, left_ref, out_ref, token_ref, square_ref,
                spread_ops, after_left):
    states, width = psi_ref.shape[1], psi_ref.shape[-1]
    spread_operators(
        left_ref[half * terms * width :, :], range(terms), spread_ops, 0, states
    )
    token_ref[...] = jnp.zeros_like(token_ref)
    square_ref[...] = jnp.zeros_like(square_ref)

    def work(block, place, own_rows, partner_rows):
        wide_psi = psi_ref[block].astype(jnp.float32)
        square_ref[...] += folded(wide_psi * wide_psi)
        rows = pl.ds(pl.multiple_of(place * (terms * width), width), terms * width)
        multiply_left(left_ref[rows, :], psi_ref.at[block], after_left)
        by_live_rows(
            own_rows,
            width // TILE,
            lambda low, high: apply_operators(
                low, high, spread_ops, after_left, out_ref.at[block]
            ),
        )

    each_live_block(half, slots, (meta, sector_rows, partners, counts), work)


def resident(count):
    return [pl.BlockSpec(memory_space=pltpu.VMEM)] * count


def in_smem(count):
    return [pl.BlockSpec(memory_space=pltpu.SMEM)] * count


def left_call(scalars, slots, terms, psi, payload, after):
    blocks, states, width = psi.shape[:3]
    groups, wide = width // TILE, states * TILE
    fold_shape = jax.ShapeDtypeStruct((8, width), jnp.float32)
    work = 2 * psi.size * terms * (width + wide)
    return pl.pallas_call(
        functools.partial(left_kernel, terms, blocks // slots, slots),
        in_specs=in_smem(4) + [pl.BlockSpec(memory_space=pl.ANY)] + resident(2),
        out_specs=resident(3),
        out_shape=[
            jax.ShapeDtypeStruct((blocks, terms, groups, wide, width), jnp.bfloat16),
            fold_shape,
            fold_shape,
        ],
        scratch_shapes=[
            pltpu.VMEM((terms, wide, wide), jnp.bfloat16),
            pltpu.VMEM((terms, groups, wide, width), jnp.bfloat16),
        ],
        compiler_params=pltpu.CompilerParams(
            vmem_limit_bytes=SPARE + 2 * terms * (wide * wide + groups * wide * width)
        ),
        cost_estimate=pl.CostEstimate(
            flops=work // HASTE, bytes_accessed=psi.size // HASTE, transcendentals=0
        ),
        name="left",
    )(*scalars, after, psi, payload)


def choose_kernel(devices, sectors, half, slots, meta, partners, after_ref, *rest):
    shards, (mine_ref, other_ref, token_ref) = rest[:devices], rest[devices:]
    token_ref[...] = jnp.zeros_like(token_ref)
    for part, out_ref in enumerate((mine_ref, other_ref)):
        for block in range(half * slots):
            sector = (meta[1] ^ part) * half + block // slots
            partner = partners[sector, block % slots]
            if devices == 1:
                out_ref[block] = shards[0][partner]
                continue
            away = lax.rem(meta[3] + devices - partner // sectors, devices)
            place = lax.rem(partner, sectors)
            for distance in range(devices):
                @pl.when(away == distance)
                def _(distance=distance, place=place, block=block, out_ref=out_ref):
                    out_ref[block] = shards[distance][place]


def choose_call(scalars, half, slots, shards, after):
    meta, _, partners, _ = scalars
    sectors, terms, width = shards[0].shape[:3]
    shape = (half * slots, terms, width, width)
    chosen = jax.ShapeDtypeStruct(shape, jnp.bfloat16)
    kept = pl.BlockSpec(shape, lambda i, *_: (0, 0, 0, 0))
    return pl.pallas_call(
        functools.partial(choose_kernel, len(shards), sectors, half, slots),
        grid_spec=pltpu.PrefetchScalarGridSpec(
            num_scalar_prefetch=2,
            grid=(1,),
            in_specs=[pl.BlockSpec(memory_space=pl.ANY)]
            + [pl.BlockSpec(shards[0].shape, lambda i, *_: (0, 0, 0, 0))] * len(shards),
            out_specs=[kept, kept, pl.BlockSpec((8, width), lambda i, *_: (0, 0))],
        ),
        out_shape=[chosen, chosen, jax.ShapeDtypeStruct((8, width), jnp.float32)],
        compiler_params=pltpu.CompilerParams(vmem_limit_bytes=24 * MIB),
        cost_estimate=pl.CostEstimate(
            flops=0, bytes_accessed=8 * half * slots * terms * width * width, transcendentals=0
        ),
        name="choose",
    )(meta, partners, after, *shards)


def chunk_kernel(first, last, held, start, far, half, slots,
                 meta, sector_rows, partners, counts, after_ref, psi_ref, early_ref,
                 near_left, *rest):
    far_lefts, rest = rest[:far], rest[far:]
    near_rights, rest = rest[:2], rest[2:]
    far_rights, rest = rest[:far], rest[far:]
    if not first:
        sum_in, rest = rest[0], rest[1:]
    sum_out, fold_ref, spread_ops, after_left, after_ops, *rest = rest
    states, width = psi_ref.shape[1], psi_ref.shape[-1]
    terms = near_rights[0].shape[1]
    groups = width // TILE
    devices = 2 + 2 * far
    lefts = [near_left] + [left.at[side] for left in far_lefts for side in (0, 1)]
    rights = list(near_rights) + [right.at[side] for right in far_rights for side in (0, 1)]
    for at, left in enumerate(lefts):
        spread_operators(
            left[half * held * width :, :], range(start, start + terms), spread_ops,
            at * terms, states,
        )
    fold_ref[...] = jnp.zeros_like(fold_ref)
    if last:
        sum_out[...] = jnp.zeros_like(sum_out)

    def work(block, place, own_rows, partner_rows):
        total = rest[0] if last else sum_out.at[block]
        rows = pl.ds(
            pl.multiple_of((place * held + start) * width, width), terms * width
        )
        multiply_left(
            jnp.concatenate([left[rows, :] for left in lefts], axis=0),
            psi_ref.at[block],
            after_left,
        )
        columns = [
            jnp.concatenate(
                [rights[pair + at][block, term] for at in range(2) for term in range(terms)],
                axis=0,
            )
            for pair in range(0, devices, 2)
        ]

        def operated(device, term, group):
            if device == 0:
                return early_ref[block, start + term, group]
            return after_ops[(device - 1) * terms + term, group]

        def multiply(low, high):
            apply_operators(low, high, spread_ops, after_left, after_ops)
            for group in range(low, high, WIDE):
                parts = []
                for pair in range(0, devices, 2):
                    rows = jnp.concatenate(
                        [
                            jnp.concatenate(
                                [
                                    operated(pair + at, term, group + side)
                                    for at in range(2)
                                    for term in range(terms)
                                ],
                                axis=1,
                            )
                            for side in range(WIDE)
                        ],
                        axis=0,
                    )
                    parts.append(
                        jnp.dot(rows, columns[pair // 2], preferred_element_type=jnp.float32)
                    )
                while len(parts) > 1:
                    parts = [parts[at] + parts[at + 1] for at in range(0, len(parts), 2)]
                done = parts[0].reshape(WIDE, states, TILE, width)
                for side in range(WIDE):
                    tile = slice((group + side) * TILE, (group + side + 1) * TILE)
                    if first:
                        total[:, tile, :] = done[side]
                    else:
                        total[:, tile, :] = sum_in[block, :, tile, :] + done[side]

        by_live_rows(own_rows, groups, multiply)
        if last:
            mask = live_entries(own_rows, partner_rows, width)
            kept = jnp.where(mask, total[...], 0.0)
            fold_ref[...] += folded(kept * psi_ref[block].astype(jnp.float32))
            sum_out[block] = kept.astype(jnp.bfloat16)

    each_live_block(half, slots, (meta, sector_rows, partners, counts), work)


def chunk_call(first, last, chunk, scalars, slots, psi, early, near_left, far_lefts, rights,
               total, after):
    far = len(far_lefts)
    late = 1 + 2 * far
    blocks, states, width = psi.shape[:3]
    groups, wide = width // TILE, states * TILE
    start, terms = chunk
    held = early.shape[1]
    operands = [after, psi, early, near_left, *far_lefts, *rights]
    aliases = {}
    if not first:
        operands.append(total)
        if not last:
            aliases = {len(scalars) + len(operands) - 1: 0}
    sum_dtype = jnp.bfloat16 if last else jnp.float32
    scratch = [
        pltpu.VMEM((late * terms, wide, wide), jnp.bfloat16),
        pltpu.VMEM((late * terms, groups, wide, width), jnp.bfloat16),
        pltpu.VMEM((late * terms, groups, wide, width), jnp.bfloat16),
    ]
    if last:
        scratch.append(pltpu.VMEM((states, width, width), jnp.float32))
    work = 2 * psi.size * terms * ((late + 1) * width + late * (width + wide))
    return pl.pallas_call(
        functools.partial(
            chunk_kernel, first, last, held, start, far, blocks // slots, slots
        ),
        in_specs=in_smem(4) + [pl.BlockSpec(memory_space=pl.ANY)] + resident(len(operands) - 1),
        out_specs=resident(2),
        out_shape=[
            jax.ShapeDtypeStruct(psi.shape, sum_dtype),
            jax.ShapeDtypeStruct((8, width), jnp.float32),
        ],
        scratch_shapes=scratch,
        input_output_aliases=aliases,
        compiler_params=pltpu.CompilerParams(
            vmem_limit_bytes=SPARE + 2 * late * terms * wide * (wide + 2 * groups * width)
        ),
        cost_estimate=pl.CostEstimate(
            flops=work // HASTE, bytes_accessed=psi.size // HASTE, transcendentals=0
        ),
        name="chunk",
    )(*scalars, *operands)


def residual_kernel(slots, half, meta, sector_rows, partners, counts,
                    folds_ref, psi_ref, own_ref, other_ref, out_ref, quotient_ref):
    width = psi_ref.shape[-1]
    step = pl.program_id(0)
    here = step < half * slots
    sector = lax.rem(meta[1] * half + step // slots, 2 * half)
    slot = lax.rem(step, slots)
    live, own_rows, partner_rows = block_facts(
        meta, sector_rows, partners, counts, sector, slot
    )

    @pl.when(step == 0)
    def _():
        quotient_ref[0] = jnp.sum(folds_ref[0:8, :]) / jnp.sum(folds_ref[8:16, :])

    mask = live_entries(jnp.where(live, own_rows, 0), partner_rows, width)
    scaled = quotient_ref[0] * jnp.where(mask, psi_ref[...].astype(jnp.float32), 0.0)

    @pl.when(here)
    def _():
        out_ref[...] = (own_ref[...].astype(jnp.float32) - scaled).astype(jnp.bfloat16)

    @pl.when(jnp.logical_not(here))
    def _():
        out_ref[...] = (other_ref[...].astype(jnp.float32) - scaled).astype(jnp.bfloat16)


def residual_call(scalars, folds, psi, own, other):
    sectors, slots, states, width = psi.shape[:4]
    half = sectors // 2
    blocks = half * slots
    whole = (None, None, states, width, width)

    def at_sector(i, meta, *_):
        return ((meta[1] * half + i // slots) % sectors, i % slots, 0, 0, 0)

    one = (None, states, width, width)
    return pl.pallas_call(
        functools.partial(residual_kernel, slots, half),
        grid_spec=pltpu.PrefetchScalarGridSpec(
            num_scalar_prefetch=len(scalars),
            grid=(2 * blocks,),
            in_specs=[
                pl.BlockSpec(folds.shape, lambda i, *_: (0, 0)),
                pl.BlockSpec(whole, at_sector),
                pl.BlockSpec(one, lambda i, *_: (jnp.minimum(i, blocks - 1), 0, 0, 0)),
                pl.BlockSpec(one, lambda i, *_: (jnp.maximum(i - blocks, 0), 0, 0, 0)),
            ],
            out_specs=[pl.BlockSpec(whole, at_sector), pl.BlockSpec(memory_space=pltpu.SMEM)],
        ),
        out_shape=[
            jax.ShapeDtypeStruct(psi.shape, jnp.bfloat16),
            jax.ShapeDtypeStruct((1,), jnp.float32),
        ],
        compiler_params=pltpu.CompilerParams(vmem_limit_bytes=32 * MIB),
        cost_estimate=pl.CostEstimate(
            flops=3 * psi.size, bytes_accessed=6 * psi.size, transcendentals=0
        ),
        name="residual",
    )(*scalars, folds, psi, own, other)


def on_device(
    devices, rings, psi, left_env, right_env, local_ops, term_op, sector_rows, block_partner,
    block_count,
):
    sectors, slots, states, width = psi.shape[:4]
    terms = left_env.shape[1]
    half = sectors // 2
    me = lax.axis_index("term")
    ring = lax.axis_index("sec")
    core = me % 2
    meta = jnp.stack([ring * sectors, core, me, ring]).astype(jnp.int32)
    scalars = (meta, sector_rows, block_partner, block_count)

    def swap(value, bits, axis="term", size=devices):
        return lax.ppermute(value, axis, [(i, i ^ bits) for i in range(size)])

    def to_far_chips(near, received):
        both = jnp.stack([near, received])
        return both, [swap(both, bits) for bits in range(2, devices, 2)]

    picker = term_op[:, None] == jnp.arange(local_ops.shape[0], dtype=jnp.int32)[None, :]
    picked = jnp.sum(
        jnp.where(picker[:, :, None, None], local_ops[None], jnp.zeros((), jnp.bfloat16)), axis=1
    )
    padded = jnp.pad(picked, ((0, 0), (0, 0), (0, width - states))).reshape(terms * states, width)
    payloads = []
    for bits in range(2):
        rows = lax.dynamic_slice_in_dim(left_env, (core ^ bits) * half, half)
        payloads.append(jnp.concatenate([rows.reshape(-1, width), padded], axis=0))
    early_lefts = [payloads[0], swap(payloads[1], 1)]
    both_lefts, far_lefts = to_far_chips(*early_lefts)

    chunks = [(at, 1) for at in range(terms)]
    shards, rights = [], []

    def gather(token, at_once=False):
        start, length = chunks[len(shards)]
        own = right_env[:, start : start + length]
        if token is not None:
            own, _ = lax.optimization_barrier((own, token))
        if at_once:
            shards.append([lax.all_gather(own, "sec", axis=0, tiled=True)])
            return
        moved = [own]
        for distance in range(1, rings):
            pairs = [(i, (i + distance) % rings) for i in range(rings)]
            moved.append(lax.ppermute(own, "sec", pairs))
        shards.append(moved)

    def choose(token):
        mine, other, token = choose_call(scalars, half, slots, shards[len(rights)], token)
        received = swap(other, 1)
        rights.append([mine, received] + to_far_chips(mine, received)[1])
        return token

    own_half = (core * half, 0, 0, 0, 0)
    rows_iota = jnp.arange(width, dtype=jnp.int32)
    hits = block_partner[:, :, None] == jnp.arange(sector_rows.shape[0], dtype=jnp.int32)
    partner_rows = jnp.sum(jnp.where(hits, sector_rows, 0), axis=2)
    own_rows = lax.dynamic_slice_in_dim(sector_rows, ring * sectors, sectors)
    live = jnp.arange(slots, dtype=jnp.int32)[None, :] < block_count[:, None]
    own_rows = jnp.where(live, own_rows[:, None], 0)
    own_rows = lax.dynamic_slice_in_dim(own_rows, core * half, half)
    partner_rows = lax.dynamic_slice_in_dim(partner_rows, core * half, half)
    mask = (rows_iota[:, None] < own_rows[:, :, None, None, None]) & (
        rows_iota < partner_rows[:, :, None, None, None]
    )
    psi_half = lax.dynamic_slice(psi, own_half, (half,) + psi.shape[1:])
    live_psi = jnp.where(mask, psi_half, jnp.zeros((), psi.dtype))
    live_psi = live_psi.reshape(half * slots, states, width, width)

    gather(None)
    early, token, squares = left_call(scalars, slots, terms, live_psi, early_lefts[0], both_lefts)
    gather(token)
    token = choose(token)
    total = None
    for at, chunk in enumerate(chunks):
        if at == 0:
            gather(token)
        if len(rights) < len(chunks):
            token = choose(token)
        last = at == len(chunks) - 1
        total, token = chunk_call(
            at == 0, last, chunk, scalars, slots, live_psi, early, early_lefts[1], far_lefts,
            rights[at], total, token,
        )
        if at == 0:
            gather(None, True)

    other = swap(total, 1)
    folds = jnp.concatenate([token, squares], axis=0)
    folds = folds + swap(folds, 1)
    bits = 1
    while bits < rings:
        folds = folds + swap(folds, bits, "sec", rings)
        bits *= 2
    residual, rayleigh = residual_call(scalars, folds, psi, total, other)
    return residual, rayleigh


def solution(mesh):
    placed = (
        P(("groups", "sec"), None, None, None, None),
        P(("groups", "sec"), "term", None, None),
        P(("groups", "sec"), "term", None, None),
        P(),
        P("term"),
        P("groups"),
        P(("groups", "sec"), None),
        P(("groups", "sec")),
    )
    return jax.shard_map(
        functools.partial(on_device, mesh.shape["term"], mesh.shape["sec"]),
        mesh=mesh,
        in_specs=placed,
        out_specs=(P(("groups", "sec"), None, None, None, None), P("groups")),
        check_vma=False,
    )
```

```python
import functools

import jax
import jax.numpy as jnp
from jax import lax
from jax.experimental import pallas as pl
from jax.experimental.pallas import tpu as pltpu
from jax.sharding import PartitionSpec as P

TILE = 16
WIDE = 2
MIB = 1024 * 1024
SPARE = 4 * MIB
HASTE = 256


def block_facts(scalars, index, slot):
    meta, places, sector_rows, partners, counts = scalars
    sector = places[index]
    live = slot < counts[sector]
    own_rows = sector_rows[meta[0] + sector]
    partner_rows = sector_rows[partners[sector, slot]]
    return sector, live, own_rows, partner_rows


def live_entries(own_rows, partner_rows, width):
    left = lax.broadcasted_iota(jnp.int32, (1, width, width), 1) < own_rows
    right = lax.broadcasted_iota(jnp.int32, (1, width, width), 2) < partner_rows
    return left & right


def folded(values):
    states, width = values.shape[0], values.shape[-1]
    return jnp.sum(values.reshape(states * width // 8, 8, width), axis=0)


def by_live_rows(own_rows, groups, work):
    always = groups // 2
    work(0, always)
    for group in range(always, groups, WIDE):
        pl.when(own_rows > group * TILE)(functools.partial(work, group, group + WIDE))


def spread_operators(ops_ref, chosen, spread_ops, at, states):
    width, wide = ops_ref.shape[-1], states * TILE
    row_state = lax.broadcasted_iota(jnp.int32, (wide, states), 0) // TILE
    column = lax.broadcasted_iota(jnp.int32, (wide, states), 1)
    pick_rows = (row_state == column).astype(jnp.bfloat16)
    row = lax.broadcasted_iota(jnp.int32, (width, wide), 0)
    column_state = lax.broadcasted_iota(jnp.int32, (width, wide), 1) // TILE
    pick_columns = (row == column_state).astype(jnp.bfloat16)
    inner_row = lax.rem(lax.broadcasted_iota(jnp.int32, (wide, wide), 0), TILE)
    inner_column = lax.rem(lax.broadcasted_iota(jnp.int32, (wide, wide), 1), TILE)
    for term in chosen:
        operator = ops_ref[term * states : (term + 1) * states, :]
        rows = jnp.dot(pick_rows, operator, preferred_element_type=jnp.float32)
        full = jnp.dot(
            rows.astype(jnp.bfloat16), pick_columns, preferred_element_type=jnp.float32
        )
        spread_ops[at] = jnp.where(inner_row == inner_column, full, 0.0).astype(jnp.bfloat16)
        at += 1


def multiply_left(lefts, live_psi, after_left):
    terms, groups = after_left.shape[:2]
    states, width = live_psi.shape[0], live_psi.shape[-1]
    for pair in range(states // WIDE):
        columns = jnp.concatenate([live_psi[pair * WIDE + at] for at in range(WIDE)], axis=1)
        done = jnp.dot(lefts, columns, preferred_element_type=jnp.float32).astype(jnp.bfloat16)
        for term in range(terms):
            for at in range(WIDE):
                state = pair * WIDE + at
                after_left[term, :, state * TILE : (state + 1) * TILE, :] = done[
                    term * width : (term + 1) * width, at * width : (at + 1) * width
                ].reshape(groups, TILE, width)


def apply_operators(low, high, spread_ops, after_left, after_ops):
    terms, width = after_left.shape[0], after_left.shape[-1]
    for group in range(low, high, WIDE):
        for term in range(terms):
            columns = jnp.concatenate(
                [after_left[term, group + at] for at in range(WIDE)], axis=1
            )
            done = jnp.dot(
                spread_ops[term], columns, preferred_element_type=jnp.float32
            ).astype(jnp.bfloat16)
            for at in range(WIDE):
                after_ops[term, group + at] = done[:, at * width : (at + 1) * width]


def each_live_block(half, slots, scalars, work):
    meta = scalars[0]

    def visit(block, carry):
        place, slot = block // slots, lax.rem(block, slots)
        sector, live, own_rows, partner_rows = block_facts(
            scalars, meta[1] * half + place, slot
        )
        pl.when(live)(functools.partial(work, block, place, sector, own_rows, partner_rows))
        return carry

    lax.fori_loop(0, half * slots, visit, 0)


def pack_kernel(chunks, half, terms, places, term_op, ops_ref, left_ref, right_ref, *rest):
    payloads, rest = rest[:2], rest[2:]
    shares, sems = rest[: len(chunks)], rest[len(chunks)]
    states, width = ops_ref.shape[1:]
    copied = half * terms * width
    for part, payload in enumerate(payloads):
        for place in range(half):
            pltpu.make_async_copy(
                left_ref.at[places[part * half + place]],
                payload.at[pl.ds(place * terms * width, terms * width)],
                sems.at[part],
            ).start()
    moves = []
    for at, (start, length) in enumerate(chunks):
        move = pltpu.make_async_copy(
            right_ref.at[:, pl.ds(start, length)], shares[at], sems.at[2 + at]
        )
        move.start()
        moves.append(move)
    for payload in payloads:
        for term in range(terms):
            rows = slice(copied + term * states, copied + (term + 1) * states)
            payload[rows, :] = ops_ref[term_op[term]]
    for part, payload in enumerate(payloads):
        whole = payload.at[pl.ds(0, copied)]
        pltpu.make_async_copy(whole, whole, sems.at[part]).wait()
    for move in moves:
        move.wait()


def pack_call(chunks, places, term_op, local_ops, left_env, right_env):
    sectors, terms, width = left_env.shape[:3]
    half, states = sectors // 2, local_ops.shape[1]
    payload = jax.ShapeDtypeStruct((terms * (half * width + states), width), jnp.bfloat16)
    shares = [
        jax.ShapeDtypeStruct((sectors, length, width, width), jnp.bfloat16)
        for start, length in chunks
    ]
    padded = jnp.pad(local_ops, ((0, 0), (0, 0), (0, width - states)))
    return pl.pallas_call(
        functools.partial(pack_kernel, chunks, half, terms),
        in_specs=in_smem(2) + resident(1) + [pl.BlockSpec(memory_space=pl.ANY)] * 2,
        out_specs=resident(2 + len(chunks)),
        out_shape=[payload, payload] + shares,
        scratch_shapes=[pltpu.SemaphoreType.DMA((2 + len(chunks),))],
        compiler_params=pltpu.CompilerParams(vmem_limit_bytes=SPARE),
        cost_estimate=pl.CostEstimate(
            flops=0, bytes_accessed=4 * left_env.size, transcendentals=0
        ),
        name="pack",
    )(places, term_op, padded, left_env.reshape(sectors, terms * width, width), right_env)


def left_kernel(terms, half, slots, meta, places, sector_rows, partners, counts,
                after_ref, psi_ref, left_ref, out_ref, live_psi, token_ref, square_ref,
                spread_ops, after_left, sems):
    scalars = (meta, places, sector_rows, partners, counts)
    states, width = live_psi.shape[1], live_psi.shape[-1]

    def fetch(block, place, sector, own_rows, partner_rows):
        pltpu.make_async_copy(
            psi_ref.at[sector, lax.rem(block, slots)], live_psi.at[block], sems.at[block]
        ).start()

    each_live_block(half, slots, scalars, fetch)
    spread_operators(
        left_ref[half * terms * width :, :], range(terms), spread_ops, 0, states
    )
    token_ref[...] = jnp.zeros_like(token_ref)
    square_ref[...] = jnp.zeros_like(square_ref)

    def work(block, place, sector, own_rows, partner_rows):
        pltpu.make_async_copy(
            psi_ref.at[sector, lax.rem(block, slots)], live_psi.at[block], sems.at[block]
        ).wait()
        mask = live_entries(own_rows, partner_rows, width)
        kept = jnp.where(mask, live_psi[block], jnp.zeros((), jnp.bfloat16))
        live_psi[block] = kept
        wide_psi = kept.astype(jnp.float32)
        square_ref[...] += folded(wide_psi * wide_psi)
        rows = pl.ds(pl.multiple_of(place * (terms * width), width), terms * width)
        multiply_left(left_ref[rows, :], live_psi.at[block], after_left)
        by_live_rows(
            own_rows,
            width // TILE,
            lambda low, high: apply_operators(
                low, high, spread_ops, after_left, out_ref.at[block]
            ),
        )

    each_live_block(half, slots, scalars, work)


def resident(count):
    return [pl.BlockSpec(memory_space=pltpu.VMEM)] * count


def in_smem(count):
    return [pl.BlockSpec(memory_space=pltpu.SMEM)] * count


def left_call(scalars, terms, psi, payload, after):
    sectors, slots, states, width = psi.shape[:4]
    half = sectors // 2
    blocks, groups, wide = half * slots, width // TILE, states * TILE
    fold_shape = jax.ShapeDtypeStruct((8, width), jnp.float32)
    return pl.pallas_call(
        functools.partial(left_kernel, terms, half, slots),
        in_specs=in_smem(len(scalars)) + [pl.BlockSpec(memory_space=pl.ANY)] * 2 + resident(1),
        out_specs=resident(4),
        out_shape=[
            jax.ShapeDtypeStruct((blocks, terms, groups, wide, width), jnp.bfloat16),
            jax.ShapeDtypeStruct((blocks, states, width, width), jnp.bfloat16),
            fold_shape,
            fold_shape,
        ],
        scratch_shapes=[
            pltpu.VMEM((terms, wide, wide), jnp.bfloat16),
            pltpu.VMEM((terms, groups, wide, width), jnp.bfloat16),
            pltpu.SemaphoreType.DMA((blocks,)),
        ],
        compiler_params=pltpu.CompilerParams(
            vmem_limit_bytes=SPARE + 2 * terms * (wide * wide + groups * wide * width)
        ),
        cost_estimate=pl.CostEstimate(
            flops=psi.size * terms * (width + wide) // HASTE,
            bytes_accessed=psi.size // HASTE,
            transcendentals=0,
        ),
        name="left",
    )(*scalars, after, psi, payload)


def choose_kernel(devices, sectors, half, slots, meta, places, partners, after_ref, *rest):
    shards, (mine_ref, other_ref) = rest[:devices], rest[devices:]
    for part, out_ref in enumerate((mine_ref, other_ref)):
        for block in range(half * slots):
            sector = places[(meta[1] ^ part) * half + block // slots]
            partner = partners[sector, block % slots]
            away = lax.rem(meta[3] + devices - partner // sectors, devices)
            place = lax.rem(partner, sectors)
            for distance in range(devices):
                @pl.when(away == distance)
                def _(distance=distance, place=place, block=block, out_ref=out_ref):
                    out_ref[block] = shards[distance][place]


def choose_call(scalars, half, slots, shards, after):
    meta, places, _, partners, _ = scalars
    sectors, terms, width = shards[0].shape[:3]
    chosen = jax.ShapeDtypeStruct((half * slots, terms, width, width), jnp.bfloat16)
    return pl.pallas_call(
        functools.partial(choose_kernel, len(shards), sectors, half, slots),
        in_specs=in_smem(3) + [pl.BlockSpec(memory_space=pl.ANY)] + resident(len(shards)),
        out_specs=resident(2),
        out_shape=[chosen, chosen],
        compiler_params=pltpu.CompilerParams(vmem_limit_bytes=SPARE),
        cost_estimate=pl.CostEstimate(
            flops=0, bytes_accessed=8 * half * slots * terms * width * width, transcendentals=0
        ),
        name="choose",
    )(meta, places, partners, after, *shards)


def chunk_kernel(first, last, held, start, far, half, slots,
                 meta, places, sector_rows, partners, counts, after_ref, psi_ref, early_ref,
                 near_left, *rest):
    far_lefts, rest = rest[:far], rest[far:]
    near_rights, rest = rest[:2], rest[2:]
    far_rights, rest = rest[:far], rest[far:]
    if not first:
        sum_in, rest = rest[0], rest[1:]
    sum_out, fold_ref, spread_ops, after_left, after_ops, *rest = rest
    states, width = psi_ref.shape[1], psi_ref.shape[-1]
    terms = near_rights[0].shape[1]
    groups = width // TILE
    devices = 2 + 2 * far
    lefts = [near_left] + [left.at[side] for left in far_lefts for side in (0, 1)]
    rights = list(near_rights) + [right.at[side] for right in far_rights for side in (0, 1)]
    for at, left in enumerate(lefts):
        spread_operators(
            left[half * held * width :, :], range(start, start + terms), spread_ops,
            at * terms, states,
        )
    fold_ref[...] = jnp.zeros_like(fold_ref)
    if last:
        sum_out[...] = jnp.zeros_like(sum_out)

    def work(block, place, sector, own_rows, partner_rows):
        total = rest[0] if last else sum_out.at[block]
        rows = pl.ds(
            pl.multiple_of((place * held + start) * width, width), terms * width
        )
        multiply_left(
            jnp.concatenate([left[rows, :] for left in lefts], axis=0),
            psi_ref.at[block],
            after_left,
        )
        columns = [
            jnp.concatenate(
                [rights[pair + at][block, term] for at in range(2) for term in range(terms)],
                axis=0,
            )
            for pair in range(0, devices, 2)
        ]

        def operated(device, term, group):
            if device == 0:
                return early_ref[block, start + term, group]
            return after_ops[(device - 1) * terms + term, group]

        def multiply(low, high):
            apply_operators(low, high, spread_ops, after_left, after_ops)
            for group in range(low, high, WIDE):
                parts = []
                for pair in range(0, devices, 2):
                    rows = jnp.concatenate(
                        [
                            jnp.concatenate(
                                [
                                    operated(pair + at, term, group + side)
                                    for at in range(2)
                                    for term in range(terms)
                                ],
                                axis=1,
                            )
                            for side in range(WIDE)
                        ],
                        axis=0,
                    )
                    parts.append(
                        jnp.dot(rows, columns[pair // 2], preferred_element_type=jnp.float32)
                    )
                while len(parts) > 1:
                    parts = [parts[at] + parts[at + 1] for at in range(0, len(parts), 2)]
                done = parts[0].reshape(WIDE, states, TILE, width)
                for side in range(WIDE):
                    tile = slice((group + side) * TILE, (group + side + 1) * TILE)
                    if first:
                        total[:, tile, :] = done[side]
                    else:
                        total[:, tile, :] = sum_in[block, :, tile, :] + done[side]

        by_live_rows(own_rows, groups, multiply)
        if last:
            mask = live_entries(own_rows, partner_rows, width)
            kept = jnp.where(mask, total[...], 0.0)
            fold_ref[...] += folded(kept * psi_ref[block].astype(jnp.float32))
            sum_out[block] = kept.astype(jnp.bfloat16)

    each_live_block(half, slots, (meta, places, sector_rows, partners, counts), work)


def chunk_call(first, last, chunk, scalars, slots, psi, early, near_left, far_lefts, rights,
               total, after):
    far = len(far_lefts)
    late = 1 + 2 * far
    blocks, states, width = psi.shape[:3]
    groups, wide = width // TILE, states * TILE
    start, terms = chunk
    held = early.shape[1]
    operands = [after, psi, early, near_left, *far_lefts, *rights]
    aliases = {}
    if not first:
        operands.append(total)
        if not last:
            aliases = {len(scalars) + len(operands) - 1: 0}
    sum_dtype = jnp.bfloat16 if last else jnp.float32
    scratch = [
        pltpu.VMEM((late * terms, wide, wide), jnp.bfloat16),
        pltpu.VMEM((late * terms, groups, wide, width), jnp.bfloat16),
        pltpu.VMEM((late * terms, groups, wide, width), jnp.bfloat16),
    ]
    if last:
        scratch.append(pltpu.VMEM((states, width, width), jnp.float32))
    work = 2 * psi.size * terms * ((late + 1) * width + late * (width + wide))
    return pl.pallas_call(
        functools.partial(
            chunk_kernel, first, last, held, start, far, blocks // slots, slots
        ),
        in_specs=in_smem(len(scalars))
        + [pl.BlockSpec(memory_space=pl.ANY)]
        + resident(len(operands) - 1),
        out_specs=resident(2),
        out_shape=[
            jax.ShapeDtypeStruct(psi.shape, sum_dtype),
            jax.ShapeDtypeStruct((8, width), jnp.float32),
        ],
        scratch_shapes=scratch,
        input_output_aliases=aliases,
        compiler_params=pltpu.CompilerParams(
            vmem_limit_bytes=SPARE + 2 * late * terms * wide * (wide + 2 * groups * width)
        ),
        cost_estimate=pl.CostEstimate(
            flops=work // HASTE, bytes_accessed=psi.size // HASTE, transcendentals=0
        ),
        name="chunk",
    )(*scalars, *operands)


def residual_kernel(half, meta, places, sector_rows, partners, counts,
                    folds_ref, psi_ref, own_ref, other_ref, out_ref, quotient_ref):
    slots, width = psi_ref.shape[0], psi_ref.shape[-1]
    step = pl.program_id(0)
    index = lax.rem(meta[1] * half + step, 2 * half)

    @pl.when(step == 0)
    def _():
        quotient_ref[0] = jnp.sum(folds_ref[0:8, :]) / jnp.sum(folds_ref[8:16, :])

    def subtract(sums_ref):
        for slot in range(slots):
            _, live, own_rows, partner_rows = block_facts(
                (meta, places, sector_rows, partners, counts), index, slot
            )
            mask = live_entries(jnp.where(live, own_rows, 0), partner_rows, width)
            scaled = quotient_ref[0] * jnp.where(mask, psi_ref[slot].astype(jnp.float32), 0.0)
            out_ref[slot] = (sums_ref[slot].astype(jnp.float32) - scaled).astype(jnp.bfloat16)

    pl.when(step < half)(functools.partial(subtract, own_ref))
    pl.when(step >= half)(functools.partial(subtract, other_ref))


def residual_call(scalars, folds, psi, own, other):
    sectors, slots, states, width = psi.shape[:4]
    half = sectors // 2
    shape = (None, slots, states, width, width)

    def at_sector(i, meta, places, *_):
        return (places[(meta[1] * half + i) % sectors], 0, 0, 0, 0)

    return pl.pallas_call(
        functools.partial(residual_kernel, half),
        grid_spec=pltpu.PrefetchScalarGridSpec(
            num_scalar_prefetch=len(scalars),
            grid=(sectors,),
            in_specs=[
                pl.BlockSpec(folds.shape, lambda i, *_: (0, 0)),
                pl.BlockSpec(shape, at_sector),
                pl.BlockSpec(shape, lambda i, *_: (jnp.minimum(i, half - 1), 0, 0, 0, 0)),
                pl.BlockSpec(shape, lambda i, *_: (jnp.maximum(i - half, 0), 0, 0, 0, 0)),
            ],
            out_specs=[pl.BlockSpec(shape, at_sector), pl.BlockSpec(memory_space=pltpu.SMEM)],
        ),
        out_shape=[
            jax.ShapeDtypeStruct(psi.shape, jnp.bfloat16),
            jax.ShapeDtypeStruct((1,), jnp.float32),
        ],
        compiler_params=pltpu.CompilerParams(vmem_limit_bytes=20 * MIB),
        cost_estimate=pl.CostEstimate(
            flops=3 * psi.size, bytes_accessed=6 * psi.size, transcendentals=0
        ),
        name="residual",
    )(*scalars, folds, psi, *(sums.reshape((half,) + psi.shape[1:]) for sums in (own, other)))


def on_device(
    devices, rings, psi, left_env, right_env, local_ops, term_op, sector_rows, block_partner,
    block_count,
):
    sectors, slots, states, width = psi.shape[:4]
    terms = left_env.shape[1]
    half = sectors // 2
    me = lax.axis_index("term")
    ring = lax.axis_index("sec")
    core = me % 2
    meta = jnp.stack([ring * sectors, core, me, ring]).astype(jnp.int32)

    near_rows = lax.dynamic_slice_in_dim(sector_rows, ring * sectors, sectors)
    weight = block_count * (near_rows + width // 2)
    order = jnp.arange(sectors, dtype=jnp.int32)
    ahead = (weight[None, :] > weight[:, None]) | (
        (weight[None, :] == weight[:, None]) & (order[None, :] < order[:, None])
    )
    rank = jnp.sum(ahead.astype(jnp.int32), axis=1)
    index = ((rank ^ (rank >> 1)) & 1) * half + (rank >> 1)
    places = jnp.sum(jnp.where(index[None, :] == order[:, None], order[None, :], 0), axis=1)
    scalars = (meta, places, sector_rows, block_partner, block_count)

    def swap(value, bits, axis="term", size=devices):
        return lax.ppermute(value, axis, [(i, i ^ bits) for i in range(size)])

    def to_far_chips(near, received):
        both = jnp.stack([near, received])
        return both, [swap(both, bits) for bits in range(2, devices, 2)]

    chunks = [(at, 1) for at in range(terms)]
    ordered = jnp.roll(places, -core * half)
    mine, theirs, *shares = pack_call(
        chunks, ordered, term_op, local_ops, left_env, right_env
    )
    near_left = swap(theirs, 1)
    both_lefts, far_lefts = to_far_chips(mine, near_left)

    shards, rights = [], []

    def gather(token):
        own = shares[len(shards)]
        if token is not None:
            own, _ = lax.optimization_barrier((own, token))
        moved = [own]
        for distance in range(1, rings):
            pairs = [(i, (i + distance) % rings) for i in range(rings)]
            moved.append(lax.ppermute(own, "sec", pairs))
        shards.append(moved)

    def choose(token):
        mine, other = choose_call(scalars, half, slots, shards[len(rights)], token)
        received = swap(other, 1)
        both, far_rights = to_far_chips(mine, received)
        rights.append([mine, received] + far_rights)
        return both

    gather(None)
    early, live_psi, token, squares = left_call(scalars, terms, psi, mine, both_lefts)
    gather(token)
    token = choose(token)
    total = None
    for at, chunk in enumerate(chunks):
        if len(shards) < len(chunks):
            gather(token)
        if len(rights) < len(chunks):
            token = choose(token)
        last = at == len(chunks) - 1
        total, token = chunk_call(
            at == 0, last, chunk, scalars, slots, live_psi, early, near_left, far_lefts,
            rights[at], total, token,
        )

    other = swap(total, 1)
    folds = jnp.concatenate([token, squares], axis=0)
    folds = folds + swap(folds, 1)
    bits = 1
    while bits < rings:
        folds = folds + swap(folds, bits, "sec", rings)
        bits *= 2
    residual, rayleigh = residual_call(scalars, folds, psi, total, other)
    return residual, rayleigh


def solution(mesh):
    placed = (
        P(("groups", "sec"), None, None, None, None),
        P(("groups", "sec"), "term", None, None),
        P(("groups", "sec"), "term", None, None),
        P(),
        P("term"),
        P("groups"),
        P(("groups", "sec"), None),
        P(("groups", "sec")),
    )
    return jax.shard_map(
        functools.partial(on_device, mesh.shape["term"], mesh.shape["sec"]),
        mesh=mesh,
        in_specs=placed,
        out_specs=(P(("groups", "sec"), None, None, None, None), P("groups")),
        check_vma=False,
    )
```

```python
import functools

import jax
import jax.numpy as jnp
from jax import lax
from jax.experimental import pallas as pl
from jax.experimental.pallas import tpu as pltpu
from jax.sharding import PartitionSpec as P

TILE = 16
WIDE = 2
MIB = 1024 * 1024
SPARE = 4 * MIB
HASTE = 256


def block_facts(scalars, index, slot):
    meta, places, sector_rows, partners, counts = scalars
    sector = places[index]
    live = slot < counts[sector]
    own_rows = sector_rows[meta[0] + sector]
    partner_rows = sector_rows[partners[sector, slot]]
    return sector, live, own_rows, partner_rows


def live_entries(own_rows, partner_rows, width):
    left = lax.broadcasted_iota(jnp.int32, (1, width, width), 1) < own_rows
    right = lax.broadcasted_iota(jnp.int32, (1, width, width), 2) < partner_rows
    return left & right


def folded(values):
    states, width = values.shape[0], values.shape[-1]
    return jnp.sum(values.reshape(states * width // 8, 8, width), axis=0)


def by_live_rows(own_rows, groups, work):
    always = groups // 2
    work(0, always)
    for group in range(always, groups, WIDE):
        pl.when(own_rows > group * TILE)(functools.partial(work, group, group + WIDE))


def spread_operators(ops_ref, chosen, spread_ops, at, states):
    width, wide = ops_ref.shape[-1], states * TILE
    row_state = lax.broadcasted_iota(jnp.int32, (wide, states), 0) // TILE
    column = lax.broadcasted_iota(jnp.int32, (wide, states), 1)
    pick_rows = (row_state == column).astype(jnp.bfloat16)
    row = lax.broadcasted_iota(jnp.int32, (width, wide), 0)
    column_state = lax.broadcasted_iota(jnp.int32, (width, wide), 1) // TILE
    pick_columns = (row == column_state).astype(jnp.bfloat16)
    inner_row = lax.rem(lax.broadcasted_iota(jnp.int32, (wide, wide), 0), TILE)
    inner_column = lax.rem(lax.broadcasted_iota(jnp.int32, (wide, wide), 1), TILE)
    for term in chosen:
        operator = ops_ref[term * states : (term + 1) * states, :]
        rows = jnp.dot(pick_rows, operator, preferred_element_type=jnp.float32)
        full = jnp.dot(
            rows.astype(jnp.bfloat16), pick_columns, preferred_element_type=jnp.float32
        )
        spread_ops[at] = jnp.where(inner_row == inner_column, full, 0.0).astype(jnp.bfloat16)
        at += 1


def multiply_left(lefts, live_psi, after_left):
    terms, groups = after_left.shape[:2]
    states, width = live_psi.shape[0], live_psi.shape[-1]
    for pair in range(states // WIDE):
        columns = jnp.concatenate([live_psi[pair * WIDE + at] for at in range(WIDE)], axis=1)
        done = jnp.dot(lefts, columns, preferred_element_type=jnp.float32).astype(jnp.bfloat16)
        for term in range(terms):
            for at in range(WIDE):
                state = pair * WIDE + at
                after_left[term, :, state * TILE : (state + 1) * TILE, :] = done[
                    term * width : (term + 1) * width, at * width : (at + 1) * width
                ].reshape(groups, TILE, width)


def apply_operators(low, high, spread_ops, after_left, targets):
    width = after_left.shape[-1]
    for group in range(low, high, WIDE):
        for term, (target, lead) in enumerate(targets):
            columns = jnp.concatenate(
                [after_left[term, group + at] for at in range(WIDE)], axis=1
            )
            done = jnp.dot(
                spread_ops[term], columns, preferred_element_type=jnp.float32
            ).astype(jnp.bfloat16)
            for at in range(WIDE):
                target[(*lead, group + at)] = done[:, at * width : (at + 1) * width]


def each_live_block(half, slots, scalars, work):
    meta = scalars[0]

    def visit(block, carry):
        place, slot = block // slots, lax.rem(block, slots)
        sector, live, own_rows, partner_rows = block_facts(
            scalars, meta[1] * half + place, slot
        )
        pl.when(live)(functools.partial(work, block, place, sector, own_rows, partner_rows))
        return carry

    lax.fori_loop(0, half * slots, visit, 0)


def pack_kernel(chunks, half, terms, places, term_op, ops_ref, left_ref, right_ref, *rest):
    payloads, rest = rest[:2], rest[2:]
    shares, sems = rest[: len(chunks)], rest[len(chunks)]
    states, width = ops_ref.shape[1:]
    copied = half * terms * width
    for part, payload in enumerate(payloads):
        for place in range(half):
            pltpu.make_async_copy(
                left_ref.at[places[part * half + place]],
                payload.at[pl.ds(place * terms * width, terms * width)],
                sems.at[part],
            ).start()
    moves = []
    for at, (start, length) in enumerate(chunks):
        move = pltpu.make_async_copy(
            right_ref.at[:, pl.ds(start, length)], shares[at], sems.at[2 + at]
        )
        move.start()
        moves.append(move)
    for payload in payloads:
        for term in range(terms):
            rows = slice(copied + term * states, copied + (term + 1) * states)
            payload[rows, :] = ops_ref[term_op[term]]
    for part, payload in enumerate(payloads):
        whole = payload.at[pl.ds(0, copied)]
        pltpu.make_async_copy(whole, whole, sems.at[part]).wait()
    for move in moves:
        move.wait()


def pack_call(chunks, places, term_op, local_ops, left_env, right_env):
    sectors, terms, width = left_env.shape[:3]
    half, states = sectors // 2, local_ops.shape[1]
    payload = jax.ShapeDtypeStruct((terms * (half * width + states), width), jnp.bfloat16)
    shares = [
        jax.ShapeDtypeStruct((sectors, length, width, width), jnp.bfloat16)
        for start, length in chunks
    ]
    padded = jnp.pad(local_ops, ((0, 0), (0, 0), (0, width - states)))
    return pl.pallas_call(
        functools.partial(pack_kernel, chunks, half, terms),
        in_specs=in_smem(2) + resident(1) + [pl.BlockSpec(memory_space=pltpu.HBM)] * 2,
        out_specs=resident(2 + len(chunks)),
        out_shape=[payload, payload] + shares,
        scratch_shapes=[pltpu.SemaphoreType.DMA((2 + len(chunks),))],
        compiler_params=pltpu.CompilerParams(vmem_limit_bytes=58 * MIB),
        cost_estimate=pl.CostEstimate(
            flops=0, bytes_accessed=4 * left_env.size, transcendentals=0
        ),
        name="pack",
    )(places, term_op, padded, left_env.reshape(sectors, terms * width, width), right_env)


def source_views(payloads):
    views = []
    for payload in payloads:
        views += [payload] if len(payload.shape) == 2 else [payload.at[0], payload.at[1]]
    return views


def term_rows(place, held, start, terms, width):
    return pl.ds(pl.multiple_of((place * held + start) * width, width), terms * width)


def left_kernel(first, held, items, count, afters, half, slots, meta, places, sector_rows,
                partners, counts, *rest):
    scalars = (meta, places, sector_rows, partners, counts)
    psi_ref, rest = rest[afters], rest[afters + 1 :]
    payloads, rest = rest[:count], rest[count:]
    outs, rest = rest[: len(items)], rest[len(items) :]
    token_ref, rest = rest[0], rest[1:]
    if first:
        live_psi, square_ref, spread_ops, after_left, sems = rest
    else:
        live_psi = psi_ref
        spread_ops, after_left = rest
    states, width = live_psi.shape[1], live_psi.shape[-1]
    views = source_views(payloads)

    def fetch(block, sector):
        return pltpu.make_async_copy(
            psi_ref.at[sector, lax.rem(block, slots)], live_psi.at[block], sems.at[block]
        )

    if first:
        each_live_block(
            half, slots, scalars, lambda block, place, sector, *rows: fetch(block, sector).start()
        )
        square_ref[...] = jnp.zeros_like(square_ref)
    at = 0
    for source, start, terms in items:
        operators = views[source][half * held * width :, :]
        spread_operators(operators, range(start, start + terms), spread_ops, at, states)
        at += terms
    token_ref[...] = jnp.zeros_like(token_ref)

    def work(block, place, sector, own_rows, partner_rows):
        if first:
            fetch(block, sector).wait()
            mask = live_entries(own_rows, partner_rows, width)
            kept = jnp.where(mask, live_psi[block], jnp.zeros((), jnp.bfloat16))
            live_psi[block] = kept
            wide_psi = kept.astype(jnp.float32)
            square_ref[...] += folded(wide_psi * wide_psi)
        lefts = [
            views[source][term_rows(place, held, start, terms, width), :]
            for source, start, terms in items
        ]
        multiply_left(jnp.concatenate(lefts, axis=0), live_psi.at[block], after_left)
        targets = [
            (outs[at], (block, term))
            for at, (source, start, terms) in enumerate(items)
            for term in range(terms)
        ]
        by_live_rows(
            own_rows,
            width // TILE,
            lambda low, high: apply_operators(low, high, spread_ops, after_left, targets),
        )

    each_live_block(half, slots, scalars, work)


def resident(count):
    return [pl.BlockSpec(memory_space=pltpu.VMEM)] * count


def in_smem(count):
    return [pl.BlockSpec(memory_space=pltpu.SMEM)] * count


def left_call(first, scalars, held, items, shape, psi, payloads, afters):
    blocks, slots, states, width = shape
    groups, wide = width // TILE, states * TILE
    every = sum(terms for source, start, terms in items)
    fold_shape = jax.ShapeDtypeStruct((8, width), jnp.float32)
    out_shape = [
        jax.ShapeDtypeStruct((blocks, terms, groups, wide, width), jnp.bfloat16)
        for source, start, terms in items
    ] + [fold_shape]
    scratch = [
        pltpu.VMEM((every, wide, wide), jnp.bfloat16),
        pltpu.VMEM((every, groups, wide, width), jnp.bfloat16),
    ]
    if first:
        live_psi = jax.ShapeDtypeStruct((blocks, states, width, width), jnp.bfloat16)
        out_shape += [live_psi, fold_shape]
        scratch.append(pltpu.SemaphoreType.DMA((blocks,)))
    psi_spec = [pl.BlockSpec(memory_space=pltpu.HBM)] if first else resident(1)
    return pl.pallas_call(
        functools.partial(
            left_kernel, first, held, items, len(payloads), len(afters), blocks // slots, slots
        ),
        in_specs=in_smem(len(scalars))
        + [pl.BlockSpec(memory_space=pl.ANY)] * len(afters)
        + psi_spec
        + resident(len(payloads)),
        out_specs=resident(len(out_shape)),
        out_shape=out_shape,
        scratch_shapes=scratch,
        compiler_params=pltpu.CompilerParams(
            vmem_limit_bytes=max(
                32 * MIB if first else 0,
                SPARE + 2 * every * (wide * wide + groups * wide * width),
            )
        ),
        cost_estimate=pl.CostEstimate(
            flops=psi.size * every * (width + wide) // HASTE,
            bytes_accessed=psi.size // HASTE,
            transcendentals=0,
        ),
        name="left",
    )(*scalars, *afters, psi, *payloads)


def choose_kernel(devices, afters, sectors, half, slots, meta, places, partners, *rest):
    rest = rest[afters:]
    shards, (mine_ref, other_ref) = rest[:devices], rest[devices:]
    for part, out_ref in enumerate((mine_ref, other_ref)):
        for block in range(half * slots):
            sector = places[(meta[1] ^ part) * half + block // slots]
            partner = partners[sector, block % slots]
            away = lax.rem(meta[3] + devices - partner // sectors, devices)
            place = lax.rem(partner, sectors)
            for distance in range(devices):
                @pl.when(away == distance)
                def _(distance=distance, place=place, block=block, out_ref=out_ref):
                    out_ref[block] = shards[distance][place]


def choose_call(scalars, half, slots, shards, afters):
    meta, places, _, partners, _ = scalars
    sectors, terms, width = shards[0].shape[:3]
    chosen = jax.ShapeDtypeStruct((half * slots, terms, width, width), jnp.bfloat16)
    return pl.pallas_call(
        functools.partial(choose_kernel, len(shards), len(afters), sectors, half, slots),
        in_specs=in_smem(3)
        + [pl.BlockSpec(memory_space=pl.ANY)] * len(afters)
        + resident(len(shards)),
        out_specs=resident(2),
        out_shape=[chosen, chosen],
        compiler_params=pltpu.CompilerParams(vmem_limit_bytes=SPARE),
        cost_estimate=pl.CostEstimate(
            flops=0, bytes_accessed=8 * half * slots * terms * width * width, transcendentals=0
        ),
        name="choose",
    )(meta, places, partners, *afters, *shards)


def chunk_kernel(first, last, held, chunk, ahead, late, count, half, slots,
                 meta, places, sector_rows, partners, counts, after_ref, psi_ref, *rest):
    start, terms = chunk
    early_refs, rest = rest[: len(ahead)], rest[len(ahead) :]
    payloads, rest = rest[:count], rest[count:]
    near_rights, rest = rest[:2], rest[2:]
    devices = len(ahead) + len(late)
    far_rights, rest = rest[: devices // 2 - 1], rest[devices // 2 - 1 :]
    if not first:
        sum_in, rest = rest[0], rest[1:]
    sum_out, fold_ref, *rest = rest
    if late:
        spread_ops, after_left, after_ops, *rest = rest
    states, width = psi_ref.shape[1], psi_ref.shape[-1]
    groups = width // TILE
    views = dict(zip(late, source_views(payloads)))
    rights = list(near_rights) + [right.at[side] for right in far_rights for side in (0, 1)]
    for at, source in enumerate(late):
        operators = views[source][half * held * width :, :]
        spread_operators(operators, range(start, start + terms), spread_ops, at * terms, states)
    fold_ref[...] = jnp.zeros_like(fold_ref)
    if last:
        sum_out[...] = jnp.zeros_like(sum_out)

    def work(block, place, sector, own_rows, partner_rows):
        total = rest[0] if last else sum_out.at[block]
        if late:
            lefts = [
                views[source][term_rows(place, held, start, terms, width), :] for source in late
            ]
            multiply_left(jnp.concatenate(lefts, axis=0), psi_ref.at[block], after_left)
        columns = [
            jnp.concatenate(
                [rights[pair + at][block, term] for at in range(2) for term in range(terms)],
                axis=0,
            )
            for pair in range(0, devices, 2)
        ]

        def operated(device, term, group):
            if device in ahead:
                return early_refs[ahead.index(device)][block, term, group]
            return after_ops[late.index(device) * terms + term, group]

        def multiply(low, high):
            if late:
                targets = [(after_ops, (term,)) for term in range(len(late) * terms)]
                apply_operators(low, high, spread_ops, after_left, targets)
            for group in range(low, high, WIDE):
                parts = []
                for pair in range(0, devices, 2):
                    rows = jnp.concatenate(
                        [
                            jnp.concatenate(
                                [
                                    operated(pair + at, term, group + side)
                                    for at in range(2)
                                    for term in range(terms)
                                ],
                                axis=1,
                            )
                            for side in range(WIDE)
                        ],
                        axis=0,
                    )
                    parts.append(
                        jnp.dot(rows, columns[pair // 2], preferred_element_type=jnp.float32)
                    )
                while len(parts) > 1:
                    parts = [parts[at] + parts[at + 1] for at in range(0, len(parts), 2)]
                done = parts[0].reshape(WIDE, states, TILE, width)
                for side in range(WIDE):
                    tile = slice((group + side) * TILE, (group + side + 1) * TILE)
                    if first:
                        total[:, tile, :] = done[side]
                    else:
                        total[:, tile, :] = sum_in[block, :, tile, :] + done[side]

        by_live_rows(own_rows, groups, multiply)
        if last:
            mask = live_entries(own_rows, partner_rows, width)
            kept = jnp.where(mask, total[...], 0.0)
            fold_ref[...] += folded(kept * psi_ref[block].astype(jnp.float32))
            sum_out[block] = kept.astype(jnp.bfloat16)

    each_live_block(half, slots, (meta, places, sector_rows, partners, counts), work)


def chunk_call(first, last, held, chunk, ahead, late, scalars, slots, psi, early, payloads,
               rights, total, after):
    blocks, states, width = psi.shape[:3]
    groups, wide = width // TILE, states * TILE
    start, terms = chunk
    operands = [after, psi, *early, *payloads, *rights]
    aliases = {}
    if not first:
        operands.append(total)
        if not last:
            aliases = {len(scalars) + len(operands) - 1: 0}
    sum_dtype = jnp.bfloat16 if last else jnp.float32
    every = len(late) * terms
    scratch = []
    if late:
        scratch += [
            pltpu.VMEM((every, wide, wide), jnp.bfloat16),
            pltpu.VMEM((every, groups, wide, width), jnp.bfloat16),
            pltpu.VMEM((every, groups, wide, width), jnp.bfloat16),
        ]
    if last:
        scratch.append(pltpu.VMEM((states, width, width), jnp.float32))
    work = psi.size * terms * ((len(ahead) + len(late)) * width + len(late) * (width + wide))
    return pl.pallas_call(
        functools.partial(
            chunk_kernel, first, last, held, chunk, ahead, late, len(payloads),
            blocks // slots, slots,
        ),
        in_specs=in_smem(len(scalars))
        + [pl.BlockSpec(memory_space=pl.ANY)]
        + resident(len(operands) - 1),
        out_specs=resident(2),
        out_shape=[
            jax.ShapeDtypeStruct(psi.shape, sum_dtype),
            jax.ShapeDtypeStruct((8, width), jnp.float32),
        ],
        scratch_shapes=scratch,
        input_output_aliases=aliases,
        compiler_params=pltpu.CompilerParams(
            vmem_limit_bytes=SPARE + 2 * every * wide * (wide + 2 * groups * width)
        ),
        cost_estimate=pl.CostEstimate(
            flops=work // HASTE, bytes_accessed=psi.size // HASTE, transcendentals=0
        ),
        name="chunk",
    )(*scalars, *operands)


def residual_kernel(half, slots, meta, places, sector_rows, partners, counts,
                    folds_ref, live_psi, own_ref, other_ref, psi_ref, out_ref, quotient_ref,
                    other_psi, staged, read_sems, write_sems):
    scalars = (meta, places, sector_rows, partners, counts)
    blocks, width = own_ref.shape[0], own_ref.shape[-1]
    depth = staged.shape[0]

    def where(block, side):
        index = (meta[1] ^ side) * half + block // slots
        return places[index], block % slots, index

    def read(block):
        sector, slot, _ = where(block, 1)
        return pltpu.make_async_copy(
            psi_ref.at[sector, slot], other_psi.at[block], read_sems.at[block]
        )

    def write(step):
        sector, slot, _ = where(step % blocks, step // blocks)
        return pltpu.make_async_copy(
            staged.at[step % depth], out_ref.at[sector, slot], write_sems.at[step % depth]
        )

    for block in range(blocks):
        read(block).start()
    quotient = jnp.sum(folds_ref[0:8, :]) / jnp.sum(folds_ref[8:16, :])
    quotient_ref[0] = quotient
    for step in range(2 * blocks):
        block, side = step % blocks, step // blocks
        if step >= depth:
            write(step - depth).wait()
        sector, slot, index = where(block, side)
        _, live, own_rows, partner_rows = block_facts(scalars, index, slot)
        mask = live_entries(jnp.where(live, own_rows, 0), partner_rows, width)
        if side:
            read(block).wait()
            values, sums = other_psi[block], other_ref[block]
        else:
            values, sums = live_psi[block], own_ref[block]
        scaled = quotient * jnp.where(mask, values.astype(jnp.float32), 0.0)
        staged[step % depth] = (sums.astype(jnp.float32) - scaled).astype(jnp.bfloat16)
        write(step).start()
    for step in range(2 * blocks - min(depth, 2 * blocks), 2 * blocks):
        write(step).wait()


def residual_call(scalars, folds, psi, live_psi, own, other):
    sectors, slots, states, width = psi.shape[:4]
    blocks = own.shape[0]
    depth = 4
    in_hbm = [pl.BlockSpec(memory_space=pltpu.HBM)]
    return pl.pallas_call(
        functools.partial(residual_kernel, sectors // 2, slots),
        in_specs=in_smem(len(scalars)) + resident(4) + in_hbm,
        out_specs=in_hbm + in_smem(1),
        out_shape=[
            jax.ShapeDtypeStruct(psi.shape, jnp.bfloat16),
            jax.ShapeDtypeStruct((1,), jnp.float32),
        ],
        scratch_shapes=[
            pltpu.VMEM((blocks, states, width, width), jnp.bfloat16),
            pltpu.VMEM((depth, states, width, width), jnp.bfloat16),
            pltpu.SemaphoreType.DMA((blocks,)),
            pltpu.SemaphoreType.DMA((depth,)),
        ],
        compiler_params=pltpu.CompilerParams(vmem_limit_bytes=44 * MIB),
        cost_estimate=pl.CostEstimate(
            flops=3 * psi.size, bytes_accessed=6 * psi.size, transcendentals=0
        ),
        name="residual",
    )(*scalars, folds, live_psi, own, other, psi)


def on_device(
    devices, rings, psi, left_env, right_env, local_ops, term_op, sector_rows, block_partner,
    block_count,
):
    sectors, slots, states, width = psi.shape[:4]
    terms = left_env.shape[1]
    half = sectors // 2
    me = lax.axis_index("term")
    ring = lax.axis_index("sec")
    core = me % 2
    meta = jnp.stack([ring * sectors, core, me, ring]).astype(jnp.int32)

    near_rows = lax.dynamic_slice_in_dim(sector_rows, ring * sectors, sectors)
    weight = block_count * (near_rows + width // 2)
    order = jnp.arange(sectors, dtype=jnp.int32)
    ahead = (weight[None, :] > weight[:, None]) | (
        (weight[None, :] == weight[:, None]) & (order[None, :] < order[:, None])
    )
    rank = jnp.sum(ahead.astype(jnp.int32), axis=1)
    index = ((rank ^ (rank >> 1)) & 1) * half + (rank >> 1)
    places = jnp.sum(jnp.where(index[None, :] == order[:, None], order[None, :], 0), axis=1)
    scalars = (meta, places, sector_rows, block_partner, block_count)

    def swap(value, bits, axis="term", size=devices):
        return lax.ppermute(value, axis, [(i, i ^ bits) for i in range(size)])

    def to_far_chips(near, received):
        both = jnp.stack([near, received])
        return both, [swap(both, bits) for bits in range(2, devices, 2)]

    chunks = [(at, 1) for at in range(terms)]
    ordered = jnp.roll(places, -core * half)
    mine, theirs, *shares = pack_call(
        chunks, ordered, term_op, local_ops, left_env, right_env
    )
    near_left = swap(theirs, 1)
    both_lefts, far_lefts = to_far_chips(mine, near_left)

    shards, rights = [], []

    def gather(token):
        own = shares[len(shards)]
        if token is not None:
            own, _ = lax.optimization_barrier((own, token))
        moved = [own]
        for distance in range(1, rings):
            pairs = [(i, (i + distance) % rings) for i in range(rings)]
            moved.append(lax.ppermute(own, "sec", pairs))
        shards.append(moved)

    def choose(token):
        afters = [token] + (rights[-1][2:] if rights else [])
        mine, other = choose_call(scalars, half, slots, shards[len(rights)], afters)
        received = swap(other, 1)
        both, far_rights = to_far_chips(mine, received)
        rights.append([mine, received] + far_rights)
        return both

    products = {}
    shape = (half * slots, slots, states, width)
    far = tuple(range(2, devices))

    def go_left(sources, which, token, first=False, waits=()):
        items = [(source, *chunks[at]) for at in which for source in sources]
        near = [source for source in sources if source < 2]
        payloads = [(mine, near_left)[source] for source in near]
        if len(near) < len(sources):
            payloads += far_lefts
        renamed = [(sources.index(source), start, count) for source, start, count in items]
        outs = left_call(
            first, scalars, terms, renamed, shape, psi if first else live_psi, payloads,
            [token, *waits],
        )
        for at, out in zip([(at, source) for at in which for source in sources], outs):
            products[at] = out
        return outs[len(items) :]

    every = range(len(chunks))
    gather(None)
    token, live_psi, squares = go_left((0,), every, both_lefts, True)
    gather(token)
    token = choose(token)
    token, = go_left((1,), every, token, waits=far_lefts)
    total = None
    for at, chunk in enumerate(chunks):
        last = at == len(chunks) - 1
        if len(shards) < len(chunks):
            gather(token)
        if len(rights) < len(chunks):
            token = choose(token)
        ahead = tuple(source for source in range(devices) if (at, source) in products)
        late = tuple(source for source in range(devices) if source not in ahead)
        total, token = chunk_call(
            at == 0, last, terms, chunk, ahead, late, scalars, slots, live_psi,
            [products.pop((at, source)) for source in ahead], far_lefts if late else [],
            rights[at], total, token,
        )
        if at == len(chunks) - 3:
            token, = go_left(far, [len(chunks) - 1], token)

    other = swap(total, 1)
    folds = jnp.concatenate([token, squares], axis=0)
    folds = folds + swap(folds, 1)
    bits = 1
    while bits < rings:
        folds = folds + swap(folds, bits, "sec", rings)
        bits *= 2
    residual, rayleigh = residual_call(scalars, folds, psi, live_psi, total, other)
    return residual, rayleigh


def solution(mesh):
    placed = (
        P(("groups", "sec"), None, None, None, None),
        P(("groups", "sec"), "term", None, None),
        P(("groups", "sec"), "term", None, None),
        P(),
        P("term"),
        P("groups"),
        P(("groups", "sec"), None),
        P(("groups", "sec")),
    )
    return jax.shard_map(
        functools.partial(on_device, mesh.shape["term"], mesh.shape["sec"]),
        mesh=mesh,
        in_specs=placed,
        out_specs=(P(("groups", "sec"), None, None, None, None), P("groups")),
        check_vma=False,
    )
```

```python
import functools

import jax
import jax.numpy as jnp
from jax import lax
from jax.experimental import pallas as pl
from jax.experimental.pallas import tpu as pltpu
from jax.sharding import PartitionSpec as P

TILE = 16
WIDE = 2
MIB = 1024 * 1024
SPARE = 4 * MIB
HASTE = 256


def block_facts(scalars, index, slot):
    meta, places, sector_rows, partners, counts = scalars
    sector = places[index]
    live = slot < counts[sector]
    own_rows = sector_rows[meta[0] + sector]
    partner_rows = sector_rows[partners[sector, slot]]
    return sector, live, own_rows, partner_rows


def live_entries(own_rows, partner_rows, width):
    left = lax.broadcasted_iota(jnp.int32, (1, width, width), 1) < own_rows
    right = lax.broadcasted_iota(jnp.int32, (1, width, width), 2) < partner_rows
    return left & right


def folded(values):
    states, width = values.shape[0], values.shape[-1]
    return jnp.sum(values.reshape(states * width // 8, 8, width), axis=0)


def by_live_rows(own_rows, groups, work):
    always = groups // 2
    work(0, always)
    for group in range(always, groups, WIDE):
        pl.when(own_rows > group * TILE)(functools.partial(work, group, group + WIDE))


def spread_operators(ops_ref, chosen, spread_ops, at, states):
    width, wide = ops_ref.shape[-1], states * TILE
    row_state = lax.broadcasted_iota(jnp.int32, (wide, states), 0) // TILE
    column = lax.broadcasted_iota(jnp.int32, (wide, states), 1)
    pick_rows = (row_state == column).astype(jnp.bfloat16)
    row = lax.broadcasted_iota(jnp.int32, (width, wide), 0)
    column_state = lax.broadcasted_iota(jnp.int32, (width, wide), 1) // TILE
    pick_columns = (row == column_state).astype(jnp.bfloat16)
    inner_row = lax.rem(lax.broadcasted_iota(jnp.int32, (wide, wide), 0), TILE)
    inner_column = lax.rem(lax.broadcasted_iota(jnp.int32, (wide, wide), 1), TILE)
    for term in chosen:
        operator = ops_ref[term * states : (term + 1) * states, :]
        rows = jnp.dot(pick_rows, operator, preferred_element_type=jnp.float32)
        full = jnp.dot(
            rows.astype(jnp.bfloat16), pick_columns, preferred_element_type=jnp.float32
        )
        spread_ops[at] = jnp.where(inner_row == inner_column, full, 0.0).astype(jnp.bfloat16)
        at += 1


def multiply_left(lefts, live_psi, after_left):
    terms, groups = after_left.shape[:2]
    states, width = live_psi.shape[0], live_psi.shape[-1]
    for pair in range(states // WIDE):
        columns = jnp.concatenate([live_psi[pair * WIDE + at] for at in range(WIDE)], axis=1)
        done = jnp.dot(lefts, columns, preferred_element_type=jnp.float32).astype(jnp.bfloat16)
        for term in range(terms):
            for at in range(WIDE):
                state = pair * WIDE + at
                after_left[term, :, state * TILE : (state + 1) * TILE, :] = done[
                    term * width : (term + 1) * width, at * width : (at + 1) * width
                ].reshape(groups, TILE, width)


def apply_operators(low, high, spread_ops, after_left, targets):
    width = after_left.shape[-1]
    for group in range(low, high, WIDE):
        for term, (target, lead) in enumerate(targets):
            columns = jnp.concatenate(
                [after_left[term, group + at] for at in range(WIDE)], axis=1
            )
            done = jnp.dot(
                spread_ops[term], columns, preferred_element_type=jnp.float32
            ).astype(jnp.bfloat16)
            for at in range(WIDE):
                target[(*lead, group + at)] = done[:, at * width : (at + 1) * width]


def each_live_block(half, slots, scalars, work):
    meta = scalars[0]

    def visit(block, carry):
        place, slot = block // slots, lax.rem(block, slots)
        sector, live, own_rows, partner_rows = block_facts(
            scalars, meta[1] * half + place, slot
        )
        pl.when(live)(functools.partial(work, block, place, sector, own_rows, partner_rows))
        return carry

    lax.fori_loop(0, half * slots, visit, 0)


def pack_kernel(chunks, half, terms, places, term_op, ops_ref, left_ref, right_ref, *rest):
    payloads, rest = rest[:2], rest[2:]
    shares, sems = rest[: len(chunks)], rest[len(chunks)]
    states, width = ops_ref.shape[1], left_ref.shape[-1]
    copied = half * terms * width
    for part, payload in enumerate(payloads):
        for place in range(half):
            pltpu.make_async_copy(
                left_ref.at[places[part * half + place]],
                payload.at[pl.ds(place * terms * width, terms * width)],
                sems.at[part],
            ).start()
    moves = []
    for at, (start, length) in enumerate(chunks):
        move = pltpu.make_async_copy(
            right_ref.at[:, pl.ds(start, length)], shares[at], sems.at[2 + at]
        )
        move.start()
        moves.append(move)
    for payload in payloads:
        for term in range(terms):
            rows = slice(copied + term * states, copied + (term + 1) * states)
            payload[rows, :] = jnp.zeros((states, width), jnp.bfloat16)
            payload[rows, :states] = ops_ref[term_op[term]]
    for part, payload in enumerate(payloads):
        whole = payload.at[pl.ds(0, copied)]
        pltpu.make_async_copy(whole, whole, sems.at[part]).wait()
    for move in moves:
        move.wait()


def pack_call(chunks, places, term_op, local_ops, left_env, right_env):
    sectors, terms, width = left_env.shape[:3]
    half, states = sectors // 2, local_ops.shape[1]
    payload = jax.ShapeDtypeStruct((terms * (half * width + states), width), jnp.bfloat16)
    shares = [
        jax.ShapeDtypeStruct((sectors, length, width, width), jnp.bfloat16)
        for start, length in chunks
    ]
    return pl.pallas_call(
        functools.partial(pack_kernel, chunks, half, terms),
        in_specs=in_smem(2) + resident(1) + [pl.BlockSpec(memory_space=pltpu.HBM)] * 2,
        out_specs=resident(2 + len(chunks)),
        out_shape=[payload, payload] + shares,
        scratch_shapes=[pltpu.SemaphoreType.DMA((2 + len(chunks),))],
        compiler_params=pltpu.CompilerParams(vmem_limit_bytes=58 * MIB),
        cost_estimate=pl.CostEstimate(
            flops=0, bytes_accessed=4 * left_env.size, transcendentals=0
        ),
        name="pack",
    )(places, term_op, local_ops, left_env.reshape(sectors, terms * width, width), right_env)


def source_views(payloads):
    views = []
    for payload in payloads:
        views += [payload] if len(payload.shape) == 2 else [payload.at[0], payload.at[1]]
    return views


def term_rows(place, held, start, terms, width):
    return pl.ds(pl.multiple_of((place * held + start) * width, width), terms * width)


def left_kernel(first, held, items, count, afters, half, slots, meta, places, sector_rows,
                partners, counts, *rest):
    scalars = (meta, places, sector_rows, partners, counts)
    psi_ref, rest = rest[afters], rest[afters + 1 :]
    payloads, rest = rest[:count], rest[count:]
    outs, rest = rest[: len(items)], rest[len(items) :]
    token_ref, rest = rest[0], rest[1:]
    if first:
        live_psi, square_ref, spread_ops, after_left, sems = rest
    else:
        live_psi = psi_ref
        spread_ops, after_left = rest
    states, width = live_psi.shape[1], live_psi.shape[-1]
    views = source_views(payloads)

    def fetch(block, sector):
        return pltpu.make_async_copy(
            psi_ref.at[sector, lax.rem(block, slots)], live_psi.at[block], sems.at[block]
        )

    if first:
        each_live_block(
            half, slots, scalars, lambda block, place, sector, *rows: fetch(block, sector).start()
        )
        square_ref[...] = jnp.zeros_like(square_ref)
    at = 0
    for source, start, terms in items:
        operators = views[source][half * held * width :, :]
        spread_operators(operators, range(start, start + terms), spread_ops, at, states)
        at += terms
    token_ref[...] = jnp.zeros_like(token_ref)

    def work(block, place, sector, own_rows, partner_rows):
        if first:
            fetch(block, sector).wait()
            mask = live_entries(own_rows, partner_rows, width)
            kept = jnp.where(mask, live_psi[block], jnp.zeros((), jnp.bfloat16))
            live_psi[block] = kept
            wide_psi = kept.astype(jnp.float32)
            square_ref[...] += folded(wide_psi * wide_psi)
        lefts = [
            views[source][term_rows(place, held, start, terms, width), :]
            for source, start, terms in items
        ]
        multiply_left(jnp.concatenate(lefts, axis=0), live_psi.at[block], after_left)
        targets = [
            (outs[at], (block, term))
            for at, (source, start, terms) in enumerate(items)
            for term in range(terms)
        ]
        by_live_rows(
            own_rows,
            width // TILE,
            lambda low, high: apply_operators(low, high, spread_ops, after_left, targets),
        )

    each_live_block(half, slots, scalars, work)


def resident(count):
    return [pl.BlockSpec(memory_space=pltpu.VMEM)] * count


def in_smem(count):
    return [pl.BlockSpec(memory_space=pltpu.SMEM)] * count


def left_call(first, scalars, held, items, shape, psi, payloads, afters):
    blocks, slots, states, width = shape
    groups, wide = width // TILE, states * TILE
    every = sum(terms for source, start, terms in items)
    fold_shape = jax.ShapeDtypeStruct((8, width), jnp.float32)
    out_shape = [
        jax.ShapeDtypeStruct((blocks, terms, groups, wide, width), jnp.bfloat16)
        for source, start, terms in items
    ] + [fold_shape]
    scratch = [
        pltpu.VMEM((every, wide, wide), jnp.bfloat16),
        pltpu.VMEM((every, groups, wide, width), jnp.bfloat16),
    ]
    if first:
        live_psi = jax.ShapeDtypeStruct((blocks, states, width, width), jnp.bfloat16)
        out_shape += [live_psi, fold_shape]
        scratch.append(pltpu.SemaphoreType.DMA((blocks,)))
    psi_spec = [pl.BlockSpec(memory_space=pltpu.HBM)] if first else resident(1)
    return pl.pallas_call(
        functools.partial(
            left_kernel, first, held, items, len(payloads), len(afters), blocks // slots, slots
        ),
        in_specs=in_smem(len(scalars))
        + [pl.BlockSpec(memory_space=pl.ANY)] * len(afters)
        + psi_spec
        + resident(len(payloads)),
        out_specs=resident(len(out_shape)),
        out_shape=out_shape,
        scratch_shapes=scratch,
        compiler_params=pltpu.CompilerParams(
            vmem_limit_bytes=max(
                28 * MIB if first else 0,
                SPARE + 2 * every * (wide * wide + groups * wide * width),
            )
        ),
        cost_estimate=pl.CostEstimate(
            flops=psi.size * every * (width + wide) // HASTE,
            bytes_accessed=psi.size // HASTE,
            transcendentals=0,
        ),
        name="left",
    )(*scalars, *afters, psi, *payloads)


def choose_kernel(devices, afters, sectors, half, slots, meta, places, partners, *rest):
    rest = rest[afters:]
    shards, (mine_ref, other_ref) = rest[:devices], rest[devices:]
    for part, out_ref in enumerate((mine_ref, other_ref)):
        for block in range(half * slots):
            sector = places[(meta[1] ^ part) * half + block // slots]
            partner = partners[sector, block % slots]
            away = lax.rem(meta[3] + devices - partner // sectors, devices)
            place = lax.rem(partner, sectors)
            for distance in range(devices):
                @pl.when(away == distance)
                def _(distance=distance, place=place, block=block, out_ref=out_ref):
                    out_ref[block] = shards[distance][place]


def choose_call(scalars, half, slots, shards, afters):
    meta, places, _, partners, _ = scalars
    sectors, terms, width = shards[0].shape[:3]
    chosen = jax.ShapeDtypeStruct((half * slots, terms, width, width), jnp.bfloat16)
    return pl.pallas_call(
        functools.partial(choose_kernel, len(shards), len(afters), sectors, half, slots),
        in_specs=in_smem(3)
        + [pl.BlockSpec(memory_space=pl.ANY)] * len(afters)
        + resident(len(shards)),
        out_specs=resident(2),
        out_shape=[chosen, chosen],
        compiler_params=pltpu.CompilerParams(vmem_limit_bytes=SPARE),
        cost_estimate=pl.CostEstimate(
            flops=0, bytes_accessed=8 * half * slots * terms * width * width, transcendentals=0
        ),
        name="choose",
    )(meta, places, partners, *afters, *shards)


def chunk_kernel(first, last, held, chunk, ahead, late, count, half, slots,
                 meta, places, sector_rows, partners, counts, after_ref, psi_ref, *rest):
    start, terms = chunk
    early_refs, rest = rest[: len(ahead)], rest[len(ahead) :]
    payloads, rest = rest[:count], rest[count:]
    near_rights, rest = rest[:2], rest[2:]
    devices = len(ahead) + len(late)
    far_rights, rest = rest[: devices // 2 - 1], rest[devices // 2 - 1 :]
    if not first:
        sum_in, rest = rest[0], rest[1:]
    sum_out, fold_ref, *rest = rest
    if late:
        spread_ops, after_left, after_ops, *rest = rest
    states, width = psi_ref.shape[1], psi_ref.shape[-1]
    groups = width // TILE
    views = dict(zip(late, source_views(payloads)))
    rights = list(near_rights) + [right.at[side] for right in far_rights for side in (0, 1)]
    for at, source in enumerate(late):
        operators = views[source][half * held * width :, :]
        spread_operators(operators, range(start, start + terms), spread_ops, at * terms, states)
    fold_ref[...] = jnp.zeros_like(fold_ref)
    if last:
        sum_out[...] = jnp.zeros_like(sum_out)

    def work(block, place, sector, own_rows, partner_rows):
        total = rest[0] if last else sum_out.at[block]
        if late:
            lefts = [
                views[source][term_rows(place, held, start, terms, width), :] for source in late
            ]
            multiply_left(jnp.concatenate(lefts, axis=0), psi_ref.at[block], after_left)
        columns = [
            jnp.concatenate(
                [rights[pair + at][block, term] for at in range(2) for term in range(terms)],
                axis=0,
            )
            for pair in range(0, devices, 2)
        ]

        def operated(device, term, group):
            if device in ahead:
                return early_refs[ahead.index(device)][block, term, group]
            return after_ops[late.index(device) * terms + term, group]

        def multiply(low, high):
            if late:
                targets = [(after_ops, (term,)) for term in range(len(late) * terms)]
                apply_operators(low, high, spread_ops, after_left, targets)
            for group in range(low, high, WIDE):
                parts = []
                for pair in range(0, devices, 2):
                    rows = jnp.concatenate(
                        [
                            jnp.concatenate(
                                [
                                    operated(pair + at, term, group + side)
                                    for at in range(2)
                                    for term in range(terms)
                                ],
                                axis=1,
                            )
                            for side in range(WIDE)
                        ],
                        axis=0,
                    )
                    parts.append(
                        jnp.dot(rows, columns[pair // 2], preferred_element_type=jnp.float32)
                    )
                while len(parts) > 1:
                    parts = [parts[at] + parts[at + 1] for at in range(0, len(parts), 2)]
                done = parts[0].reshape(WIDE, states, TILE, width)
                for side in range(WIDE):
                    tile = slice((group + side) * TILE, (group + side + 1) * TILE)
                    if first:
                        total[:, tile, :] = done[side]
                    else:
                        total[:, tile, :] = sum_in[block, :, tile, :] + done[side]

        by_live_rows(own_rows, groups, multiply)
        if last:
            mask = live_entries(own_rows, partner_rows, width)
            kept = jnp.where(mask, total[...], 0.0)
            fold_ref[...] += folded(kept * psi_ref[block].astype(jnp.float32))
            sum_out[block] = kept.astype(jnp.bfloat16)

    each_live_block(half, slots, (meta, places, sector_rows, partners, counts), work)


def chunk_call(first, last, held, chunk, ahead, late, scalars, slots, psi, early, payloads,
               rights, total, after):
    blocks, states, width = psi.shape[:3]
    groups, wide = width // TILE, states * TILE
    start, terms = chunk
    operands = [after, psi, *early, *payloads, *rights]
    aliases = {}
    if not first:
        operands.append(total)
        if not last:
            aliases = {len(scalars) + len(operands) - 1: 0}
    sum_dtype = jnp.bfloat16 if last else jnp.float32
    every = len(late) * terms
    scratch = []
    if late:
        scratch += [
            pltpu.VMEM((every, wide, wide), jnp.bfloat16),
            pltpu.VMEM((every, groups, wide, width), jnp.bfloat16),
            pltpu.VMEM((every, groups, wide, width), jnp.bfloat16),
        ]
    if last:
        scratch.append(pltpu.VMEM((states, width, width), jnp.float32))
    work = psi.size * terms * ((len(ahead) + len(late)) * width + len(late) * (width + wide))
    return pl.pallas_call(
        functools.partial(
            chunk_kernel, first, last, held, chunk, ahead, late, len(payloads),
            blocks // slots, slots,
        ),
        in_specs=in_smem(len(scalars))
        + [pl.BlockSpec(memory_space=pl.ANY)]
        + resident(len(operands) - 1),
        out_specs=resident(2),
        out_shape=[
            jax.ShapeDtypeStruct(psi.shape, sum_dtype),
            jax.ShapeDtypeStruct((8, width), jnp.float32),
        ],
        scratch_shapes=scratch,
        input_output_aliases=aliases,
        compiler_params=pltpu.CompilerParams(
            vmem_limit_bytes=SPARE + 2 * every * wide * (wide + 2 * groups * width)
        ),
        cost_estimate=pl.CostEstimate(
            flops=work // HASTE, bytes_accessed=psi.size // HASTE, transcendentals=0
        ),
        name="chunk",
    )(*scalars, *operands)


def residual_kernel(half, slots, meta, places, sector_rows, partners, counts,
                    folds_ref, live_psi, own_ref, other_ref, psi_ref, out_ref, quotient_ref,
                    other_psi, staged, read_sems, write_sems):
    scalars = (meta, places, sector_rows, partners, counts)
    blocks, width = own_ref.shape[0], own_ref.shape[-1]
    depth = staged.shape[0]

    def where(block, side):
        index = (meta[1] ^ side) * half + block // slots
        return places[index], block % slots, index

    def read(block):
        sector, slot, _ = where(block, 1)
        return pltpu.make_async_copy(
            psi_ref.at[sector, slot], other_psi.at[block], read_sems.at[block]
        )

    def write(step):
        sector, slot, _ = where(step % blocks, step // blocks)
        return pltpu.make_async_copy(
            staged.at[step % depth], out_ref.at[sector, slot], write_sems.at[step % depth]
        )

    for block in range(blocks):
        read(block).start()
    quotient = jnp.sum(folds_ref[0:8, :]) / jnp.sum(folds_ref[8:16, :])
    quotient_ref[0] = quotient
    for step in range(2 * blocks):
        block, side = step % blocks, step // blocks
        if step >= depth:
            write(step - depth).wait()
        sector, slot, index = where(block, side)
        _, live, own_rows, partner_rows = block_facts(scalars, index, slot)
        mask = live_entries(jnp.where(live, own_rows, 0), partner_rows, width)
        if side:
            read(block).wait()
            values, sums = other_psi[block], other_ref[block]
        else:
            values, sums = live_psi[block], own_ref[block]
        scaled = quotient * jnp.where(mask, values.astype(jnp.float32), 0.0)
        staged[step % depth] = (sums.astype(jnp.float32) - scaled).astype(jnp.bfloat16)
        write(step).start()
    for step in range(2 * blocks - min(depth, 2 * blocks), 2 * blocks):
        write(step).wait()


def residual_call(scalars, folds, psi, live_psi, own, other):
    sectors, slots, states, width = psi.shape[:4]
    blocks = own.shape[0]
    depth = 4
    in_hbm = [pl.BlockSpec(memory_space=pltpu.HBM)]
    return pl.pallas_call(
        functools.partial(residual_kernel, sectors // 2, slots),
        in_specs=in_smem(len(scalars)) + resident(4) + in_hbm,
        out_specs=in_hbm + in_smem(1),
        out_shape=[
            jax.ShapeDtypeStruct(psi.shape, jnp.bfloat16),
            jax.ShapeDtypeStruct((1,), jnp.float32),
        ],
        scratch_shapes=[
            pltpu.VMEM((blocks, states, width, width), jnp.bfloat16),
            pltpu.VMEM((depth, states, width, width), jnp.bfloat16),
            pltpu.SemaphoreType.DMA((blocks,)),
            pltpu.SemaphoreType.DMA((depth,)),
        ],
        compiler_params=pltpu.CompilerParams(vmem_limit_bytes=41 * MIB),
        cost_estimate=pl.CostEstimate(
            flops=3 * psi.size, bytes_accessed=6 * psi.size, transcendentals=0
        ),
        name="residual",
    )(*scalars, folds, live_psi, own, other, psi)


def on_device(
    devices, rings, psi, left_env, right_env, local_ops, term_op, sector_rows, block_partner,
    block_count,
):
    sectors, slots, states, width = psi.shape[:4]
    terms = left_env.shape[1]
    half = sectors // 2
    me = lax.axis_index("term")
    ring = lax.axis_index("sec")
    core = me % 2
    meta = jnp.stack([ring * sectors, core, me, ring]).astype(jnp.int32)

    near_rows = lax.dynamic_slice_in_dim(sector_rows, ring * sectors, sectors)
    weight = block_count * (near_rows + width // 2)
    order = jnp.arange(sectors, dtype=jnp.int32)
    ahead = (weight[None, :] > weight[:, None]) | (
        (weight[None, :] == weight[:, None]) & (order[None, :] < order[:, None])
    )
    rank = jnp.sum(ahead.astype(jnp.int32), axis=1)
    index = ((rank ^ (rank >> 1)) & 1) * half + (rank >> 1)
    places = jnp.sum(jnp.where(index[None, :] == order[:, None], order[None, :], 0), axis=1)
    scalars = (meta, places, sector_rows, block_partner, block_count)

    def swap(value, bits, axis="term", size=devices):
        return lax.ppermute(value, axis, [(i, i ^ bits) for i in range(size)])

    def to_far_chips(near, received):
        both = jnp.stack([near, received])
        return both, [swap(both, bits) for bits in range(2, devices, 2)]

    chunks = [(0, terms // 2)] + [(at, 1) for at in range(terms // 2, terms)]
    ordered = jnp.roll(places, -core * half)
    mine, theirs, *shares = pack_call(
        chunks, ordered, term_op, local_ops, left_env, right_env
    )
    near_left = swap(theirs, 1)
    both_lefts, far_lefts = to_far_chips(mine, near_left)

    shards, rights = [], []

    def gather(token):
        own = shares[len(shards)]
        if token is not None:
            own, _ = lax.optimization_barrier((own, token))
        moved = [own]
        for distance in range(1, rings):
            pairs = [(i, (i + distance) % rings) for i in range(rings)]
            moved.append(lax.ppermute(own, "sec", pairs))
        shards.append(moved)

    def choose(token):
        afters = [token] + (rights[-1][2:] if rights else [])
        mine, other = choose_call(scalars, half, slots, shards[len(rights)], afters)
        received = swap(other, 1)
        both, far_rights = to_far_chips(mine, received)
        rights.append([mine, received] + far_rights)
        return both

    products = {}
    shape = (half * slots, slots, states, width)
    far = tuple(range(2, devices))

    def go_left(sources, which, token, first=False, waits=()):
        items = [(source, *chunks[at]) for at in which for source in sources]
        near = [source for source in sources if source < 2]
        payloads = [(mine, near_left)[source] for source in near]
        if len(near) < len(sources):
            payloads += far_lefts
        renamed = [(sources.index(source), start, count) for source, start, count in items]
        outs = left_call(
            first, scalars, terms, renamed, shape, psi if first else live_psi, payloads,
            [token, *waits],
        )
        for at, out in zip([(at, source) for at in which for source in sources], outs):
            products[at] = out
        return outs[len(items) :]

    every = range(len(chunks))
    gather(None)
    token, live_psi, squares = go_left((0,), every, both_lefts, True)
    token, = go_left((1,), every, token, waits=far_lefts)
    gather(token)
    token = choose(token)
    total = None
    for at, chunk in enumerate(chunks):
        last = at == len(chunks) - 1
        if at == len(chunks) - 2:
            token, = go_left(far, [len(chunks) - 1], token)
        if len(rights) < len(chunks):
            token = choose(token)
        if len(shards) < len(chunks):
            gather(token)
        ahead = tuple(source for source in range(devices) if (at, source) in products)
        late = tuple(source for source in range(devices) if source not in ahead)
        total, token = chunk_call(
            at == 0, last, terms, chunk, ahead, late, scalars, slots, live_psi,
            [products.pop((at, source)) for source in ahead], far_lefts if late else [],
            rights[at], total, token,
        )

    other = swap(total, 1)
    folds = jnp.concatenate([token, squares], axis=0)
    bits = 1
    while bits < rings:
        folds = folds + swap(folds, bits, "sec", rings)
        bits *= 2
    folds = folds + swap(folds, 1)
    residual, rayleigh = residual_call(scalars, folds, psi, live_psi, total, other)
    return residual, rayleigh


def solution(mesh):
    placed = (
        P(("groups", "sec"), None, None, None, None),
        P(("groups", "sec"), "term", None, None),
        P(("groups", "sec"), "term", None, None),
        P(),
        P("term"),
        P("groups"),
        P(("groups", "sec"), None),
        P(("groups", "sec")),
    )
    return jax.shard_map(
        functools.partial(on_device, mesh.shape["term"], mesh.shape["sec"]),
        mesh=mesh,
        in_specs=placed,
        out_specs=(P(("groups", "sec"), None, None, None, None), P("groups")),
        check_vma=False,
    )
```

```python
import functools

import jax
import jax.numpy as jnp
from jax import lax
from jax.experimental import pallas as pl
from jax.experimental.pallas import tpu as pltpu
from jax.sharding import PartitionSpec as P

TILE = 16
WIDE = 2
MIB = 1024 * 1024
SPARE = 3 * MIB // 2
HASTE = 256


def block_facts(scalars, index, slot):
    meta, places, sector_rows, partners, counts = scalars
    sector = places[index]
    live = slot < counts[sector]
    own_rows = sector_rows[meta[0] + sector]
    partner_rows = sector_rows[partners[sector, slot]]
    return sector, live, own_rows, partner_rows


def live_entries(own_rows, partner_rows, width):
    left = lax.broadcasted_iota(jnp.int32, (1, width, width), 1) < own_rows
    right = lax.broadcasted_iota(jnp.int32, (1, width, width), 2) < partner_rows
    return left & right


def folded(values):
    states, width = values.shape[0], values.shape[-1]
    return jnp.sum(values.reshape(states * width // 8, 8, width), axis=0)


def by_live_rows(own_rows, groups, work):
    always = groups // 2
    work(0, always)
    for group in range(always, groups, WIDE):
        pl.when(own_rows > group * TILE)(functools.partial(work, group, group + WIDE))


def spread_operators(ops_ref, chosen, spread_ops, at, states):
    width, wide = ops_ref.shape[-1], states * TILE
    row_state = lax.broadcasted_iota(jnp.int32, (wide, states), 0) // TILE
    column = lax.broadcasted_iota(jnp.int32, (wide, states), 1)
    pick_rows = (row_state == column).astype(jnp.bfloat16)
    row = lax.broadcasted_iota(jnp.int32, (width, wide), 0)
    column_state = lax.broadcasted_iota(jnp.int32, (width, wide), 1) // TILE
    pick_columns = (row == column_state).astype(jnp.bfloat16)
    inner_row = lax.rem(lax.broadcasted_iota(jnp.int32, (wide, wide), 0), TILE)
    inner_column = lax.rem(lax.broadcasted_iota(jnp.int32, (wide, wide), 1), TILE)
    for term in chosen:
        operator = ops_ref[term * states : (term + 1) * states, :]
        rows = jnp.dot(pick_rows, operator, preferred_element_type=jnp.float32)
        full = jnp.dot(
            rows.astype(jnp.bfloat16), pick_columns, preferred_element_type=jnp.float32
        )
        spread_ops[at] = jnp.where(inner_row == inner_column, full, 0.0).astype(jnp.bfloat16)
        at += 1


def multiply_left(lefts, live_psi, after_left):
    terms, groups = after_left.shape[:2]
    states, width = live_psi.shape[0], live_psi.shape[-1]
    for pair in range(states // WIDE):
        columns = jnp.concatenate([live_psi[pair * WIDE + at] for at in range(WIDE)], axis=1)
        done = jnp.dot(lefts, columns, preferred_element_type=jnp.float32).astype(jnp.bfloat16)
        for term in range(terms):
            for at in range(WIDE):
                state = pair * WIDE + at
                after_left[term, :, state * TILE : (state + 1) * TILE, :] = done[
                    term * width : (term + 1) * width, at * width : (at + 1) * width
                ].reshape(groups, TILE, width)


def apply_operators(low, high, spread_ops, after_left, targets):
    width = after_left.shape[-1]
    for group in range(low, high, WIDE):
        for term, (target, lead) in enumerate(targets):
            columns = jnp.concatenate(
                [after_left[term, group + at] for at in range(WIDE)], axis=1
            )
            done = jnp.dot(
                spread_ops[term], columns, preferred_element_type=jnp.float32
            ).astype(jnp.bfloat16)
            for at in range(WIDE):
                target[(*lead, group + at)] = done[:, at * width : (at + 1) * width]


def each_live_block(half, slots, scalars, work):
    meta = scalars[0]

    def visit(block, carry):
        place, slot = block // slots, lax.rem(block, slots)
        sector, live, own_rows, partner_rows = block_facts(
            scalars, meta[1] * half + place, slot
        )
        pl.when(live)(functools.partial(work, block, place, sector, own_rows, partner_rows))
        return carry

    lax.fori_loop(0, half * slots, visit, 0)


def pack_kernel(chunks, half, terms, places, term_op, ops_ref, left_ref, right_ref, *rest):
    payloads, rest = rest[:2], rest[2:]
    shares, sems = rest[: len(chunks)], rest[len(chunks)]
    states, width = ops_ref.shape[1], left_ref.shape[-1]
    copied = half * terms * width
    for part, payload in enumerate(payloads):
        for place in range(half):
            pltpu.make_async_copy(
                left_ref.at[places[part * half + place]],
                payload.at[pl.ds(place * terms * width, terms * width)],
                sems.at[part],
            ).start()
    moves = []
    for at, (start, length) in enumerate(chunks):
        move = pltpu.make_async_copy(
            right_ref.at[:, pl.ds(start, length)], shares[at], sems.at[2 + at]
        )
        move.start()
        moves.append(move)
    for payload in payloads:
        for term in range(terms):
            rows = slice(copied + term * states, copied + (term + 1) * states)
            payload[rows, :] = jnp.zeros((states, width), jnp.bfloat16)
            payload[rows, :states] = ops_ref[term_op[term]]
    for part, payload in enumerate(payloads):
        whole = payload.at[pl.ds(0, copied)]
        pltpu.make_async_copy(whole, whole, sems.at[part]).wait()
    for move in moves:
        move.wait()


def pack_call(chunks, places, term_op, local_ops, left_env, right_env):
    sectors, terms, width = left_env.shape[:3]
    half, states = sectors // 2, local_ops.shape[1]
    payload = jax.ShapeDtypeStruct((terms * (half * width + states), width), jnp.bfloat16)
    shares = [
        jax.ShapeDtypeStruct((sectors, length, width, width), jnp.bfloat16)
        for start, length in chunks
    ]
    return pl.pallas_call(
        functools.partial(pack_kernel, chunks, half, terms),
        in_specs=in_smem(2) + resident(1) + [pl.BlockSpec(memory_space=pltpu.HBM)] * 2,
        out_specs=resident(2 + len(chunks)),
        out_shape=[payload, payload] + shares,
        scratch_shapes=[pltpu.SemaphoreType.DMA((2 + len(chunks),))],
        compiler_params=pltpu.CompilerParams(vmem_limit_bytes=58 * MIB),
        cost_estimate=pl.CostEstimate(
            flops=0, bytes_accessed=4 * left_env.size, transcendentals=0
        ),
        name="pack",
    )(places, term_op, local_ops, left_env.reshape(sectors, terms * width, width), right_env)


def source_views(payloads):
    views = []
    for payload in payloads:
        views += [payload] if len(payload.shape) == 2 else [payload.at[0], payload.at[1]]
    return views


def term_rows(place, held, start, terms, width):
    return pl.ds(pl.multiple_of((place * held + start) * width, width), terms * width)


def left_kernel(first, held, items, count, afters, half, slots, meta, places, sector_rows,
                partners, counts, *rest):
    scalars = (meta, places, sector_rows, partners, counts)
    psi_ref, rest = rest[afters], rest[afters + 1 :]
    payloads, rest = rest[:count], rest[count:]
    outs, rest = rest[: len(items)], rest[len(items) :]
    token_ref, rest = rest[0], rest[1:]
    if first:
        live_psi, square_ref, spread_ops, after_left, sems = rest
    else:
        live_psi = psi_ref
        spread_ops, after_left = rest
    states, width = live_psi.shape[1], live_psi.shape[-1]
    views = source_views(payloads)

    def fetch(block, sector):
        return pltpu.make_async_copy(
            psi_ref.at[sector, lax.rem(block, slots)], live_psi.at[block], sems.at[block]
        )

    if first:
        each_live_block(
            half, slots, scalars, lambda block, place, sector, *rows: fetch(block, sector).start()
        )
        square_ref[...] = jnp.zeros_like(square_ref)
    at = 0
    for source, start, terms in items:
        operators = views[source][half * held * width :, :]
        spread_operators(operators, range(start, start + terms), spread_ops, at, states)
        at += terms
    token_ref[...] = jnp.zeros_like(token_ref)

    def work(block, place, sector, own_rows, partner_rows):
        if first:
            fetch(block, sector).wait()
            mask = live_entries(own_rows, partner_rows, width)
            kept = jnp.where(mask, live_psi[block], jnp.zeros((), jnp.bfloat16))
            live_psi[block] = kept
            wide_psi = kept.astype(jnp.float32)
            square_ref[...] += folded(wide_psi * wide_psi)
        lefts = [
            views[source][term_rows(place, held, start, terms, width), :]
            for source, start, terms in items
        ]
        multiply_left(jnp.concatenate(lefts, axis=0), live_psi.at[block], after_left)
        targets = [
            (outs[at], (block, term))
            for at, (source, start, terms) in enumerate(items)
            for term in range(terms)
        ]
        by_live_rows(
            own_rows,
            width // TILE,
            lambda low, high: apply_operators(low, high, spread_ops, after_left, targets),
        )

    each_live_block(half, slots, scalars, work)


def resident(count):
    return [pl.BlockSpec(memory_space=pltpu.VMEM)] * count


def in_smem(count):
    return [pl.BlockSpec(memory_space=pltpu.SMEM)] * count


def left_call(first, scalars, held, items, shape, psi, payloads, afters):
    blocks, slots, states, width = shape
    groups, wide = width // TILE, states * TILE
    every = sum(terms for source, start, terms in items)
    fold_shape = jax.ShapeDtypeStruct((8, width), jnp.float32)
    out_shape = [
        jax.ShapeDtypeStruct((blocks, terms, groups, wide, width), jnp.bfloat16)
        for source, start, terms in items
    ] + [fold_shape]
    scratch = [
        pltpu.VMEM((every, wide, wide), jnp.bfloat16),
        pltpu.VMEM((every, groups, wide, width), jnp.bfloat16),
    ]
    if first:
        live_psi = jax.ShapeDtypeStruct((blocks, states, width, width), jnp.bfloat16)
        out_shape += [live_psi, fold_shape]
        scratch.append(pltpu.SemaphoreType.DMA((blocks,)))
    psi_spec = [pl.BlockSpec(memory_space=pltpu.HBM)] if first else resident(1)
    return pl.pallas_call(
        functools.partial(
            left_kernel, first, held, items, len(payloads), len(afters), blocks // slots, slots
        ),
        in_specs=in_smem(len(scalars))
        + [pl.BlockSpec(memory_space=pl.ANY)] * len(afters)
        + psi_spec
        + resident(len(payloads)),
        out_specs=resident(len(out_shape)),
        out_shape=out_shape,
        scratch_shapes=scratch,
        compiler_params=pltpu.CompilerParams(
            vmem_limit_bytes=max(
                28 * MIB if first else 0,
                SPARE + 2 * every * (wide * wide + groups * wide * width),
            )
        ),
        cost_estimate=pl.CostEstimate(
            flops=psi.size * every * (width + wide) // HASTE,
            bytes_accessed=psi.size // HASTE,
            transcendentals=0,
        ),
        name="left",
    )(*scalars, *afters, psi, *payloads)


def choose_kernel(devices, afters, sectors, half, slots, meta, places, partners, *rest):
    rest = rest[afters:]
    shards, (mine_ref, other_ref) = rest[:devices], rest[devices:]
    for part, out_ref in enumerate((mine_ref, other_ref)):
        for block in range(half * slots):
            sector = places[(meta[1] ^ part) * half + block // slots]
            partner = partners[sector, block % slots]
            away = lax.rem(meta[3] + devices - partner // sectors, devices)
            place = lax.rem(partner, sectors)
            for distance in range(devices):
                @pl.when(away == distance)
                def _(distance=distance, place=place, block=block, out_ref=out_ref):
                    out_ref[block] = shards[distance][place]


def choose_call(scalars, half, slots, shards, afters):
    meta, places, _, partners, _ = scalars
    sectors, terms, width = shards[0].shape[:3]
    chosen = jax.ShapeDtypeStruct((half * slots, terms, width, width), jnp.bfloat16)
    return pl.pallas_call(
        functools.partial(choose_kernel, len(shards), len(afters), sectors, half, slots),
        in_specs=in_smem(3)
        + [pl.BlockSpec(memory_space=pl.ANY)] * len(afters)
        + resident(len(shards)),
        out_specs=resident(2),
        out_shape=[chosen, chosen],
        compiler_params=pltpu.CompilerParams(vmem_limit_bytes=SPARE),
        cost_estimate=pl.CostEstimate(
            flops=0, bytes_accessed=8 * half * slots * terms * width * width, transcendentals=0
        ),
        name="choose",
    )(meta, places, partners, *afters, *shards)


def chunk_kernel(first, last, held, chunk, ahead, late, count, half, slots,
                 meta, places, sector_rows, partners, counts, after_ref, psi_ref, *rest):
    start, terms = chunk
    early_refs, rest = rest[: len(ahead)], rest[len(ahead) :]
    payloads, rest = rest[:count], rest[count:]
    near_rights, rest = rest[:2], rest[2:]
    devices = len(ahead) + len(late)
    far_rights, rest = rest[: devices // 2 - 1], rest[devices // 2 - 1 :]
    if not first:
        sum_in, rest = rest[0], rest[1:]
    sum_out, fold_ref, *rest = rest
    if late:
        spread_ops, after_left, after_ops, *rest = rest
    states, width = psi_ref.shape[1], psi_ref.shape[-1]
    groups = width // TILE
    views = dict(zip(late, source_views(payloads)))
    rights = list(near_rights) + [right.at[side] for right in far_rights for side in (0, 1)]
    for at, source in enumerate(late):
        operators = views[source][half * held * width :, :]
        spread_operators(operators, range(start, start + terms), spread_ops, at * terms, states)
    fold_ref[...] = jnp.zeros_like(fold_ref)
    if last:
        sum_out[...] = jnp.zeros_like(sum_out)

    def work(block, place, sector, own_rows, partner_rows):
        total = rest[0] if last else sum_out.at[block]
        if late:
            lefts = [
                views[source][term_rows(place, held, start, terms, width), :] for source in late
            ]
            multiply_left(jnp.concatenate(lefts, axis=0), psi_ref.at[block], after_left)
        columns = [
            jnp.concatenate(
                [rights[pair + at][block, term] for at in range(2) for term in range(terms)],
                axis=0,
            )
            for pair in range(0, devices, 2)
        ]

        def operated(device, term, group):
            if device in ahead:
                return early_refs[ahead.index(device)][block, term, group]
            return after_ops[late.index(device) * terms + term, group]

        def multiply(low, high):
            if late:
                targets = [(after_ops, (term,)) for term in range(len(late) * terms)]
                apply_operators(low, high, spread_ops, after_left, targets)
            for group in range(low, high, WIDE):
                parts = []
                for pair in range(0, devices, 2):
                    rows = jnp.concatenate(
                        [
                            jnp.concatenate(
                                [
                                    operated(pair + at, term, group + side)
                                    for at in range(2)
                                    for term in range(terms)
                                ],
                                axis=1,
                            )
                            for side in range(WIDE)
                        ],
                        axis=0,
                    )
                    parts.append(
                        jnp.dot(rows, columns[pair // 2], preferred_element_type=jnp.float32)
                    )
                while len(parts) > 1:
                    parts = [parts[at] + parts[at + 1] for at in range(0, len(parts), 2)]
                done = parts[0].reshape(WIDE, states, TILE, width)
                for side in range(WIDE):
                    tile = slice((group + side) * TILE, (group + side + 1) * TILE)
                    if first:
                        total[:, tile, :] = done[side]
                    else:
                        total[:, tile, :] = sum_in[block, :, tile, :] + done[side]

        by_live_rows(own_rows, groups, multiply)
        if last:
            mask = live_entries(own_rows, partner_rows, width)
            kept = jnp.where(mask, total[...], 0.0)
            fold_ref[...] += folded(kept * psi_ref[block].astype(jnp.float32))
            sum_out[block] = kept.astype(jnp.bfloat16)

    each_live_block(half, slots, (meta, places, sector_rows, partners, counts), work)


def chunk_call(first, last, held, chunk, ahead, late, scalars, slots, psi, early, payloads,
               rights, total, after):
    blocks, states, width = psi.shape[:3]
    groups, wide = width // TILE, states * TILE
    start, terms = chunk
    operands = [after, psi, *early, *payloads, *rights]
    aliases = {}
    if not first:
        operands.append(total)
        if not last:
            aliases = {len(scalars) + len(operands) - 1: 0}
    sum_dtype = jnp.bfloat16 if last else jnp.float32
    every = len(late) * terms
    scratch = []
    if late:
        scratch += [
            pltpu.VMEM((every, wide, wide), jnp.bfloat16),
            pltpu.VMEM((every, groups, wide, width), jnp.bfloat16),
            pltpu.VMEM((every, groups, wide, width), jnp.bfloat16),
        ]
    if last:
        scratch.append(pltpu.VMEM((states, width, width), jnp.float32))
    work = psi.size * terms * ((len(ahead) + len(late)) * width + len(late) * (width + wide))
    return pl.pallas_call(
        functools.partial(
            chunk_kernel, first, last, held, chunk, ahead, late, len(payloads),
            blocks // slots, slots,
        ),
        in_specs=in_smem(len(scalars))
        + [pl.BlockSpec(memory_space=pl.ANY)]
        + resident(len(operands) - 1),
        out_specs=resident(2),
        out_shape=[
            jax.ShapeDtypeStruct(psi.shape, sum_dtype),
            jax.ShapeDtypeStruct((8, width), jnp.float32),
        ],
        scratch_shapes=scratch,
        input_output_aliases=aliases,
        compiler_params=pltpu.CompilerParams(
            vmem_limit_bytes=(len(ahead) + len(late)) * SPARE // 4
            + 2 * every * wide * (wide + 2 * groups * width)
            + 4 * int(last) * states * width * width
        ),
        cost_estimate=pl.CostEstimate(
            flops=work // HASTE, bytes_accessed=psi.size // HASTE, transcendentals=0
        ),
        name="chunk",
    )(*scalars, *operands)


def residual_kernel(half, slots, meta, places, sector_rows, partners, counts,
                    folds_ref, live_psi, own_ref, other_ref, psi_ref, out_ref, quotient_ref,
                    other_psi, staged, read_sems, write_sems):
    scalars = (meta, places, sector_rows, partners, counts)
    blocks, width = own_ref.shape[0], own_ref.shape[-1]
    depth = staged.shape[0]

    def where(block, side):
        index = (meta[1] ^ side) * half + block // slots
        return places[index], block % slots, index

    def read(block):
        sector, slot, _ = where(block, 1)
        return pltpu.make_async_copy(
            psi_ref.at[sector, slot], other_psi.at[block], read_sems.at[block]
        )

    def write(step):
        sector, slot, _ = where(step % blocks, step // blocks)
        return pltpu.make_async_copy(
            staged.at[step % depth], out_ref.at[sector, slot], write_sems.at[step % depth]
        )

    for block in range(blocks):
        read(block).start()
    quotient = jnp.sum(folds_ref[0:8, :]) / jnp.sum(folds_ref[8:16, :])
    quotient_ref[0] = quotient
    for step in range(2 * blocks):
        block, side = step % blocks, step // blocks
        if step >= depth:
            write(step - depth).wait()
        sector, slot, index = where(block, side)
        _, live, own_rows, partner_rows = block_facts(scalars, index, slot)
        mask = live_entries(jnp.where(live, own_rows, 0), partner_rows, width)
        if side:
            read(block).wait()
            values, sums = other_psi[block], other_ref[block]
        else:
            values, sums = live_psi[block], own_ref[block]
        scaled = quotient * jnp.where(mask, values.astype(jnp.float32), 0.0)
        staged[step % depth] = (sums.astype(jnp.float32) - scaled).astype(jnp.bfloat16)
        write(step).start()
    for step in range(2 * blocks - min(depth, 2 * blocks), 2 * blocks):
        write(step).wait()


def residual_call(scalars, folds, psi, live_psi, own, other):
    sectors, slots, states, width = psi.shape[:4]
    blocks = own.shape[0]
    depth = 4
    in_hbm = [pl.BlockSpec(memory_space=pltpu.HBM)]
    return pl.pallas_call(
        functools.partial(residual_kernel, sectors // 2, slots),
        in_specs=in_smem(len(scalars)) + resident(4) + in_hbm,
        out_specs=in_hbm + in_smem(1),
        out_shape=[
            jax.ShapeDtypeStruct(psi.shape, jnp.bfloat16),
            jax.ShapeDtypeStruct((1,), jnp.float32),
        ],
        scratch_shapes=[
            pltpu.VMEM((blocks, states, width, width), jnp.bfloat16),
            pltpu.VMEM((depth, states, width, width), jnp.bfloat16),
            pltpu.SemaphoreType.DMA((blocks,)),
            pltpu.SemaphoreType.DMA((depth,)),
        ],
        compiler_params=pltpu.CompilerParams(vmem_limit_bytes=41 * MIB),
        cost_estimate=pl.CostEstimate(
            flops=3 * psi.size, bytes_accessed=6 * psi.size, transcendentals=0
        ),
        name="residual",
    )(*scalars, folds, live_psi, own, other, psi)


def on_device(
    devices, rings, psi, left_env, right_env, local_ops, term_op, sector_rows, block_partner,
    block_count,
):
    sectors, slots, states, width = psi.shape[:4]
    terms = left_env.shape[1]
    half = sectors // 2
    me = lax.axis_index("term")
    ring = lax.axis_index("sec")
    core = me % 2
    meta = jnp.stack([ring * sectors, core, me, ring]).astype(jnp.int32)

    near_rows = lax.dynamic_slice_in_dim(sector_rows, ring * sectors, sectors)
    weight = block_count * (near_rows + width // 2)
    order = jnp.arange(sectors, dtype=jnp.int32)
    ahead = (weight[None, :] > weight[:, None]) | (
        (weight[None, :] == weight[:, None]) & (order[None, :] < order[:, None])
    )
    rank = jnp.sum(ahead.astype(jnp.int32), axis=1)
    index = ((rank ^ (rank >> 1)) & 1) * half + (rank >> 1)
    places = jnp.sum(jnp.where(index[None, :] == order[:, None], order[None, :], 0), axis=1)
    scalars = (meta, places, sector_rows, block_partner, block_count)

    def swap(value, bits, axis="term", size=devices):
        return lax.ppermute(value, axis, [(i, i ^ bits) for i in range(size)])

    def to_far_chips(near, received):
        both = jnp.stack([near, received])
        return both, [swap(both, bits) for bits in range(2, devices, 2)]

    chunks = [(at, 1) for at in range(terms)]
    ordered = jnp.roll(places, -core * half)
    mine, theirs, *shares = pack_call(
        chunks, ordered, term_op, local_ops, left_env, right_env
    )
    near_left = swap(theirs, 1)
    both_lefts, far_lefts = to_far_chips(mine, near_left)

    shards, rights = [], []

    def gather(token):
        own = shares[len(shards)]
        if token is not None:
            own, _ = lax.optimization_barrier((own, token))
        moved = [own]
        for distance in range(1, rings):
            pairs = [(i, (i + distance) % rings) for i in range(rings)]
            moved.append(lax.ppermute(own, "sec", pairs))
        shards.append(moved)

    def choose(token):
        afters = [token] + (rights[-1][2:] if rights else [])
        mine, other = choose_call(scalars, half, slots, shards[len(rights)], afters)
        received = swap(other, 1)
        both, far_rights = to_far_chips(mine, received)
        rights.append([mine, received] + far_rights)
        return both

    products = {}
    shape = (half * slots, slots, states, width)
    far = tuple(range(2, devices))

    def go_left(sources, which, token, first=False, waits=()):
        items = [(source, *chunks[at]) for at in which for source in sources]
        near = [source for source in sources if source < 2]
        payloads = [(mine, near_left)[source] for source in near]
        if len(near) < len(sources):
            payloads += far_lefts
        renamed = [(sources.index(source), start, count) for source, start, count in items]
        outs = left_call(
            first, scalars, terms, renamed, shape, psi if first else live_psi, payloads,
            [token, *waits],
        )
        for at, out in zip([(at, source) for at in which for source in sources], outs):
            products[at] = out
        return outs[len(items) :]

    every = range(len(chunks))
    gather(None)
    token, live_psi, squares = go_left((0,), every, both_lefts, True)
    gather(token)
    token = choose(token)
    token, = go_left((1,), every[1:], token, waits=far_lefts)
    total = None
    for at, chunk in enumerate(chunks):
        last = at == len(chunks) - 1
        if len(rights) < len(chunks):
            token = choose(token)
        if len(shards) < len(chunks):
            gather(token)
        ahead = tuple(source for source in range(devices) if (at, source) in products)
        late = tuple(source for source in range(devices) if source not in ahead)
        payloads = ([near_left] if 1 in late else []) + (far_lefts if late else [])
        total, token = chunk_call(
            at == 0, last, terms, chunk, ahead, late, scalars, slots, live_psi,
            [products.pop((at, source)) for source in ahead], payloads,
            rights[at], total, token,
        )
        if at == len(chunks) - 3:
            token, = go_left(far, [len(chunks) - 1], token)

    other = swap(total, 1)
    folds = jnp.concatenate([token, squares], axis=0)
    bits = 1
    while bits < rings:
        folds = folds + swap(folds, bits, "sec", rings)
        bits *= 2
    folds = folds + swap(folds, 1)
    residual, rayleigh = residual_call(scalars, folds, psi, live_psi, total, other)
    return residual, rayleigh


def solution(mesh):
    placed = (
        P(("groups", "sec"), None, None, None, None),
        P(("groups", "sec"), "term", None, None),
        P(("groups", "sec"), "term", None, None),
        P(),
        P("term"),
        P("groups"),
        P(("groups", "sec"), None),
        P(("groups", "sec")),
    )
    return jax.shard_map(
        functools.partial(on_device, mesh.shape["term"], mesh.shape["sec"]),
        mesh=mesh,
        in_specs=placed,
        out_specs=(P(("groups", "sec"), None, None, None, None), P("groups")),
        check_vma=False,
    )
```

```python
import functools

import jax
import jax.numpy as jnp
from jax import lax
from jax.experimental import pallas as pl
from jax.experimental.pallas import tpu as pltpu
from jax.sharding import PartitionSpec as P

TILE = 16
WIDE = 2
MIB = 1024 * 1024
SPARE = 3 * MIB // 2
HASTE = 256


def block_facts(scalars, index, slot):
    meta, places, sector_rows, partners, counts = scalars
    sector = places[index]
    live = slot < counts[sector]
    own_rows = sector_rows[meta[0] + sector]
    partner_rows = sector_rows[partners[sector, slot]]
    return sector, live, own_rows, partner_rows


def live_entries(own_rows, partner_rows, width):
    left = lax.broadcasted_iota(jnp.int32, (1, width, width), 1) < own_rows
    right = lax.broadcasted_iota(jnp.int32, (1, width, width), 2) < partner_rows
    return left & right


def folded(values):
    states, width = values.shape[0], values.shape[-1]
    return jnp.sum(values.reshape(states * width // 8, 8, width), axis=0)


def by_live_rows(own_rows, groups, work):
    few = 3 * groups // 4
    pl.when(own_rows <= few * TILE)(functools.partial(work, few))
    pl.when(own_rows > few * TILE)(functools.partial(work, groups))


def spread_operators(ops_ref, chosen, spread_ops, at, states):
    width, wide = ops_ref.shape[-1], states * TILE
    row_state = lax.broadcasted_iota(jnp.int32, (wide, states), 0) // TILE
    column = lax.broadcasted_iota(jnp.int32, (wide, states), 1)
    pick_rows = (row_state == column).astype(jnp.bfloat16)
    row = lax.broadcasted_iota(jnp.int32, (width, wide), 0)
    column_state = lax.broadcasted_iota(jnp.int32, (width, wide), 1) // TILE
    pick_columns = (row == column_state).astype(jnp.bfloat16)
    inner_row = lax.rem(lax.broadcasted_iota(jnp.int32, (wide, wide), 0), TILE)
    inner_column = lax.rem(lax.broadcasted_iota(jnp.int32, (wide, wide), 1), TILE)
    for term in chosen:
        operator = ops_ref[term * states : (term + 1) * states, :]
        rows = jnp.dot(pick_rows, operator, preferred_element_type=jnp.float32)
        full = jnp.dot(
            rows.astype(jnp.bfloat16), pick_columns, preferred_element_type=jnp.float32
        )
        spread_ops[at] = jnp.where(inner_row == inner_column, full, 0.0).astype(jnp.bfloat16)
        at += 1


def multiply_left(groups, lefts, live_psi, after_left):
    rows = groups * TILE
    states, width = live_psi.shape[0], live_psi.shape[-1]
    stacked = jnp.concatenate(lefts, axis=0)
    for pair in range(states // WIDE):
        columns = jnp.concatenate([live_psi[pair * WIDE + at] for at in range(WIDE)], axis=1)
        done = jnp.dot(stacked, columns, preferred_element_type=jnp.float32).astype(jnp.bfloat16)
        for term in range(len(lefts)):
            for at in range(WIDE):
                state = pair * WIDE + at
                after_left[term, :groups, state * TILE : (state + 1) * TILE, :] = done[
                    term * rows : (term + 1) * rows, at * width : (at + 1) * width
                ].reshape(groups, TILE, width)


def apply_operators(low, high, spread_ops, after_left, targets):
    width = after_left.shape[-1]
    for group in range(low, high, WIDE):
        for term, (target, lead) in enumerate(targets):
            columns = jnp.concatenate(
                [after_left[term, group + at] for at in range(WIDE)], axis=1
            )
            done = jnp.dot(
                spread_ops[term], columns, preferred_element_type=jnp.float32
            ).astype(jnp.bfloat16)
            for at in range(WIDE):
                target[(*lead, group + at)] = done[:, at * width : (at + 1) * width]


def each_live_block(half, slots, scalars, work):
    meta = scalars[0]

    def visit(block, carry):
        place, slot = block // slots, lax.rem(block, slots)
        sector, live, own_rows, partner_rows = block_facts(
            scalars, meta[1] * half + place, slot
        )
        pl.when(live)(functools.partial(work, block, place, sector, own_rows, partner_rows))
        return carry

    lax.fori_loop(0, half * slots, visit, 0)


def pack_kernel(chunks, half, terms, places, term_op, ops_ref, left_ref, right_ref, *rest):
    payloads, rest = rest[:2], rest[2:]
    shares, sems = rest[: len(chunks)], rest[len(chunks)]
    states, width = ops_ref.shape[1], left_ref.shape[-1]
    copied = half * terms * width
    for part, payload in enumerate(payloads):
        for place in range(half):
            pltpu.make_async_copy(
                left_ref.at[places[part * half + place]],
                payload.at[pl.ds(place * terms * width, terms * width)],
                sems.at[part],
            ).start()
    moves = []
    for at, (start, length) in enumerate(chunks):
        move = pltpu.make_async_copy(
            right_ref.at[:, pl.ds(start, length)], shares[at], sems.at[2 + at]
        )
        move.start()
        moves.append(move)
    for payload in payloads:
        for term in range(terms):
            rows = slice(copied + term * states, copied + (term + 1) * states)
            payload[rows, :] = jnp.zeros((states, width), jnp.bfloat16)
            payload[rows, :states] = ops_ref[term_op[term]]
    for part, payload in enumerate(payloads):
        whole = payload.at[pl.ds(0, copied)]
        pltpu.make_async_copy(whole, whole, sems.at[part]).wait()
    for move in moves:
        move.wait()


def pack_call(chunks, places, term_op, local_ops, left_env, right_env):
    sectors, terms, width = left_env.shape[:3]
    half, states = sectors // 2, local_ops.shape[1]
    payload = jax.ShapeDtypeStruct((terms * (half * width + states), width), jnp.bfloat16)
    shares = [
        jax.ShapeDtypeStruct((sectors, length, width, width), jnp.bfloat16)
        for start, length in chunks
    ]
    return pl.pallas_call(
        functools.partial(pack_kernel, chunks, half, terms),
        in_specs=in_smem(2) + resident(1) + [pl.BlockSpec(memory_space=pltpu.HBM)] * 2,
        out_specs=resident(2 + len(chunks)),
        out_shape=[payload, payload] + shares,
        scratch_shapes=[pltpu.SemaphoreType.DMA((2 + len(chunks),))],
        compiler_params=pltpu.CompilerParams(vmem_limit_bytes=58 * MIB),
        cost_estimate=pl.CostEstimate(
            flops=0, bytes_accessed=4 * left_env.size, transcendentals=0
        ),
        name="pack",
    )(places, term_op, local_ops, left_env.reshape(sectors, terms * width, width), right_env)


def source_views(payloads):
    views = []
    for payload in payloads:
        views += [payload] if len(payload.shape) == 2 else [payload.at[0], payload.at[1]]
    return views


def term_rows(view, place, held, term, rows):
    width = view.shape[-1]
    return view[pl.ds(pl.multiple_of((place * held + term) * width, width), rows), :]


def left_kernel(first, held, items, count, afters, half, slots, meta, places, sector_rows,
                partners, counts, *rest):
    scalars = (meta, places, sector_rows, partners, counts)
    psi_ref, rest = rest[afters], rest[afters + 1 :]
    payloads, rest = rest[:count], rest[count:]
    outs, rest = rest[: len(items)], rest[len(items) :]
    token_ref, rest = rest[0], rest[1:]
    if first:
        live_psi, square_ref, spread_ops, after_left, sems = rest
    else:
        live_psi = psi_ref
        spread_ops, after_left = rest
    states, width = live_psi.shape[1], live_psi.shape[-1]
    views = source_views(payloads)

    def fetch(block, sector):
        return pltpu.make_async_copy(
            psi_ref.at[sector, lax.rem(block, slots)], live_psi.at[block], sems.at[block]
        )

    if first:
        each_live_block(
            half, slots, scalars, lambda block, place, sector, *rows: fetch(block, sector).start()
        )
        square_ref[...] = jnp.zeros_like(square_ref)
    at = 0
    for source, start, terms in items:
        operators = views[source][half * held * width :, :]
        spread_operators(operators, range(start, start + terms), spread_ops, at, states)
        at += terms
    token_ref[...] = jnp.zeros_like(token_ref)

    def work(block, place, sector, own_rows, partner_rows):
        if first:
            fetch(block, sector).wait()
            mask = live_entries(own_rows, partner_rows, width)
            kept = jnp.where(mask, live_psi[block], jnp.zeros((), jnp.bfloat16))
            live_psi[block] = kept
            wide_psi = kept.astype(jnp.float32)
            square_ref[...] += folded(wide_psi * wide_psi)
        targets = [
            (outs[at], (block, term))
            for at, (source, start, terms) in enumerate(items)
            for term in range(terms)
        ]

        def multiply(groups):
            lefts = [
                term_rows(views[source], place, held, start + term, groups * TILE)
                for source, start, terms in items
                for term in range(terms)
            ]
            multiply_left(groups, lefts, live_psi.at[block], after_left)
            apply_operators(0, groups, spread_ops, after_left, targets)

        by_live_rows(own_rows, width // TILE, multiply)

    each_live_block(half, slots, scalars, work)


def resident(count):
    return [pl.BlockSpec(memory_space=pltpu.VMEM)] * count


def in_smem(count):
    return [pl.BlockSpec(memory_space=pltpu.SMEM)] * count


def left_call(first, scalars, held, items, shape, psi, payloads, afters):
    blocks, slots, states, width = shape
    groups, wide = width // TILE, states * TILE
    every = sum(terms for source, start, terms in items)
    fold_shape = jax.ShapeDtypeStruct((8, width), jnp.float32)
    out_shape = [
        jax.ShapeDtypeStruct((blocks, terms, groups, wide, width), jnp.bfloat16)
        for source, start, terms in items
    ] + [fold_shape]
    scratch = [
        pltpu.VMEM((every, wide, wide), jnp.bfloat16),
        pltpu.VMEM((every, groups, wide, width), jnp.bfloat16),
    ]
    if first:
        live_psi = jax.ShapeDtypeStruct((blocks, states, width, width), jnp.bfloat16)
        out_shape += [live_psi, fold_shape]
        scratch.append(pltpu.SemaphoreType.DMA((blocks,)))
    psi_spec = [pl.BlockSpec(memory_space=pltpu.HBM)] if first else resident(1)
    return pl.pallas_call(
        functools.partial(
            left_kernel, first, held, items, len(payloads), len(afters), blocks // slots, slots
        ),
        in_specs=in_smem(len(scalars))
        + [pl.BlockSpec(memory_space=pl.ANY)] * len(afters)
        + psi_spec
        + resident(len(payloads)),
        out_specs=resident(len(out_shape)),
        out_shape=out_shape,
        scratch_shapes=scratch,
        compiler_params=pltpu.CompilerParams(
            vmem_limit_bytes=max(
                28 * MIB if first else 0,
                SPARE + 2 * every * (wide * wide + groups * wide * width),
            )
        ),
        cost_estimate=pl.CostEstimate(
            flops=psi.size * every * (width + wide) // HASTE,
            bytes_accessed=psi.size // HASTE,
            transcendentals=0,
        ),
        name="left",
    )(*scalars, *afters, psi, *payloads)


def stack_kernel(near_ref, received_ref, both_ref):
    both_ref[0] = near_ref[...]
    both_ref[1] = received_ref[...]


def stack_call(near, received):
    return pl.pallas_call(
        stack_kernel,
        in_specs=resident(2),
        out_specs=resident(1)[0],
        out_shape=jax.ShapeDtypeStruct((2,) + near.shape, near.dtype),
        compiler_params=pltpu.CompilerParams(vmem_limit_bytes=SPARE),
        cost_estimate=pl.CostEstimate(flops=0, bytes_accessed=8 * near.size, transcendentals=0),
        name="stack",
    )(near, received)


def choose_kernel(devices, afters, sectors, half, slots, meta, places, partners, *rest):
    rest = rest[afters:]
    shards, (mine_ref, other_ref) = rest[:devices], rest[devices:]
    for part, out_ref in enumerate((mine_ref, other_ref)):
        for block in range(half * slots):
            sector = places[(meta[1] ^ part) * half + block // slots]
            partner = partners[sector, block % slots]
            away = lax.rem(meta[3] + devices - partner // sectors, devices)
            place = lax.rem(partner, sectors)
            for distance in range(devices):
                @pl.when(away == distance)
                def _(distance=distance, place=place, block=block, out_ref=out_ref):
                    out_ref[block] = shards[distance][place]


def choose_call(scalars, half, slots, shards, afters):
    meta, places, _, partners, _ = scalars
    sectors, terms, width = shards[0].shape[:3]
    chosen = jax.ShapeDtypeStruct((half * slots, terms, width, width), jnp.bfloat16)
    return pl.pallas_call(
        functools.partial(choose_kernel, len(shards), len(afters), sectors, half, slots),
        in_specs=in_smem(3)
        + [pl.BlockSpec(memory_space=pl.ANY)] * len(afters)
        + resident(len(shards)),
        out_specs=resident(2),
        out_shape=[chosen, chosen],
        compiler_params=pltpu.CompilerParams(vmem_limit_bytes=SPARE),
        cost_estimate=pl.CostEstimate(
            flops=0, bytes_accessed=8 * half * slots * terms * width * width, transcendentals=0
        ),
        name="choose",
    )(meta, places, partners, *afters, *shards)


def chunk_kernel(first, last, held, chunk, ahead, late, count, half, slots,
                 meta, places, sector_rows, partners, counts, after_ref, psi_ref, *rest):
    start, terms = chunk
    early_refs, rest = rest[: len(ahead)], rest[len(ahead) :]
    payloads, rest = rest[:count], rest[count:]
    near_rights, rest = rest[:2], rest[2:]
    devices = len(ahead) + len(late)
    far_rights, rest = rest[: devices // 2 - 1], rest[devices // 2 - 1 :]
    if not first:
        sum_in, rest = rest[0], rest[1:]
    sum_out, fold_ref, *rest = rest
    if late:
        spread_ops, after_left, after_ops, *rest = rest
    states, width = psi_ref.shape[1], psi_ref.shape[-1]
    groups = width // TILE
    views = dict(zip(late, source_views(payloads)))
    rights = list(near_rights) + [right.at[side] for right in far_rights for side in (0, 1)]
    for at, source in enumerate(late):
        operators = views[source][half * held * width :, :]
        spread_operators(operators, range(start, start + terms), spread_ops, at * terms, states)
    fold_ref[...] = jnp.zeros_like(fold_ref)
    if last:
        sum_out[...] = jnp.zeros_like(sum_out)

    def work(block, place, sector, own_rows, partner_rows):
        total = rest[0] if last else sum_out.at[block]
        columns = [
            jnp.concatenate(
                [rights[pair + at][block, term] for at in range(2) for term in range(terms)],
                axis=0,
            )
            for pair in range(0, devices, 2)
        ]

        def operated(device, term, group):
            if device in ahead:
                return early_refs[ahead.index(device)][block, term, group]
            return after_ops[late.index(device) * terms + term, group]

        def multiply(live_groups):
            if late:
                lefts = [
                    term_rows(views[source], place, held, start + term, live_groups * TILE)
                    for source in late
                    for term in range(terms)
                ]
                multiply_left(live_groups, lefts, psi_ref.at[block], after_left)
            targets = [(after_ops, (term,)) for term in range(len(late) * terms)]
            for group in range(0, live_groups, WIDE):
                if late:
                    apply_operators(group, group + WIDE, spread_ops, after_left, targets)
                parts = []
                for pair in range(0, devices, 2):
                    rows = jnp.concatenate(
                        [
                            jnp.concatenate(
                                [
                                    operated(pair + at, term, group + side)
                                    for at in range(2)
                                    for term in range(terms)
                                ],
                                axis=1,
                            )
                            for side in range(WIDE)
                        ],
                        axis=0,
                    )
                    parts.append(
                        jnp.dot(rows, columns[pair // 2], preferred_element_type=jnp.float32)
                    )
                while len(parts) > 1:
                    parts = [parts[at] + parts[at + 1] for at in range(0, len(parts), 2)]
                done = parts[0].reshape(WIDE, states, TILE, width)
                for side in range(WIDE):
                    tile = slice((group + side) * TILE, (group + side + 1) * TILE)
                    if first:
                        total[:, tile, :] = done[side]
                    else:
                        total[:, tile, :] = sum_in[block, :, tile, :] + done[side]

        by_live_rows(own_rows, groups, multiply)
        if last:
            mask = live_entries(own_rows, partner_rows, width)
            kept = jnp.where(mask, total[...], 0.0)
            fold_ref[...] += folded(kept * psi_ref[block].astype(jnp.float32))
            sum_out[block] = kept.astype(jnp.bfloat16)

    each_live_block(half, slots, (meta, places, sector_rows, partners, counts), work)


def chunk_call(first, last, held, chunk, ahead, late, scalars, slots, psi, early, payloads,
               rights, total, after):
    blocks, states, width = psi.shape[:3]
    groups, wide = width // TILE, states * TILE
    start, terms = chunk
    operands = [after, psi, *early, *payloads, *rights]
    aliases = {}
    if not first:
        operands.append(total)
        if not last:
            aliases = {len(scalars) + len(operands) - 1: 0}
    sum_dtype = jnp.bfloat16 if last else jnp.float32
    every = len(late) * terms
    scratch = []
    if late:
        scratch += [
            pltpu.VMEM((every, wide, wide), jnp.bfloat16),
            pltpu.VMEM((every, groups, wide, width), jnp.bfloat16),
            pltpu.VMEM((every, groups, wide, width), jnp.bfloat16),
        ]
    if last:
        scratch.append(pltpu.VMEM((states, width, width), jnp.float32))
    work = psi.size * terms * ((len(ahead) + len(late)) * width + len(late) * (width + wide))
    return pl.pallas_call(
        functools.partial(
            chunk_kernel, first, last, held, chunk, ahead, late, len(payloads),
            blocks // slots, slots,
        ),
        in_specs=in_smem(len(scalars))
        + [pl.BlockSpec(memory_space=pl.ANY)]
        + resident(len(operands) - 1),
        out_specs=resident(2),
        out_shape=[
            jax.ShapeDtypeStruct(psi.shape, sum_dtype),
            jax.ShapeDtypeStruct((8, width), jnp.float32),
        ],
        scratch_shapes=scratch,
        input_output_aliases=aliases,
        compiler_params=pltpu.CompilerParams(
            vmem_limit_bytes=(len(ahead) + len(late)) * SPARE // 4
            + 2 * every * wide * (wide + 2 * groups * width)
            + 4 * int(last) * states * width * width
        ),
        cost_estimate=pl.CostEstimate(
            flops=work // HASTE, bytes_accessed=psi.size // HASTE, transcendentals=0
        ),
        name="chunk",
    )(*scalars, *operands)


def residual_kernel(half, slots, meta, places, sector_rows, partners, counts,
                    folds_ref, live_psi, own_ref, other_ref, psi_ref, out_ref, quotient_ref,
                    other_psi, staged, read_sems, write_sems):
    scalars = (meta, places, sector_rows, partners, counts)
    blocks, width = own_ref.shape[0], own_ref.shape[-1]
    depth = staged.shape[0]

    def where(block, side):
        index = (meta[1] ^ side) * half + block // slots
        return places[index], block % slots, index

    def read(block):
        sector, slot, _ = where(block, 1)
        return pltpu.make_async_copy(
            psi_ref.at[sector, slot], other_psi.at[block], read_sems.at[block]
        )

    def write(step):
        sector, slot, _ = where(step % blocks, step // blocks)
        return pltpu.make_async_copy(
            staged.at[step % depth], out_ref.at[sector, slot], write_sems.at[step % depth]
        )

    for block in range(blocks):
        read(block).start()
    quotient = jnp.sum(folds_ref[0:8, :]) / jnp.sum(folds_ref[8:16, :])
    quotient_ref[0] = quotient
    for step in range(2 * blocks):
        block, side = step % blocks, step // blocks
        if step >= depth:
            write(step - depth).wait()
        sector, slot, index = where(block, side)
        _, live, own_rows, partner_rows = block_facts(scalars, index, slot)
        mask = live_entries(jnp.where(live, own_rows, 0), partner_rows, width)
        if side:
            read(block).wait()
            values, sums = other_psi[block], other_ref[block]
        else:
            values, sums = live_psi[block], own_ref[block]
        scaled = quotient * jnp.where(mask, values.astype(jnp.float32), 0.0)
        staged[step % depth] = (sums.astype(jnp.float32) - scaled).astype(jnp.bfloat16)
        write(step).start()
    for step in range(2 * blocks - min(depth, 2 * blocks), 2 * blocks):
        write(step).wait()


def residual_call(scalars, folds, psi, live_psi, own, other):
    sectors, slots, states, width = psi.shape[:4]
    blocks = own.shape[0]
    depth = 4
    in_hbm = [pl.BlockSpec(memory_space=pltpu.HBM)]
    return pl.pallas_call(
        functools.partial(residual_kernel, sectors // 2, slots),
        in_specs=in_smem(len(scalars)) + resident(4) + in_hbm,
        out_specs=in_hbm + in_smem(1),
        out_shape=[
            jax.ShapeDtypeStruct(psi.shape, jnp.bfloat16),
            jax.ShapeDtypeStruct((1,), jnp.float32),
        ],
        scratch_shapes=[
            pltpu.VMEM((blocks, states, width, width), jnp.bfloat16),
            pltpu.VMEM((depth, states, width, width), jnp.bfloat16),
            pltpu.SemaphoreType.DMA((blocks,)),
            pltpu.SemaphoreType.DMA((depth,)),
        ],
        compiler_params=pltpu.CompilerParams(vmem_limit_bytes=41 * MIB),
        cost_estimate=pl.CostEstimate(
            flops=3 * psi.size, bytes_accessed=6 * psi.size, transcendentals=0
        ),
        name="residual",
    )(*scalars, folds, live_psi, own, other, psi)


def on_device(
    devices, rings, psi, left_env, right_env, local_ops, term_op, sector_rows, block_partner,
    block_count,
):
    sectors, slots, states, width = psi.shape[:4]
    terms = left_env.shape[1]
    half = sectors // 2
    me = lax.axis_index("term")
    ring = lax.axis_index("sec")
    core = me % 2
    meta = jnp.stack([ring * sectors, core, me, ring]).astype(jnp.int32)

    near_rows = lax.dynamic_slice_in_dim(sector_rows, ring * sectors, sectors)
    weight = block_count * (near_rows + width // 2)
    order = jnp.arange(sectors, dtype=jnp.int32)
    ahead = (weight[None, :] > weight[:, None]) | (
        (weight[None, :] == weight[:, None]) & (order[None, :] < order[:, None])
    )
    rank = jnp.sum(ahead.astype(jnp.int32), axis=1)
    index = ((rank ^ (rank >> 1)) & 1) * half + (rank >> 1)
    places = jnp.sum(jnp.where(index[None, :] == order[:, None], order[None, :], 0), axis=1)
    scalars = (meta, places, sector_rows, block_partner, block_count)

    def swap(value, bits, axis="term", size=devices):
        return lax.ppermute(value, axis, [(i, i ^ bits) for i in range(size)])

    def to_far_chips(near, received):
        both = stack_call(near, received)
        return both, [swap(both, bits) for bits in range(2, devices, 2)]

    chunks = [(at, 1) for at in range(terms)]
    ordered = jnp.roll(places, -core * half)
    mine, theirs, *shares = pack_call(
        chunks, ordered, term_op, local_ops, left_env, right_env
    )
    near_left = swap(theirs, 1)
    both_lefts, far_lefts = to_far_chips(mine, near_left)

    shards, rights = [], []

    def gather(token):
        own = shares[len(shards)]
        if token is not None:
            own, _ = lax.optimization_barrier((own, token))
        moved = [own]
        for distance in range(1, rings):
            pairs = [(i, (i + distance) % rings) for i in range(rings)]
            moved.append(lax.ppermute(own, "sec", pairs))
        shards.append(moved)

    def choose(token):
        afters = [token] + (rights[-1][2:] if rights else [])
        mine, other = choose_call(scalars, half, slots, shards[len(rights)], afters)
        received = swap(other, 1)
        both, far_rights = to_far_chips(mine, received)
        rights.append([mine, received] + far_rights)
        return both

    products = {}
    shape = (half * slots, slots, states, width)
    far = tuple(range(2, devices))

    def go_left(sources, which, token, first=False, waits=()):
        items = [(source, *chunks[at]) for at in which for source in sources]
        near = [source for source in sources if source < 2]
        payloads = [(mine, near_left)[source] for source in near]
        if len(near) < len(sources):
            payloads += far_lefts
        renamed = [(sources.index(source), start, count) for source, start, count in items]
        outs = left_call(
            first, scalars, terms, renamed, shape, psi if first else live_psi, payloads,
            [token, *waits],
        )
        for at, out in zip([(at, source) for at in which for source in sources], outs):
            products[at] = out
        return outs[len(items) :]

    every = range(len(chunks))
    gather(None)
    token, live_psi, squares = go_left((0,), every, both_lefts, True)
    gather(token)
    token = choose(token)
    token, = go_left((1,), every[1:], token, waits=far_lefts)
    total = None
    for at, chunk in enumerate(chunks):
        last = at == len(chunks) - 1
        if len(rights) < len(chunks):
            token = choose(token)
        if len(shards) < len(chunks):
            gather(token)
        ahead = tuple(source for source in range(devices) if (at, source) in products)
        late = tuple(source for source in range(devices) if source not in ahead)
        payloads = ([near_left] if 1 in late else []) + (far_lefts if late else [])
        total, token = chunk_call(
            at == 0, last, terms, chunk, ahead, late, scalars, slots, live_psi,
            [products.pop((at, source)) for source in ahead], payloads,
            rights[at], total, token,
        )
        if at == len(chunks) - 3:
            token, = go_left(far, [len(chunks) - 1], token)

    other = swap(total, 1)
    folds = jnp.concatenate([token, squares], axis=0)
    bits = 1
    while bits < rings:
        folds = folds + swap(folds, bits, "sec", rings)
        bits *= 2
    folds = folds + swap(folds, 1)
    residual, rayleigh = residual_call(scalars, folds, psi, live_psi, total, other)
    return residual, rayleigh


def solution(mesh):
    placed = (
        P(("groups", "sec"), None, None, None, None),
        P(("groups", "sec"), "term", None, None),
        P(("groups", "sec"), "term", None, None),
        P(),
        P("term"),
        P("groups"),
        P(("groups", "sec"), None),
        P(("groups", "sec")),
    )
    return jax.shard_map(
        functools.partial(on_device, mesh.shape["term"], mesh.shape["sec"]),
        mesh=mesh,
        in_specs=placed,
        out_specs=(P(("groups", "sec"), None, None, None, None), P("groups")),
        check_vma=False,
    )
```

```python
import functools

import jax
import jax.numpy as jnp
from jax import lax
from jax.experimental import pallas as pl
from jax.experimental.pallas import tpu as pltpu
from jax.sharding import PartitionSpec as P

TILE = 16
WIDE = 2
MIB = 1024 * 1024
SPARE = 3 * MIB // 2
HASTE = 256


def block_facts(scalars, index, slot):
    meta, places, sector_rows, partners, counts = scalars
    sector = places[index]
    live = slot < counts[sector]
    own_rows = sector_rows[meta[0] + sector]
    partner_rows = sector_rows[partners[sector, slot]]
    return sector, live, own_rows, partner_rows


def live_entries(own_rows, partner_rows, width):
    left = lax.broadcasted_iota(jnp.int32, (1, width, width), 1) < own_rows
    right = lax.broadcasted_iota(jnp.int32, (1, width, width), 2) < partner_rows
    return left & right


def folded(values):
    states, width = values.shape[0], values.shape[-1]
    return jnp.sum(values.reshape(states * width // 8, 8, width), axis=0)


def by_live_rows(own_rows, groups, work):
    few = 3 * groups // 4
    pl.when(own_rows <= few * TILE)(functools.partial(work, few))
    pl.when(own_rows > few * TILE)(functools.partial(work, groups))


def spread_operators(ops_ref, chosen, spread_ops, at, states):
    width, wide = ops_ref.shape[-1], states * TILE
    row_state = lax.broadcasted_iota(jnp.int32, (wide, states), 0) // TILE
    column = lax.broadcasted_iota(jnp.int32, (wide, states), 1)
    pick_rows = (row_state == column).astype(jnp.bfloat16)
    row = lax.broadcasted_iota(jnp.int32, (width, wide), 0)
    column_state = lax.broadcasted_iota(jnp.int32, (width, wide), 1) // TILE
    pick_columns = (row == column_state).astype(jnp.bfloat16)
    inner_row = lax.rem(lax.broadcasted_iota(jnp.int32, (wide, wide), 0), TILE)
    inner_column = lax.rem(lax.broadcasted_iota(jnp.int32, (wide, wide), 1), TILE)
    for term in chosen:
        operator = ops_ref[term * states : (term + 1) * states, :]
        rows = jnp.dot(pick_rows, operator, preferred_element_type=jnp.float32)
        full = jnp.dot(
            rows.astype(jnp.bfloat16), pick_columns, preferred_element_type=jnp.float32
        )
        spread_ops[at] = jnp.where(inner_row == inner_column, full, 0.0).astype(jnp.bfloat16)
        at += 1


def multiply_left(groups, lefts, live_psi, after_left):
    rows = groups * TILE
    states, width = live_psi.shape[0], live_psi.shape[-1]
    stacked = jnp.concatenate(lefts, axis=0)
    for pair in range(states // WIDE):
        columns = jnp.concatenate([live_psi[pair * WIDE + at] for at in range(WIDE)], axis=1)
        done = jnp.dot(stacked, columns, preferred_element_type=jnp.float32).astype(jnp.bfloat16)
        for term in range(len(lefts)):
            for at in range(WIDE):
                state = pair * WIDE + at
                after_left[term, :groups, state * TILE : (state + 1) * TILE, :] = done[
                    term * rows : (term + 1) * rows, at * width : (at + 1) * width
                ].reshape(groups, TILE, width)


def apply_operators(low, high, spread_ops, after_left, targets):
    width = after_left.shape[-1]
    for group in range(low, high, WIDE):
        for term, (target, lead) in enumerate(targets):
            columns = jnp.concatenate(
                [after_left[term, group + at] for at in range(WIDE)], axis=1
            )
            done = jnp.dot(
                spread_ops[term], columns, preferred_element_type=jnp.float32
            ).astype(jnp.bfloat16)
            for at in range(WIDE):
                target[(*lead, group + at)] = done[:, at * width : (at + 1) * width]


def each_live_block(half, slots, scalars, work):
    meta = scalars[0]

    def visit(block, carry):
        place, slot = block // slots, lax.rem(block, slots)
        sector, live, own_rows, partner_rows = block_facts(
            scalars, meta[1] * half + place, slot
        )
        pl.when(live)(functools.partial(work, block, place, sector, own_rows, partner_rows))
        return carry

    lax.fori_loop(0, half * slots, visit, 0)


def pack_kernel(chunks, half, terms, places, term_op, ops_ref, left_ref, right_ref, *rest):
    payloads, rest = rest[:2], rest[2:]
    shares, sems = rest[: len(chunks)], rest[len(chunks)]
    states, width = ops_ref.shape[1], left_ref.shape[-1]
    copied = half * terms * width
    for part, payload in enumerate(payloads):
        for place in range(half):
            pltpu.make_async_copy(
                left_ref.at[places[part * half + place]],
                payload.at[pl.ds(place * terms * width, terms * width)],
                sems.at[part],
            ).start()
    moves = []
    for at, (start, length) in enumerate(chunks):
        move = pltpu.make_async_copy(
            right_ref.at[:, pl.ds(start, length)], shares[at], sems.at[2 + at]
        )
        move.start()
        moves.append(move)
    for payload in payloads:
        for term in range(terms):
            rows = slice(copied + term * states, copied + (term + 1) * states)
            payload[rows, :] = jnp.zeros((states, width), jnp.bfloat16)
            payload[rows, :states] = ops_ref[term_op[term]]
    for part, payload in enumerate(payloads):
        whole = payload.at[pl.ds(0, copied)]
        pltpu.make_async_copy(whole, whole, sems.at[part]).wait()
    for move in moves:
        move.wait()


def pack_call(chunks, places, term_op, local_ops, left_env, right_env):
    sectors, terms, width = left_env.shape[:3]
    half, states = sectors // 2, local_ops.shape[1]
    payload = jax.ShapeDtypeStruct((terms * (half * width + states), width), jnp.bfloat16)
    shares = [
        jax.ShapeDtypeStruct((sectors, length, width, width), jnp.bfloat16)
        for start, length in chunks
    ]
    return pl.pallas_call(
        functools.partial(pack_kernel, chunks, half, terms),
        in_specs=in_smem(2) + resident(1) + [pl.BlockSpec(memory_space=pltpu.HBM)] * 2,
        out_specs=resident(2 + len(chunks)),
        out_shape=[payload, payload] + shares,
        scratch_shapes=[pltpu.SemaphoreType.DMA((2 + len(chunks),))],
        compiler_params=pltpu.CompilerParams(vmem_limit_bytes=58 * MIB),
        cost_estimate=pl.CostEstimate(
            flops=0, bytes_accessed=4 * left_env.size, transcendentals=0
        ),
        name="pack",
    )(places, term_op, local_ops, left_env.reshape(sectors, terms * width, width), right_env)


def source_views(payloads):
    views = []
    for payload in payloads:
        views += [payload] if len(payload.shape) == 2 else [payload.at[0], payload.at[1]]
    return views


def term_rows(view, place, held, term, rows):
    width = view.shape[-1]
    return view[pl.ds(pl.multiple_of((place * held + term) * width, width), rows), :]


def left_kernel(first, held, items, count, afters, half, slots, meta, places, sector_rows,
                partners, counts, *rest):
    scalars = (meta, places, sector_rows, partners, counts)
    psi_ref, rest = rest[afters], rest[afters + 1 :]
    payloads, rest = rest[:count], rest[count:]
    outs, rest = rest[: len(items)], rest[len(items) :]
    token_ref, rest = rest[0], rest[1:]
    if first:
        live_psi, square_ref, spread_ops, after_left, sems = rest
    else:
        live_psi = psi_ref
        spread_ops, after_left = rest
    states, width = live_psi.shape[1], live_psi.shape[-1]
    views = source_views(payloads)

    def fetch(block, sector):
        return pltpu.make_async_copy(
            psi_ref.at[sector, lax.rem(block, slots)], live_psi.at[block], sems.at[block]
        )

    if first:
        each_live_block(
            half, slots, scalars, lambda block, place, sector, *rows: fetch(block, sector).start()
        )
        square_ref[...] = jnp.zeros_like(square_ref)
    at = 0
    for source, start, terms in items:
        operators = views[source][half * held * width :, :]
        spread_operators(operators, range(start, start + terms), spread_ops, at, states)
        at += terms
    token_ref[...] = jnp.zeros_like(token_ref)

    def work(block, place, sector, own_rows, partner_rows):
        if first:
            fetch(block, sector).wait()
            mask = live_entries(own_rows, partner_rows, width)
            kept = jnp.where(mask, live_psi[block], jnp.zeros((), jnp.bfloat16))
            live_psi[block] = kept
            wide_psi = kept.astype(jnp.float32)
            square_ref[...] += folded(wide_psi * wide_psi)
        targets = [
            (outs[at], (block, term))
            for at, (source, start, terms) in enumerate(items)
            for term in range(terms)
        ]

        def multiply(groups):
            lefts = [
                term_rows(views[source], place, held, start + term, groups * TILE)
                for source, start, terms in items
                for term in range(terms)
            ]
            multiply_left(groups, lefts, live_psi.at[block], after_left)
            apply_operators(0, groups, spread_ops, after_left, targets)

        by_live_rows(own_rows, width // TILE, multiply)

    each_live_block(half, slots, scalars, work)


def resident(count):
    return [pl.BlockSpec(memory_space=pltpu.VMEM)] * count


def in_smem(count):
    return [pl.BlockSpec(memory_space=pltpu.SMEM)] * count


def left_call(first, scalars, held, items, shape, psi, payloads, afters):
    blocks, slots, states, width = shape
    groups, wide = width // TILE, states * TILE
    every = sum(terms for source, start, terms in items)
    fold_shape = jax.ShapeDtypeStruct((8, width), jnp.float32)
    out_shape = [
        jax.ShapeDtypeStruct((blocks, terms, groups, wide, width), jnp.bfloat16)
        for source, start, terms in items
    ] + [fold_shape]
    scratch = [
        pltpu.VMEM((every, wide, wide), jnp.bfloat16),
        pltpu.VMEM((every, groups, wide, width), jnp.bfloat16),
    ]
    if first:
        live_psi = jax.ShapeDtypeStruct((blocks, states, width, width), jnp.bfloat16)
        out_shape += [live_psi, fold_shape]
        scratch.append(pltpu.SemaphoreType.DMA((blocks,)))
    psi_spec = [pl.BlockSpec(memory_space=pltpu.HBM)] if first else resident(1)
    return pl.pallas_call(
        functools.partial(
            left_kernel, first, held, items, len(payloads), len(afters), blocks // slots, slots
        ),
        in_specs=in_smem(len(scalars))
        + [pl.BlockSpec(memory_space=pl.ANY)] * len(afters)
        + psi_spec
        + resident(len(payloads)),
        out_specs=resident(len(out_shape)),
        out_shape=out_shape,
        scratch_shapes=scratch,
        compiler_params=pltpu.CompilerParams(
            vmem_limit_bytes=max(
                28 * MIB if first else 0,
                SPARE + 2 * every * (wide * wide + groups * wide * width),
            )
        ),
        cost_estimate=pl.CostEstimate(
            flops=psi.size * every * (width + wide) // HASTE,
            bytes_accessed=psi.size // HASTE,
            transcendentals=0,
        ),
        name="left",
    )(*scalars, *afters, psi, *payloads)


def stack_kernel(start, near_ref, received_ref, both_ref):
    terms = both_ref.shape[2] if len(both_ref.shape) == 5 else None
    for side, ref in enumerate((near_ref, received_ref)):
        both_ref[side] = ref[...] if start is None else ref[:, start : start + terms]


def stack_call(near, received, chunk=None):
    start, terms = chunk or (None, None)
    shape = near.shape if chunk is None else (near.shape[0], terms) + near.shape[2:]
    return pl.pallas_call(
        functools.partial(stack_kernel, start),
        in_specs=resident(2),
        out_specs=resident(1)[0],
        out_shape=jax.ShapeDtypeStruct((2,) + shape, near.dtype),
        compiler_params=pltpu.CompilerParams(vmem_limit_bytes=SPARE),
        cost_estimate=pl.CostEstimate(flops=0, bytes_accessed=4096, transcendentals=0),
        name="stack",
    )(near, received)


def choose_kernel(count, afters, half, slots, meta, places, partners, *rest):
    rest = rest[afters:]
    pieces, (mine_ref, other_ref) = rest[:count], rest[count:]
    sectors = pieces[0].shape[1]
    for part, out_ref in enumerate((mine_ref, other_ref)):
        for block in range(half * slots):
            sector = places[(meta[1] ^ part) * half + block // slots]
            partner = partners[sector, block % slots]
            away = meta[3] ^ (partner // sectors)
            place = lax.rem(partner, sectors)
            for at in range(count):
                @pl.when(away // 2 == at)
                def _(at=at, away=away, place=place, block=block, out_ref=out_ref):
                    out_ref[block] = pieces[at][away & 1, place]


def choose_call(scalars, half, slots, pieces, afters):
    meta, places, _, partners, _ = scalars
    terms, width = pieces[0].shape[2:4]
    chosen = jax.ShapeDtypeStruct((half * slots, terms, width, width), jnp.bfloat16)
    return pl.pallas_call(
        functools.partial(choose_kernel, len(pieces), len(afters), half, slots),
        in_specs=in_smem(3)
        + [pl.BlockSpec(memory_space=pl.ANY)] * len(afters)
        + resident(len(pieces)),
        out_specs=resident(2),
        out_shape=[chosen, chosen],
        compiler_params=pltpu.CompilerParams(vmem_limit_bytes=SPARE),
        cost_estimate=pl.CostEstimate(flops=0, bytes_accessed=4096, transcendentals=0),
        name="choose",
    )(meta, places, partners, *afters, *pieces)


def chunk_kernel(first, last, held, chunk, ahead, late, count, half, slots,
                 meta, places, sector_rows, partners, counts, after_ref, psi_ref, *rest):
    start, terms = chunk
    early_refs, rest = rest[: len(ahead)], rest[len(ahead) :]
    payloads, rest = rest[:count], rest[count:]
    near_rights, rest = rest[:2], rest[2:]
    devices = len(ahead) + len(late)
    far_rights, rest = rest[: devices // 2 - 1], rest[devices // 2 - 1 :]
    if not first:
        sum_in, rest = rest[0], rest[1:]
    sum_out, fold_ref, *rest = rest
    if late:
        spread_ops, after_left, after_ops, *rest = rest
    states, width = psi_ref.shape[1], psi_ref.shape[-1]
    groups = width // TILE
    views = dict(zip(late, source_views(payloads)))
    rights = list(near_rights) + [right.at[side] for right in far_rights for side in (0, 1)]
    for at, source in enumerate(late):
        operators = views[source][half * held * width :, :]
        spread_operators(operators, range(start, start + terms), spread_ops, at * terms, states)
    fold_ref[...] = jnp.zeros_like(fold_ref)
    if last:
        sum_out[...] = jnp.zeros_like(sum_out)

    def work(block, place, sector, own_rows, partner_rows):
        total = rest[0] if last else sum_out.at[block]
        columns = [
            jnp.concatenate(
                [rights[pair + at][block, term] for at in range(2) for term in range(terms)],
                axis=0,
            )
            for pair in range(0, devices, 2)
        ]

        def operated(device, term, group):
            if device in ahead:
                return early_refs[ahead.index(device)][block, term, group]
            return after_ops[late.index(device) * terms + term, group]

        def multiply(live_groups):
            if late:
                lefts = [
                    term_rows(views[source], place, held, start + term, live_groups * TILE)
                    for source in late
                    for term in range(terms)
                ]
                multiply_left(live_groups, lefts, psi_ref.at[block], after_left)
            targets = [(after_ops, (term,)) for term in range(len(late) * terms)]
            for group in range(0, live_groups, WIDE):
                if late:
                    apply_operators(group, group + WIDE, spread_ops, after_left, targets)
                parts = []
                for pair in range(0, devices, 2):
                    rows = jnp.concatenate(
                        [
                            jnp.concatenate(
                                [
                                    operated(pair + at, term, group + side)
                                    for at in range(2)
                                    for term in range(terms)
                                ],
                                axis=1,
                            )
                            for side in range(WIDE)
                        ],
                        axis=0,
                    )
                    parts.append(
                        jnp.dot(rows, columns[pair // 2], preferred_element_type=jnp.float32)
                    )
                while len(parts) > 1:
                    parts = [parts[at] + parts[at + 1] for at in range(0, len(parts), 2)]
                done = parts[0].reshape(WIDE, states, TILE, width)
                for side in range(WIDE):
                    tile = slice((group + side) * TILE, (group + side + 1) * TILE)
                    if first:
                        total[:, tile, :] = done[side]
                    else:
                        total[:, tile, :] = sum_in[block, :, tile, :] + done[side]

        by_live_rows(own_rows, groups, multiply)
        if last:
            mask = live_entries(own_rows, partner_rows, width)
            kept = jnp.where(mask, total[...], 0.0)
            fold_ref[...] += folded(kept * psi_ref[block].astype(jnp.float32))
            sum_out[block] = kept.astype(jnp.bfloat16)

    each_live_block(half, slots, (meta, places, sector_rows, partners, counts), work)


def chunk_call(first, last, held, chunk, ahead, late, scalars, slots, psi, early, payloads,
               rights, total, after):
    blocks, states, width = psi.shape[:3]
    groups, wide = width // TILE, states * TILE
    start, terms = chunk
    operands = [after, psi, *early, *payloads, *rights]
    aliases = {}
    if not first:
        operands.append(total)
        if not last:
            aliases = {len(scalars) + len(operands) - 1: 0}
    sum_dtype = jnp.bfloat16 if last else jnp.float32
    every = len(late) * terms
    scratch = []
    if late:
        scratch += [
            pltpu.VMEM((every, wide, wide), jnp.bfloat16),
            pltpu.VMEM((every, groups, wide, width), jnp.bfloat16),
            pltpu.VMEM((every, groups, wide, width), jnp.bfloat16),
        ]
    if last:
        scratch.append(pltpu.VMEM((states, width, width), jnp.float32))
    work = psi.size * terms * ((len(ahead) + len(late)) * width + len(late) * (width + wide))
    return pl.pallas_call(
        functools.partial(
            chunk_kernel, first, last, held, chunk, ahead, late, len(payloads),
            blocks // slots, slots,
        ),
        in_specs=in_smem(len(scalars))
        + [pl.BlockSpec(memory_space=pl.ANY)]
        + resident(len(operands) - 1),
        out_specs=resident(2),
        out_shape=[
            jax.ShapeDtypeStruct(psi.shape, sum_dtype),
            jax.ShapeDtypeStruct((8, width), jnp.float32),
        ],
        scratch_shapes=scratch,
        input_output_aliases=aliases,
        compiler_params=pltpu.CompilerParams(
            vmem_limit_bytes=(len(ahead) + len(late)) * SPARE // 4
            + 2 * every * wide * (wide + 2 * groups * width)
            + 4 * int(last) * states * width * width
        ),
        cost_estimate=pl.CostEstimate(
            flops=work // HASTE, bytes_accessed=psi.size // HASTE, transcendentals=0
        ),
        name="chunk",
    )(*scalars, *operands)


def residual_kernel(half, slots, meta, places, sector_rows, partners, counts,
                    folds_ref, live_psi, own_ref, other_ref, psi_ref, out_ref, quotient_ref,
                    other_psi, staged, read_sems, write_sems):
    scalars = (meta, places, sector_rows, partners, counts)
    blocks, width = own_ref.shape[0], own_ref.shape[-1]
    depth = staged.shape[0]

    def where(block, side):
        index = (meta[1] ^ side) * half + block // slots
        return places[index], block % slots, index

    def read(block):
        sector, slot, _ = where(block, 1)
        return pltpu.make_async_copy(
            psi_ref.at[sector, slot], other_psi.at[block], read_sems.at[block]
        )

    def write(step):
        sector, slot, _ = where(step % blocks, step // blocks)
        return pltpu.make_async_copy(
            staged.at[step % depth], out_ref.at[sector, slot], write_sems.at[step % depth]
        )

    for block in range(blocks):
        read(block).start()
    quotient = jnp.sum(folds_ref[0:8, :]) / jnp.sum(folds_ref[8:16, :])
    quotient_ref[0] = quotient
    for step in range(2 * blocks):
        block, side = step % blocks, step // blocks
        if step >= depth:
            write(step - depth).wait()
        sector, slot, index = where(block, side)
        _, live, own_rows, partner_rows = block_facts(scalars, index, slot)
        mask = live_entries(jnp.where(live, own_rows, 0), partner_rows, width)
        if side:
            read(block).wait()
            values, sums = other_psi[block], other_ref[block]
        else:
            values, sums = live_psi[block], own_ref[block]
        scaled = quotient * jnp.where(mask, values.astype(jnp.float32), 0.0)
        staged[step % depth] = (sums.astype(jnp.float32) - scaled).astype(jnp.bfloat16)
        write(step).start()
    for step in range(2 * blocks - min(depth, 2 * blocks), 2 * blocks):
        write(step).wait()


def residual_call(scalars, folds, psi, live_psi, own, other):
    sectors, slots, states, width = psi.shape[:4]
    blocks = own.shape[0]
    depth = 4
    in_hbm = [pl.BlockSpec(memory_space=pltpu.HBM)]
    return pl.pallas_call(
        functools.partial(residual_kernel, sectors // 2, slots),
        in_specs=in_smem(len(scalars)) + resident(4) + in_hbm,
        out_specs=in_hbm + in_smem(1),
        out_shape=[
            jax.ShapeDtypeStruct(psi.shape, jnp.bfloat16),
            jax.ShapeDtypeStruct((1,), jnp.float32),
        ],
        scratch_shapes=[
            pltpu.VMEM((blocks, states, width, width), jnp.bfloat16),
            pltpu.VMEM((depth, states, width, width), jnp.bfloat16),
            pltpu.SemaphoreType.DMA((blocks,)),
            pltpu.SemaphoreType.DMA((depth,)),
        ],
        compiler_params=pltpu.CompilerParams(vmem_limit_bytes=41 * MIB),
        cost_estimate=pl.CostEstimate(
            flops=3 * psi.size, bytes_accessed=6 * psi.size, transcendentals=0
        ),
        name="residual",
    )(*scalars, folds, live_psi, own, other, psi)


def on_device(
    devices, rings, psi, left_env, right_env, local_ops, term_op, sector_rows, block_partner,
    block_count,
):
    sectors, slots, states, width = psi.shape[:4]
    terms = left_env.shape[1]
    half = sectors // 2
    me = lax.axis_index("term")
    ring = lax.axis_index("sec")
    core = me % 2
    meta = jnp.stack([ring * sectors, core, me, ring]).astype(jnp.int32)

    near_rows = lax.dynamic_slice_in_dim(sector_rows, ring * sectors, sectors)
    weight = block_count * (near_rows + width // 2)
    order = jnp.arange(sectors, dtype=jnp.int32)
    ahead = (weight[None, :] > weight[:, None]) | (
        (weight[None, :] == weight[:, None]) & (order[None, :] < order[:, None])
    )
    rank = jnp.sum(ahead.astype(jnp.int32), axis=1)
    index = ((rank ^ (rank >> 1)) & 1) * half + (rank >> 1)
    places = jnp.sum(jnp.where(index[None, :] == order[:, None], order[None, :], 0), axis=1)
    scalars = (meta, places, sector_rows, block_partner, block_count)

    def swap(value, bits, axis="term", size=devices):
        return lax.ppermute(value, axis, [(i, i ^ bits) for i in range(size)])

    def to_far_chips(near, received):
        both = stack_call(near, received)
        return both, [swap(both, bits) for bits in range(2, devices, 2)]

    chunks = [(at, 1) for at in range(terms)]
    ordered = jnp.roll(places, -core * half)
    parcels = [chunks[0], (chunks[0][1], terms - chunks[0][1])]
    mine, theirs, *shares = pack_call(
        parcels, ordered, term_op, local_ops, left_env, right_env
    )
    near_left = swap(theirs, 1)
    both_lefts, far_lefts = to_far_chips(mine, near_left)

    shards, rights = [], []
    swapped = [swap(share, 1, "sec", rings) for share in shares]

    def gather(token=None):
        at = len(shards)
        if at == 0:
            pair = stack_call(shares[0], swapped[0])
        else:
            start, length = chunks[at]
            pair = stack_call(shares[1], swapped[1], (start - parcels[1][0], length))
        sent = pair
        if token is not None:
            sent, _ = lax.optimization_barrier((pair, token))
        pieces = [pair]
        bits = 2
        while bits < rings:
            source = [sent] + pieces[1:]
            pieces = pieces + [swap(piece, bits, "sec", rings) for piece in source]
            bits *= 2
        shards.append(pieces)

    def choose(token):
        afters = [token] + (rights[-1][2:] if rights else [])
        mine, other = choose_call(scalars, half, slots, shards[len(rights)], afters)
        received = swap(other, 1)
        both, far_rights = to_far_chips(mine, received)
        rights.append([mine, received] + far_rights)
        return both

    products = {}
    shape = (half * slots, slots, states, width)
    far = tuple(range(2, devices))

    def go_left(sources, which, token, first=False, waits=()):
        items = [(source, *chunks[at]) for at in which for source in sources]
        near = [source for source in sources if source < 2]
        payloads = [(mine, near_left)[source] for source in near]
        if len(near) < len(sources):
            payloads += far_lefts
        renamed = [(sources.index(source), start, count) for source, start, count in items]
        outs = left_call(
            first, scalars, terms, renamed, shape, psi if first else live_psi, payloads,
            [token, *waits],
        )
        for at, out in zip([(at, source) for at in which for source in sources], outs):
            products[at] = out
        return outs[len(items) :]

    every = range(len(chunks))
    gather()
    token, live_psi, squares = go_left((0,), every, both_lefts, True)
    gather()
    token = choose(token)
    token, = go_left((1,), every[1:], token, waits=far_lefts)
    total = None
    for at, chunk in enumerate(chunks):
        last = at == len(chunks) - 1
        if len(shards) < len(chunks):
            gather(shards[at][-1])
        if len(rights) < len(chunks):
            token = choose(token)
        ahead = tuple(source for source in range(devices) if (at, source) in products)
        late = tuple(source for source in range(devices) if source not in ahead)
        payloads = ([near_left] if 1 in late else []) + (far_lefts if late else [])
        total, token = chunk_call(
            at == 0, last, terms, chunk, ahead, late, scalars, slots, live_psi,
            [products.pop((at, source)) for source in ahead], payloads,
            rights[at], total, token,
        )
        if at == len(chunks) - 3:
            token, = go_left(far, [len(chunks) - 1], token)

    other = swap(total, 1)
    folds = jnp.concatenate([token, squares], axis=0)
    bits = 1
    while bits < rings:
        folds = folds + swap(folds, bits, "sec", rings)
        bits *= 2
    folds = folds + swap(folds, 1)
    residual, rayleigh = residual_call(scalars, folds, psi, live_psi, total, other)
    return residual, rayleigh


def solution(mesh):
    placed = (
        P(("groups", "sec"), None, None, None, None),
        P(("groups", "sec"), "term", None, None),
        P(("groups", "sec"), "term", None, None),
        P(),
        P("term"),
        P("groups"),
        P(("groups", "sec"), None),
        P(("groups", "sec")),
    )
    return jax.shard_map(
        functools.partial(on_device, mesh.shape["term"], mesh.shape["sec"]),
        mesh=mesh,
        in_specs=placed,
        out_specs=(P(("groups", "sec"), None, None, None, None), P("groups")),
        check_vma=False,
    )
```

```python
import functools

import jax
import jax.numpy as jnp
from jax import lax
from jax.experimental import pallas as pl
from jax.experimental.pallas import tpu as pltpu
from jax.sharding import PartitionSpec as P

TILE = 16
WIDE = 2
MIB = 1024 * 1024
SPARE = 3 * MIB // 2
HASTE = 256


def block_facts(scalars, index, slot):
    meta, places, sector_rows, partners, counts = scalars
    sector = places[index]
    live = slot < counts[sector]
    own_rows = sector_rows[meta[0] + sector]
    partner_rows = sector_rows[partners[sector, slot]]
    return sector, live, own_rows, partner_rows


def live_entries(own_rows, partner_rows, width):
    left = lax.broadcasted_iota(jnp.int32, (1, width, width), 1) < own_rows
    right = lax.broadcasted_iota(jnp.int32, (1, width, width), 2) < partner_rows
    return left & right


def folded(values):
    states, width = values.shape[0], values.shape[-1]
    return jnp.sum(values.reshape(states * width // 8, 8, width), axis=0)


def by_live_rows(own_rows, groups, work):
    few = 3 * groups // 4
    pl.when(own_rows <= few * TILE)(functools.partial(work, few))
    pl.when(own_rows > few * TILE)(functools.partial(work, groups))


def spread_operators(ops_ref, chosen, spread_ops, at, states):
    width, wide = ops_ref.shape[-1], states * TILE
    row_state = lax.broadcasted_iota(jnp.int32, (wide, states), 0) // TILE
    column = lax.broadcasted_iota(jnp.int32, (wide, states), 1)
    pick_rows = (row_state == column).astype(jnp.bfloat16)
    row = lax.broadcasted_iota(jnp.int32, (width, wide), 0)
    column_state = lax.broadcasted_iota(jnp.int32, (width, wide), 1) // TILE
    pick_columns = (row == column_state).astype(jnp.bfloat16)
    inner_row = lax.rem(lax.broadcasted_iota(jnp.int32, (wide, wide), 0), TILE)
    inner_column = lax.rem(lax.broadcasted_iota(jnp.int32, (wide, wide), 1), TILE)
    for term in chosen:
        operator = ops_ref[term * states : (term + 1) * states, :]
        rows = jnp.dot(pick_rows, operator, preferred_element_type=jnp.float32)
        full = jnp.dot(
            rows.astype(jnp.bfloat16), pick_columns, preferred_element_type=jnp.float32
        )
        spread_ops[at] = jnp.where(inner_row == inner_column, full, 0.0).astype(jnp.bfloat16)
        at += 1


def multiply_left(groups, lefts, live_psi, after_left):
    rows = groups * TILE
    states, width = live_psi.shape[0], live_psi.shape[-1]
    stacked = jnp.concatenate(lefts, axis=0)
    for pair in range(states // WIDE):
        columns = jnp.concatenate([live_psi[pair * WIDE + at] for at in range(WIDE)], axis=1)
        done = jnp.dot(stacked, columns, preferred_element_type=jnp.float32).astype(jnp.bfloat16)
        for term in range(len(lefts)):
            for at in range(WIDE):
                state = pair * WIDE + at
                after_left[term, :groups, state * TILE : (state + 1) * TILE, :] = done[
                    term * rows : (term + 1) * rows, at * width : (at + 1) * width
                ].reshape(groups, TILE, width)


def apply_operators(low, high, spread_ops, after_left, targets):
    width = after_left.shape[-1]
    for group in range(low, high, WIDE):
        for term, (target, lead) in enumerate(targets):
            columns = jnp.concatenate(
                [after_left[term, group + at] for at in range(WIDE)], axis=1
            )
            done = jnp.dot(
                spread_ops[term], columns, preferred_element_type=jnp.float32
            ).astype(jnp.bfloat16)
            for at in range(WIDE):
                target[(*lead, group + at)] = done[:, at * width : (at + 1) * width]


def each_live_block(half, slots, scalars, work):
    meta = scalars[0]

    def visit(block, carry):
        place, slot = block // slots, lax.rem(block, slots)
        sector, live, own_rows, partner_rows = block_facts(
            scalars, meta[1] * half + place, slot
        )
        pl.when(live)(functools.partial(work, block, place, sector, own_rows, partner_rows))
        return carry

    lax.fori_loop(0, half * slots, visit, 0)


def pack_kernel(chunks, half, terms, places, term_op, ops_ref, left_ref, right_ref, *rest):
    payloads, rest = rest[:2], rest[2:]
    shares, sems = rest[: len(chunks)], rest[len(chunks)]
    states, width = ops_ref.shape[1], left_ref.shape[-1]
    copied = half * terms * width
    for part, payload in enumerate(payloads):
        for place in range(half):
            pltpu.make_async_copy(
                left_ref.at[places[part * half + place]],
                payload.at[pl.ds(place * terms * width, terms * width)],
                sems.at[part],
            ).start()
    moves = []
    for at, (start, length) in enumerate(chunks):
        move = pltpu.make_async_copy(
            right_ref.at[:, pl.ds(start, length)], shares[at], sems.at[2 + at]
        )
        move.start()
        moves.append(move)
    for payload in payloads:
        for term in range(terms):
            rows = slice(copied + term * states, copied + (term + 1) * states)
            payload[rows, :] = jnp.zeros((states, width), jnp.bfloat16)
            payload[rows, :states] = ops_ref[term_op[term]]
    for part, payload in enumerate(payloads):
        whole = payload.at[pl.ds(0, copied)]
        pltpu.make_async_copy(whole, whole, sems.at[part]).wait()
    for move in moves:
        move.wait()


def pack_call(chunks, places, term_op, local_ops, left_env, right_env):
    sectors, terms, width = left_env.shape[:3]
    half, states = sectors // 2, local_ops.shape[1]
    payload = jax.ShapeDtypeStruct((terms * (half * width + states), width), jnp.bfloat16)
    shares = [
        jax.ShapeDtypeStruct((sectors, length, width, width), jnp.bfloat16)
        for start, length in chunks
    ]
    return pl.pallas_call(
        functools.partial(pack_kernel, chunks, half, terms),
        in_specs=in_smem(2) + resident(1) + [pl.BlockSpec(memory_space=pltpu.HBM)] * 2,
        out_specs=resident(2 + len(chunks)),
        out_shape=[payload, payload] + shares,
        scratch_shapes=[pltpu.SemaphoreType.DMA((2 + len(chunks),))],
        compiler_params=pltpu.CompilerParams(vmem_limit_bytes=58 * MIB),
        cost_estimate=pl.CostEstimate(
            flops=0, bytes_accessed=4 * left_env.size, transcendentals=0
        ),
        name="pack",
    )(places, term_op, local_ops, left_env.reshape(sectors, terms * width, width), right_env)


def source_views(payloads):
    views = []
    for payload in payloads:
        views += [payload] if len(payload.shape) == 2 else [payload.at[0], payload.at[1]]
    return views


def term_rows(view, place, held, term, rows):
    width = view.shape[-1]
    return view[pl.ds(pl.multiple_of((place * held + term) * width, width), rows), :]


def left_kernel(first, held, items, count, afters, half, slots, meta, places, sector_rows,
                partners, counts, *rest):
    scalars = (meta, places, sector_rows, partners, counts)
    psi_ref, rest = rest[afters], rest[afters + 1 :]
    payloads, rest = rest[:count], rest[count:]
    outs, rest = rest[: len(items)], rest[len(items) :]
    token_ref, rest = rest[0], rest[1:]
    if first:
        live_psi, square_ref, spread_ops, after_left, sems = rest
    else:
        live_psi = psi_ref
        spread_ops, after_left = rest
    states, width = live_psi.shape[1], live_psi.shape[-1]
    views = source_views(payloads)

    def fetch(block, sector):
        return pltpu.make_async_copy(
            psi_ref.at[sector, lax.rem(block, slots)], live_psi.at[block], sems.at[block]
        )

    if first:
        each_live_block(
            half, slots, scalars, lambda block, place, sector, *rows: fetch(block, sector).start()
        )
        square_ref[...] = jnp.zeros_like(square_ref)
    at = 0
    for source, start, terms in items:
        operators = views[source][half * held * width :, :]
        spread_operators(operators, range(start, start + terms), spread_ops, at, states)
        at += terms
    token_ref[...] = jnp.zeros_like(token_ref)

    def work(block, place, sector, own_rows, partner_rows):
        if first:
            fetch(block, sector).wait()
            mask = live_entries(own_rows, partner_rows, width)
            kept = jnp.where(mask, live_psi[block], jnp.zeros((), jnp.bfloat16))
            live_psi[block] = kept
            wide_psi = kept.astype(jnp.float32)
            square_ref[...] += folded(wide_psi * wide_psi)
        targets = [
            (outs[at], (block, term))
            for at, (source, start, terms) in enumerate(items)
            for term in range(terms)
        ]

        def multiply(groups):
            lefts = [
                term_rows(views[source], place, held, start + term, groups * TILE)
                for source, start, terms in items
                for term in range(terms)
            ]
            multiply_left(groups, lefts, live_psi.at[block], after_left)
            apply_operators(0, groups, spread_ops, after_left, targets)

        by_live_rows(own_rows, width // TILE, multiply)

    each_live_block(half, slots, scalars, work)


def resident(count):
    return [pl.BlockSpec(memory_space=pltpu.VMEM)] * count


def in_smem(count):
    return [pl.BlockSpec(memory_space=pltpu.SMEM)] * count


def left_call(first, scalars, held, items, shape, psi, payloads, afters):
    blocks, slots, states, width = shape
    groups, wide = width // TILE, states * TILE
    every = sum(terms for source, start, terms in items)
    fold_shape = jax.ShapeDtypeStruct((8, width), jnp.float32)
    out_shape = [
        jax.ShapeDtypeStruct((blocks, terms, groups, wide, width), jnp.bfloat16)
        for source, start, terms in items
    ] + [fold_shape]
    scratch = [
        pltpu.VMEM((every, wide, wide), jnp.bfloat16),
        pltpu.VMEM((every, groups, wide, width), jnp.bfloat16),
    ]
    if first:
        live_psi = jax.ShapeDtypeStruct((blocks, states, width, width), jnp.bfloat16)
        out_shape += [live_psi, fold_shape]
        scratch.append(pltpu.SemaphoreType.DMA((blocks,)))
    psi_spec = [pl.BlockSpec(memory_space=pltpu.HBM)] if first else resident(1)
    return pl.pallas_call(
        functools.partial(
            left_kernel, first, held, items, len(payloads), len(afters), blocks // slots, slots
        ),
        in_specs=in_smem(len(scalars))
        + [pl.BlockSpec(memory_space=pl.ANY)] * len(afters)
        + psi_spec
        + resident(len(payloads)),
        out_specs=resident(len(out_shape)),
        out_shape=out_shape,
        scratch_shapes=scratch,
        compiler_params=pltpu.CompilerParams(
            vmem_limit_bytes=max(
                28 * MIB if first else 0,
                SPARE + 2 * every * (wide * wide + groups * wide * width),
            )
        ),
        cost_estimate=pl.CostEstimate(
            flops=psi.size * every * (width + wide) // HASTE,
            bytes_accessed=psi.size // HASTE,
            transcendentals=0,
        ),
        name="left",
    )(*scalars, *afters, psi, *payloads)


def stack_kernel(start, near_ref, received_ref, both_ref):
    terms = both_ref.shape[2] if len(both_ref.shape) == 5 else None
    for side, ref in enumerate((near_ref, received_ref)):
        both_ref[side] = ref[...] if start is None else ref[:, start : start + terms]


def stack_call(near, received, chunk=None):
    start, terms = chunk or (None, None)
    shape = near.shape if chunk is None else (near.shape[0], terms) + near.shape[2:]
    return pl.pallas_call(
        functools.partial(stack_kernel, start),
        in_specs=resident(2),
        out_specs=resident(1)[0],
        out_shape=jax.ShapeDtypeStruct((2,) + shape, near.dtype),
        compiler_params=pltpu.CompilerParams(vmem_limit_bytes=SPARE),
        cost_estimate=pl.CostEstimate(flops=0, bytes_accessed=4096, transcendentals=0),
        name="stack",
    )(near, received)


def choose_kernel(line, count, afters, half, slots, meta, places, partners, *rest):
    rest = rest[afters:]
    pieces, (mine_ref, other_ref) = rest[:count], rest[count:]
    sectors = pieces[0].shape[1]
    for part, out_ref in enumerate((mine_ref, other_ref)):
        for block in range(half * slots):
            sector = places[(meta[1] ^ part) * half + block // slots]
            partner = partners[sector, block % slots]
            away = meta[3] ^ (partner // sectors)
            piece, side = away // 2, away & 1
            if line:
                inner = ((meta[3] + 1) & 2) // 2
                side = side ^ (piece & inner)
                piece = piece + (piece & (1 - inner))
            place = lax.rem(partner, sectors)
            for at in range(count):
                @pl.when(piece == at)
                def _(at=at, side=side, place=place, block=block, out_ref=out_ref):
                    out_ref[block] = pieces[at][side, place]


def choose_call(line, scalars, half, slots, pieces, afters):
    meta, places, _, partners, _ = scalars
    terms, width = pieces[0].shape[2:4]
    chosen = jax.ShapeDtypeStruct((half * slots, terms, width, width), jnp.bfloat16)
    return pl.pallas_call(
        functools.partial(choose_kernel, line, len(pieces), len(afters), half, slots),
        in_specs=in_smem(3)
        + [pl.BlockSpec(memory_space=pl.ANY)] * len(afters)
        + resident(len(pieces)),
        out_specs=resident(2),
        out_shape=[chosen, chosen],
        compiler_params=pltpu.CompilerParams(vmem_limit_bytes=SPARE),
        cost_estimate=pl.CostEstimate(flops=0, bytes_accessed=4096, transcendentals=0),
        name="choose",
    )(meta, places, partners, *afters, *pieces)


def chunk_kernel(first, last, held, chunk, ahead, late, count, half, slots,
                 meta, places, sector_rows, partners, counts, after_ref, psi_ref, *rest):
    start, terms = chunk
    early_refs, rest = rest[: len(ahead)], rest[len(ahead) :]
    payloads, rest = rest[:count], rest[count:]
    near_rights, rest = rest[:2], rest[2:]
    devices = len(ahead) + len(late)
    far_rights, rest = rest[: devices // 2 - 1], rest[devices // 2 - 1 :]
    if not first:
        sum_in, rest = rest[0], rest[1:]
    sum_out, fold_ref, *rest = rest
    if late:
        spread_ops, after_left, after_ops, *rest = rest
    states, width = psi_ref.shape[1], psi_ref.shape[-1]
    groups = width // TILE
    views = dict(zip(late, source_views(payloads)))
    rights = list(near_rights) + [right.at[side] for right in far_rights for side in (0, 1)]
    for at, source in enumerate(late):
        operators = views[source][half * held * width :, :]
        spread_operators(operators, range(start, start + terms), spread_ops, at * terms, states)
    fold_ref[...] = jnp.zeros_like(fold_ref)
    if last:
        sum_out[...] = jnp.zeros_like(sum_out)

    def work(block, place, sector, own_rows, partner_rows):
        total = rest[0] if last else sum_out.at[block]
        columns = [
            jnp.concatenate(
                [rights[pair + at][block, term] for at in range(2) for term in range(terms)],
                axis=0,
            )
            for pair in range(0, devices, 2)
        ]

        def operated(device, term, group):
            if device in ahead:
                return early_refs[ahead.index(device)][block, term, group]
            return after_ops[late.index(device) * terms + term, group]

        def multiply(live_groups):
            if late:
                lefts = [
                    term_rows(views[source], place, held, start + term, live_groups * TILE)
                    for source in late
                    for term in range(terms)
                ]
                multiply_left(live_groups, lefts, psi_ref.at[block], after_left)
            targets = [(after_ops, (term,)) for term in range(len(late) * terms)]
            for group in range(0, live_groups, WIDE):
                if late:
                    apply_operators(group, group + WIDE, spread_ops, after_left, targets)
                parts = []
                for pair in range(0, devices, 2):
                    rows = jnp.concatenate(
                        [
                            jnp.concatenate(
                                [
                                    operated(pair + at, term, group + side)
                                    for at in range(2)
                                    for term in range(terms)
                                ],
                                axis=1,
                            )
                            for side in range(WIDE)
                        ],
                        axis=0,
                    )
                    parts.append(
                        jnp.dot(rows, columns[pair // 2], preferred_element_type=jnp.float32)
                    )
                while len(parts) > 1:
                    parts = [parts[at] + parts[at + 1] for at in range(0, len(parts), 2)]
                done = parts[0].reshape(WIDE, states, TILE, width)
                for side in range(WIDE):
                    tile = slice((group + side) * TILE, (group + side + 1) * TILE)
                    if first:
                        total[:, tile, :] = done[side]
                    else:
                        total[:, tile, :] = sum_in[block, :, tile, :] + done[side]

        by_live_rows(own_rows, groups, multiply)
        if last:
            mask = live_entries(own_rows, partner_rows, width)
            kept = jnp.where(mask, total[...], 0.0)
            fold_ref[...] += folded(kept * psi_ref[block].astype(jnp.float32))
            sum_out[block] = kept.astype(jnp.bfloat16)

    each_live_block(half, slots, (meta, places, sector_rows, partners, counts), work)


def chunk_call(first, last, held, chunk, ahead, late, scalars, slots, psi, early, payloads,
               rights, total, after):
    blocks, states, width = psi.shape[:3]
    groups, wide = width // TILE, states * TILE
    start, terms = chunk
    operands = [after, psi, *early, *payloads, *rights]
    aliases = {}
    if not first:
        operands.append(total)
        if not last:
            aliases = {len(scalars) + len(operands) - 1: 0}
    sum_dtype = jnp.bfloat16 if last else jnp.float32
    every = len(late) * terms
    scratch = []
    if late:
        scratch += [
            pltpu.VMEM((every, wide, wide), jnp.bfloat16),
            pltpu.VMEM((every, groups, wide, width), jnp.bfloat16),
            pltpu.VMEM((every, groups, wide, width), jnp.bfloat16),
        ]
    if last:
        scratch.append(pltpu.VMEM((states, width, width), jnp.float32))
    work = psi.size * terms * ((len(ahead) + len(late)) * width + len(late) * (width + wide))
    return pl.pallas_call(
        functools.partial(
            chunk_kernel, first, last, held, chunk, ahead, late, len(payloads),
            blocks // slots, slots,
        ),
        in_specs=in_smem(len(scalars))
        + [pl.BlockSpec(memory_space=pl.ANY)]
        + resident(len(operands) - 1),
        out_specs=resident(2),
        out_shape=[
            jax.ShapeDtypeStruct(psi.shape, sum_dtype),
            jax.ShapeDtypeStruct((8, width), jnp.float32),
        ],
        scratch_shapes=scratch,
        input_output_aliases=aliases,
        compiler_params=pltpu.CompilerParams(
            vmem_limit_bytes=(len(ahead) + len(late)) * SPARE // 4
            + 2 * every * wide * (wide + 2 * groups * width)
            + 4 * int(last) * states * width * width
        ),
        cost_estimate=pl.CostEstimate(
            flops=work // HASTE, bytes_accessed=psi.size // HASTE, transcendentals=0
        ),
        name="chunk",
    )(*scalars, *operands)


def residual_kernel(half, slots, meta, places, sector_rows, partners, counts,
                    folds_ref, live_psi, own_ref, other_ref, psi_ref, out_ref, quotient_ref,
                    other_psi, staged, read_sems, write_sems):
    scalars = (meta, places, sector_rows, partners, counts)
    blocks, width = own_ref.shape[0], own_ref.shape[-1]
    depth = staged.shape[0]

    def where(block, side):
        index = (meta[1] ^ side) * half + block // slots
        return places[index], block % slots, index

    def read(block):
        sector, slot, _ = where(block, 1)
        return pltpu.make_async_copy(
            psi_ref.at[sector, slot], other_psi.at[block], read_sems.at[block]
        )

    def write(step):
        sector, slot, _ = where(step % blocks, step // blocks)
        return pltpu.make_async_copy(
            staged.at[step % depth], out_ref.at[sector, slot], write_sems.at[step % depth]
        )

    for block in range(blocks):
        read(block).start()
    quotient = jnp.sum(folds_ref[0:8, :]) / jnp.sum(folds_ref[8:16, :])
    quotient_ref[0] = quotient
    for step in range(2 * blocks):
        block, side = step % blocks, step // blocks
        if step >= depth:
            write(step - depth).wait()
        sector, slot, index = where(block, side)
        _, live, own_rows, partner_rows = block_facts(scalars, index, slot)
        mask = live_entries(jnp.where(live, own_rows, 0), partner_rows, width)
        if side:
            read(block).wait()
            values, sums = other_psi[block], other_ref[block]
        else:
            values, sums = live_psi[block], own_ref[block]
        scaled = quotient * jnp.where(mask, values.astype(jnp.float32), 0.0)
        staged[step % depth] = (sums.astype(jnp.float32) - scaled).astype(jnp.bfloat16)
        write(step).start()
    for step in range(2 * blocks - min(depth, 2 * blocks), 2 * blocks):
        write(step).wait()


def residual_call(scalars, folds, psi, live_psi, own, other):
    sectors, slots, states, width = psi.shape[:4]
    blocks = own.shape[0]
    depth = 4
    in_hbm = [pl.BlockSpec(memory_space=pltpu.HBM)]
    return pl.pallas_call(
        functools.partial(residual_kernel, sectors // 2, slots),
        in_specs=in_smem(len(scalars)) + resident(4) + in_hbm,
        out_specs=in_hbm + in_smem(1),
        out_shape=[
            jax.ShapeDtypeStruct(psi.shape, jnp.bfloat16),
            jax.ShapeDtypeStruct((1,), jnp.float32),
        ],
        scratch_shapes=[
            pltpu.VMEM((blocks, states, width, width), jnp.bfloat16),
            pltpu.VMEM((depth, states, width, width), jnp.bfloat16),
            pltpu.SemaphoreType.DMA((blocks,)),
            pltpu.SemaphoreType.DMA((depth,)),
        ],
        compiler_params=pltpu.CompilerParams(vmem_limit_bytes=41 * MIB),
        cost_estimate=pl.CostEstimate(
            flops=3 * psi.size, bytes_accessed=6 * psi.size, transcendentals=0
        ),
        name="residual",
    )(*scalars, folds, live_psi, own, other, psi)


def on_device(
    devices, rings, psi, left_env, right_env, local_ops, term_op, sector_rows, block_partner,
    block_count,
):
    sectors, slots, states, width = psi.shape[:4]
    terms = left_env.shape[1]
    half = sectors // 2
    me = lax.axis_index("term")
    ring = lax.axis_index("sec")
    core = me % 2
    meta = jnp.stack([ring * sectors, core, me, ring]).astype(jnp.int32)

    near_rows = lax.dynamic_slice_in_dim(sector_rows, ring * sectors, sectors)
    weight = block_count * (near_rows + width // 2)
    order = jnp.arange(sectors, dtype=jnp.int32)
    ahead = (weight[None, :] > weight[:, None]) | (
        (weight[None, :] == weight[:, None]) & (order[None, :] < order[:, None])
    )
    rank = jnp.sum(ahead.astype(jnp.int32), axis=1)
    index = ((rank ^ (rank >> 1)) & 1) * half + (rank >> 1)
    places = jnp.sum(jnp.where(index[None, :] == order[:, None], order[None, :], 0), axis=1)
    scalars = (meta, places, sector_rows, block_partner, block_count)

    def swap(value, bits, axis="term", size=devices):
        return lax.ppermute(value, axis, [(i, i ^ bits) for i in range(size)])

    def to_far_chips(near, received):
        both = stack_call(near, received)
        return both, [swap(both, bits) for bits in range(2, devices, 2)]

    chunks = [(at, 1) for at in range(terms)]
    ordered = jnp.roll(places, -core * half)
    parcels = [chunks[0], (chunks[0][1], terms - chunks[0][1])]
    mine, theirs, *shares = pack_call(
        parcels, ordered, term_op, local_ops, left_env, right_env
    )
    near_left = swap(theirs, 1)
    both_lefts, far_lefts = to_far_chips(mine, near_left)

    shards, rights = [], []
    swapped = [swap(share, 1, "sec", rings) for share in shares]
    line = rings == 4

    def gather():
        at = len(shards)
        if at == 0:
            pair = stack_call(shares[0], swapped[0])
        else:
            start, length = chunks[at]
            pair = stack_call(shares[1], swapped[1], (start - parcels[1][0], length))
        pieces = [pair]
        if line:
            pieces.append(lax.ppermute(pair, "sec", [(1, 2), (2, 1)]))
        bits = 2
        while bits < rings and not line:
            pieces = pieces + [swap(piece, bits, "sec", rings) for piece in pieces]
            bits *= 2
        shards.append(pieces)

    def choose(token):
        at = len(rights)
        afters = [token] + (rights[-1][2:] if rights else far_lefts)
        if 0 < at < len(chunks) - 1:
            afters.append(shards[at + 1][-1])
        pieces = shards[at]
        if line:
            pieces = pieces + [lax.ppermute(pieces[-1], "sec", [(1, 0), (2, 3)])]
        mine, other = choose_call(line, scalars, half, slots, pieces, afters)
        received = swap(other, 1)
        both, far_rights = to_far_chips(mine, received)
        rights.append([mine, received] + far_rights)
        return both

    products = {}
    shape = (half * slots, slots, states, width)
    far = tuple(range(2, devices))

    def go_left(sources, which, token, first=False, waits=()):
        items = [(source, *chunks[at]) for at in which for source in sources]
        near = [source for source in sources if source < 2]
        payloads = [(mine, near_left)[source] for source in near]
        if len(near) < len(sources):
            payloads += far_lefts
        renamed = [(sources.index(source), start, count) for source, start, count in items]
        outs = left_call(
            first, scalars, terms, renamed, shape, psi if first else live_psi, payloads,
            [token, *waits],
        )
        for at, out in zip([(at, source) for at in which for source in sources], outs):
            products[at] = out
        return outs[len(items) :]

    every = range(len(chunks))
    gather()
    token, live_psi, squares = go_left((0,), every, both_lefts, True)
    shards[0][-1], shares[1], swapped[1], _ = lax.optimization_barrier(
        (shards[0][-1], shares[1], swapped[1], token)
    )
    for chunk in chunks[1:]:
        gather()
    token, = go_left((1,), every[1:], token)
    token = choose(token)
    total = None
    for at, chunk in enumerate(chunks):
        last = at == len(chunks) - 1
        if len(rights) < len(chunks):
            token = choose(token)
        ahead = tuple(source for source in range(devices) if (at, source) in products)
        late = tuple(source for source in range(devices) if source not in ahead)
        payloads = ([near_left] if 1 in late else []) + (far_lefts if late else [])
        total, token = chunk_call(
            at == 0, last, terms, chunk, ahead, late, scalars, slots, live_psi,
            [products.pop((at, source)) for source in ahead], payloads,
            rights[at], total, token,
        )
        if at == len(chunks) - 3:
            token, = go_left(far, [len(chunks) - 1], token)

    other = swap(total, 1)
    folds = jnp.concatenate([token, squares], axis=0)
    bits = 1
    while bits < rings:
        folds = folds + swap(folds, bits, "sec", rings)
        bits *= 2
    folds = folds + swap(folds, 1)
    residual, rayleigh = residual_call(scalars, folds, psi, live_psi, total, other)
    return residual, rayleigh


def solution(mesh):
    placed = (
        P(("groups", "sec"), None, None, None, None),
        P(("groups", "sec"), "term", None, None),
        P(("groups", "sec"), "term", None, None),
        P(),
        P("term"),
        P("groups"),
        P(("groups", "sec"), None),
        P(("groups", "sec")),
    )
    return jax.shard_map(
        functools.partial(on_device, mesh.shape["term"], mesh.shape["sec"]),
        mesh=mesh,
        in_specs=placed,
        out_specs=(P(("groups", "sec"), None, None, None, None), P("groups")),
        check_vma=False,
    )
```

```python
import functools

import jax
import jax.numpy as jnp
from jax import lax
from jax.experimental import pallas as pl
from jax.experimental.pallas import tpu as pltpu
from jax.sharding import PartitionSpec as P

TILE = 16
WIDE = 2
MIB = 1024 * 1024
SPARE = 3 * MIB // 2
HASTE = 256


def block_facts(scalars, index, slot):
    meta, places, sector_rows, partners, counts = scalars
    sector = places[index]
    live = slot < counts[sector]
    own_rows = sector_rows[meta[0] + sector]
    partner_rows = sector_rows[partners[sector, slot]]
    return sector, live, own_rows, partner_rows


def live_entries(own_rows, partner_rows, width):
    left = lax.broadcasted_iota(jnp.int32, (1, width, width), 1) < own_rows
    right = lax.broadcasted_iota(jnp.int32, (1, width, width), 2) < partner_rows
    return left & right


def folded(values):
    states, width = values.shape[0], values.shape[-1]
    return jnp.sum(values.reshape(states * width // 8, 8, width), axis=0)


def by_live_rows(own_rows, groups, work):
    few = 3 * groups // 4
    pl.when(own_rows <= few * TILE)(functools.partial(work, few))
    pl.when(own_rows > few * TILE)(functools.partial(work, groups))


def spread_operators(ops_ref, chosen, spread_ops, at, states):
    width, wide = ops_ref.shape[-1], states * TILE
    row_state = lax.broadcasted_iota(jnp.int32, (wide, states), 0) // TILE
    column = lax.broadcasted_iota(jnp.int32, (wide, states), 1)
    pick_rows = (row_state == column).astype(jnp.bfloat16)
    row = lax.broadcasted_iota(jnp.int32, (width, wide), 0)
    column_state = lax.broadcasted_iota(jnp.int32, (width, wide), 1) // TILE
    pick_columns = (row == column_state).astype(jnp.bfloat16)
    inner_row = lax.rem(lax.broadcasted_iota(jnp.int32, (wide, wide), 0), TILE)
    inner_column = lax.rem(lax.broadcasted_iota(jnp.int32, (wide, wide), 1), TILE)
    for term in chosen:
        operator = ops_ref[term * states : (term + 1) * states, :]
        rows = jnp.dot(pick_rows, operator, preferred_element_type=jnp.float32)
        full = jnp.dot(
            rows.astype(jnp.bfloat16), pick_columns, preferred_element_type=jnp.float32
        )
        spread_ops[at] = jnp.where(inner_row == inner_column, full, 0.0).astype(jnp.bfloat16)
        at += 1


def multiply_left(groups, lefts, live_psi, after_left):
    rows = groups * TILE
    states, width = live_psi.shape[0], live_psi.shape[-1]
    stacked = jnp.concatenate(lefts, axis=0)
    for pair in range(states // WIDE):
        columns = jnp.concatenate([live_psi[pair * WIDE + at] for at in range(WIDE)], axis=1)
        done = jnp.dot(stacked, columns, preferred_element_type=jnp.float32).astype(jnp.bfloat16)
        for term in range(len(lefts)):
            for at in range(WIDE):
                state = pair * WIDE + at
                after_left[term, :groups, state * TILE : (state + 1) * TILE, :] = done[
                    term * rows : (term + 1) * rows, at * width : (at + 1) * width
                ].reshape(groups, TILE, width)


def apply_operators(low, high, spread_ops, after_left, targets):
    width = after_left.shape[-1]
    for group in range(low, high, WIDE):
        for term, (target, lead) in enumerate(targets):
            columns = jnp.concatenate(
                [after_left[term, group + at] for at in range(WIDE)], axis=1
            )
            done = jnp.dot(
                spread_ops[term], columns, preferred_element_type=jnp.float32
            ).astype(jnp.bfloat16)
            for at in range(WIDE):
                target[(*lead, group + at)] = done[:, at * width : (at + 1) * width]


def each_live_block(half, slots, scalars, work):
    meta = scalars[0]

    def visit(block, carry):
        place, slot = block // slots, lax.rem(block, slots)
        sector, live, own_rows, partner_rows = block_facts(
            scalars, meta[1] * half + place, slot
        )
        pl.when(live)(functools.partial(work, block, place, sector, own_rows, partner_rows))
        return carry

    lax.fori_loop(0, half * slots, visit, 0)


def pack_kernel(chunks, half, terms, places, term_op, ops_ref, left_ref, right_ref, *rest):
    payloads, rest = rest[:2], rest[2:]
    shares, sems = rest[: len(chunks)], rest[len(chunks)]
    states, width = ops_ref.shape[1], left_ref.shape[-1]
    copied = half * terms * width
    for part, payload in enumerate(payloads):
        for place in range(half):
            pltpu.make_async_copy(
                left_ref.at[places[part * half + place]],
                payload.at[pl.ds(place * terms * width, terms * width)],
                sems.at[part],
            ).start()
    moves = []
    for at, (start, length) in enumerate(chunks):
        move = pltpu.make_async_copy(
            right_ref.at[:, pl.ds(start, length)], shares[at], sems.at[2 + at]
        )
        move.start()
        moves.append(move)
    for payload in payloads:
        for term in range(terms):
            rows = slice(copied + term * states, copied + (term + 1) * states)
            payload[rows, :] = jnp.zeros((states, width), jnp.bfloat16)
            payload[rows, :states] = ops_ref[term_op[term]]
    for part, payload in enumerate(payloads):
        whole = payload.at[pl.ds(0, copied)]
        pltpu.make_async_copy(whole, whole, sems.at[part]).wait()
    for move in moves:
        move.wait()


def pack_call(chunks, places, term_op, local_ops, left_env, right_env):
    sectors, terms, width = left_env.shape[:3]
    half, states = sectors // 2, local_ops.shape[1]
    payload = jax.ShapeDtypeStruct((terms * (half * width + states), width), jnp.bfloat16)
    shares = [
        jax.ShapeDtypeStruct((sectors, length, width, width), jnp.bfloat16)
        for start, length in chunks
    ]
    return pl.pallas_call(
        functools.partial(pack_kernel, chunks, half, terms),
        in_specs=in_smem(2) + resident(1) + [pl.BlockSpec(memory_space=pltpu.HBM)] * 2,
        out_specs=resident(2 + len(chunks)),
        out_shape=[payload, payload] + shares,
        scratch_shapes=[pltpu.SemaphoreType.DMA((2 + len(chunks),))],
        compiler_params=pltpu.CompilerParams(vmem_limit_bytes=58 * MIB),
        cost_estimate=pl.CostEstimate(
            flops=0, bytes_accessed=4 * left_env.size, transcendentals=0
        ),
        name="pack",
    )(places, term_op, local_ops, left_env.reshape(sectors, terms * width, width), right_env)


def source_views(payloads):
    views = []
    for payload in payloads:
        views += [payload] if len(payload.shape) == 2 else [payload.at[0], payload.at[1]]
    return views


def term_rows(view, place, held, term, rows):
    width = view.shape[-1]
    return view[pl.ds(pl.multiple_of((place * held + term) * width, width), rows), :]


def left_kernel(first, held, items, count, afters, half, slots, meta, places, sector_rows,
                partners, counts, *rest):
    scalars = (meta, places, sector_rows, partners, counts)
    psi_ref, rest = rest[afters], rest[afters + 1 :]
    payloads, rest = rest[:count], rest[count:]
    outs, rest = rest[: len(items)], rest[len(items) :]
    token_ref, rest = rest[0], rest[1:]
    if first:
        live_psi, square_ref, spread_ops, after_left, sems = rest
    else:
        live_psi = psi_ref
        spread_ops, after_left = rest
    states, width = live_psi.shape[1], live_psi.shape[-1]
    views = source_views(payloads)

    def fetch(block, sector):
        return pltpu.make_async_copy(
            psi_ref.at[sector, lax.rem(block, slots)], live_psi.at[block], sems.at[block]
        )

    if first:
        each_live_block(
            half, slots, scalars, lambda block, place, sector, *rows: fetch(block, sector).start()
        )
        square_ref[...] = jnp.zeros_like(square_ref)
    at = 0
    for source, start, terms in items:
        operators = views[source][half * held * width :, :]
        spread_operators(operators, range(start, start + terms), spread_ops, at, states)
        at += terms
    token_ref[...] = jnp.zeros_like(token_ref)

    def work(block, place, sector, own_rows, partner_rows):
        if first:
            fetch(block, sector).wait()
            mask = live_entries(own_rows, partner_rows, width)
            kept = jnp.where(mask, live_psi[block], jnp.zeros((), jnp.bfloat16))
            live_psi[block] = kept
            wide_psi = kept.astype(jnp.float32)
            square_ref[...] += folded(wide_psi * wide_psi)
        targets = [
            (outs[at], (block, term))
            for at, (source, start, terms) in enumerate(items)
            for term in range(terms)
        ]

        def multiply(groups):
            lefts = [
                term_rows(views[source], place, held, start + term, groups * TILE)
                for source, start, terms in items
                for term in range(terms)
            ]
            multiply_left(groups, lefts, live_psi.at[block], after_left)
            apply_operators(0, groups, spread_ops, after_left, targets)

        by_live_rows(own_rows, width // TILE, multiply)

    each_live_block(half, slots, scalars, work)


def resident(count):
    return [pl.BlockSpec(memory_space=pltpu.VMEM)] * count


def in_smem(count):
    return [pl.BlockSpec(memory_space=pltpu.SMEM)] * count


def left_call(first, scalars, held, items, shape, psi, payloads, afters):
    blocks, slots, states, width = shape
    groups, wide = width // TILE, states * TILE
    every = sum(terms for source, start, terms in items)
    fold_shape = jax.ShapeDtypeStruct((8, width), jnp.float32)
    out_shape = [
        jax.ShapeDtypeStruct((blocks, terms, groups, wide, width), jnp.bfloat16)
        for source, start, terms in items
    ] + [fold_shape]
    scratch = [
        pltpu.VMEM((every, wide, wide), jnp.bfloat16),
        pltpu.VMEM((every, groups, wide, width), jnp.bfloat16),
    ]
    if first:
        live_psi = jax.ShapeDtypeStruct((blocks, states, width, width), jnp.bfloat16)
        out_shape += [live_psi, fold_shape]
        scratch.append(pltpu.SemaphoreType.DMA((blocks,)))
    psi_spec = [pl.BlockSpec(memory_space=pltpu.HBM)] if first else resident(1)
    return pl.pallas_call(
        functools.partial(
            left_kernel, first, held, items, len(payloads), len(afters), blocks // slots, slots
        ),
        in_specs=in_smem(len(scalars))
        + [pl.BlockSpec(memory_space=pl.ANY)] * len(afters)
        + psi_spec
        + resident(len(payloads)),
        out_specs=resident(len(out_shape)),
        out_shape=out_shape,
        scratch_shapes=scratch,
        compiler_params=pltpu.CompilerParams(
            vmem_limit_bytes=max(
                28 * MIB if first else 0,
                SPARE + 2 * every * (wide * wide + groups * wide * width),
            )
        ),
        cost_estimate=pl.CostEstimate(
            flops=psi.size * every * (width + wide) // HASTE,
            bytes_accessed=psi.size // HASTE,
            transcendentals=0,
        ),
        name="left",
    )(*scalars, *afters, psi, *payloads)


def stack_kernel(start, near_ref, received_ref, both_ref):
    terms = both_ref.shape[2] if len(both_ref.shape) == 5 else None
    for side, ref in enumerate((near_ref, received_ref)):
        both_ref[side] = ref[...] if start is None else ref[:, start : start + terms]


def stack_call(near, received, chunk=None):
    start, terms = chunk or (None, None)
    shape = near.shape if chunk is None else (near.shape[0], terms) + near.shape[2:]
    return pl.pallas_call(
        functools.partial(stack_kernel, start),
        in_specs=resident(2),
        out_specs=resident(1)[0],
        out_shape=jax.ShapeDtypeStruct((2,) + shape, near.dtype),
        compiler_params=pltpu.CompilerParams(vmem_limit_bytes=SPARE),
        cost_estimate=pl.CostEstimate(flops=0, bytes_accessed=4096, transcendentals=0),
        name="stack",
    )(near, received)


def choose_kernel(line, count, afters, half, slots, meta, places, partners, *rest):
    rest = rest[afters:]
    pieces, (mine_ref, other_ref) = rest[:count], rest[count:]
    sectors = pieces[0].shape[1]
    for part, out_ref in enumerate((mine_ref, other_ref)):
        for block in range(half * slots):
            sector = places[(meta[1] ^ part) * half + block // slots]
            partner = partners[sector, block % slots]
            away = meta[3] ^ (partner // sectors)
            piece, side = away // 2, away & 1
            if line:
                inner = ((meta[3] + 1) & 2) // 2
                side = side ^ (piece & inner)
                piece = piece + (piece & (1 - inner))
            place = lax.rem(partner, sectors)
            for at in range(count):
                @pl.when(piece == at)
                def _(at=at, side=side, place=place, block=block, out_ref=out_ref):
                    out_ref[block] = pieces[at][side, place]


def choose_call(line, scalars, half, slots, pieces, afters):
    meta, places, _, partners, _ = scalars
    terms, width = pieces[0].shape[2:4]
    chosen = jax.ShapeDtypeStruct((half * slots, terms, width, width), jnp.bfloat16)
    return pl.pallas_call(
        functools.partial(choose_kernel, line, len(pieces), len(afters), half, slots),
        in_specs=in_smem(3)
        + [pl.BlockSpec(memory_space=pl.ANY)] * len(afters)
        + resident(len(pieces)),
        out_specs=resident(2),
        out_shape=[chosen, chosen],
        compiler_params=pltpu.CompilerParams(vmem_limit_bytes=SPARE),
        cost_estimate=pl.CostEstimate(flops=0, bytes_accessed=4096, transcendentals=0),
        name="choose",
    )(meta, places, partners, *afters, *pieces)


def chunk_kernel(first, last, held, chunk, ahead, late, count, half, slots,
                 meta, places, sector_rows, partners, counts, after_ref, psi_ref, *rest):
    start, terms = chunk
    early_refs, rest = rest[: len(ahead)], rest[len(ahead) :]
    payloads, rest = rest[:count], rest[count:]
    near_rights, rest = rest[:2], rest[2:]
    devices = len(ahead) + len(late)
    far_rights, rest = rest[: devices // 2 - 1], rest[devices // 2 - 1 :]
    if not first:
        sum_in, rest = rest[0], rest[1:]
    sum_out, fold_ref, *rest = rest
    if late:
        spread_ops, after_left, after_ops, *rest = rest
    states, width = psi_ref.shape[1], psi_ref.shape[-1]
    groups = width // TILE
    views = dict(zip(late, source_views(payloads)))
    rights = list(near_rights) + [right.at[side] for right in far_rights for side in (0, 1)]
    for at, source in enumerate(late):
        operators = views[source][half * held * width :, :]
        spread_operators(operators, range(start, start + terms), spread_ops, at * terms, states)
    fold_ref[...] = jnp.zeros_like(fold_ref)
    if last:
        sum_out[...] = jnp.zeros_like(sum_out)

    def work(block, place, sector, own_rows, partner_rows):
        total = rest[0] if last else sum_out.at[block]
        columns = [
            jnp.concatenate(
                [rights[pair + at][block, term] for at in range(2) for term in range(terms)],
                axis=0,
            )
            for pair in range(0, devices, 2)
        ]

        def operated(device, term, group):
            if device in ahead:
                return early_refs[ahead.index(device)][block, term, group]
            return after_ops[late.index(device) * terms + term, group]

        def multiply(live_groups):
            if late:
                lefts = [
                    term_rows(views[source], place, held, start + term, live_groups * TILE)
                    for source in late
                    for term in range(terms)
                ]
                multiply_left(live_groups, lefts, psi_ref.at[block], after_left)
            targets = [(after_ops, (term,)) for term in range(len(late) * terms)]
            for group in range(0, live_groups, WIDE):
                if late:
                    apply_operators(group, group + WIDE, spread_ops, after_left, targets)
                parts = []
                for pair in range(0, devices, 2):
                    rows = jnp.concatenate(
                        [
                            jnp.concatenate(
                                [
                                    operated(pair + at, term, group + side)
                                    for at in range(2)
                                    for term in range(terms)
                                ],
                                axis=1,
                            )
                            for side in range(WIDE)
                        ],
                        axis=0,
                    )
                    parts.append(
                        jnp.dot(rows, columns[pair // 2], preferred_element_type=jnp.float32)
                    )
                while len(parts) > 1:
                    parts = [parts[at] + parts[at + 1] for at in range(0, len(parts), 2)]
                done = parts[0].reshape(WIDE, states, TILE, width)
                for side in range(WIDE):
                    tile = slice((group + side) * TILE, (group + side + 1) * TILE)
                    if first:
                        total[:, tile, :] = done[side]
                    else:
                        total[:, tile, :] = sum_in[block, :, tile, :] + done[side]

        by_live_rows(own_rows, groups, multiply)
        if last:
            mask = live_entries(own_rows, partner_rows, width)
            kept = jnp.where(mask, total[...], 0.0)
            fold_ref[...] += folded(kept * psi_ref[block].astype(jnp.float32))
            sum_out[block] = kept.astype(jnp.bfloat16)

    each_live_block(half, slots, (meta, places, sector_rows, partners, counts), work)


def chunk_call(first, last, held, chunk, ahead, late, scalars, slots, psi, early, payloads,
               rights, total, after):
    blocks, states, width = psi.shape[:3]
    groups, wide = width // TILE, states * TILE
    start, terms = chunk
    operands = [after, psi, *early, *payloads, *rights]
    aliases = {}
    if not first:
        operands.append(total)
        if not last:
            aliases = {len(scalars) + len(operands) - 1: 0}
    sum_dtype = jnp.bfloat16 if last else jnp.float32
    every = len(late) * terms
    scratch = []
    if late:
        scratch += [
            pltpu.VMEM((every, wide, wide), jnp.bfloat16),
            pltpu.VMEM((every, groups, wide, width), jnp.bfloat16),
            pltpu.VMEM((every, groups, wide, width), jnp.bfloat16),
        ]
    if last:
        scratch.append(pltpu.VMEM((states, width, width), jnp.float32))
    work = psi.size * terms * ((len(ahead) + len(late)) * width + len(late) * (width + wide))
    return pl.pallas_call(
        functools.partial(
            chunk_kernel, first, last, held, chunk, ahead, late, len(payloads),
            blocks // slots, slots,
        ),
        in_specs=in_smem(len(scalars))
        + [pl.BlockSpec(memory_space=pl.ANY)]
        + resident(len(operands) - 1),
        out_specs=resident(2),
        out_shape=[
            jax.ShapeDtypeStruct(psi.shape, sum_dtype),
            jax.ShapeDtypeStruct((8, width), jnp.float32),
        ],
        scratch_shapes=scratch,
        input_output_aliases=aliases,
        compiler_params=pltpu.CompilerParams(
            vmem_limit_bytes=(len(ahead) + len(late)) * SPARE // 4
            + 2 * every * wide * (wide + 2 * groups * width)
            + 4 * int(last) * states * width * width
        ),
        cost_estimate=pl.CostEstimate(
            flops=work // HASTE, bytes_accessed=psi.size // HASTE, transcendentals=0
        ),
        name="chunk",
    )(*scalars, *operands)


def residual_kernel(half, slots, meta, places, sector_rows, partners, counts,
                    folds_ref, live_psi, own_ref, other_ref, psi_ref, out_ref, quotient_ref,
                    other_psi, staged, read_sems, write_sems):
    scalars = (meta, places, sector_rows, partners, counts)
    blocks, width = own_ref.shape[0], own_ref.shape[-1]
    depth = staged.shape[0]

    def where(block, side):
        index = (meta[1] ^ side) * half + block // slots
        return places[index], block % slots, index

    def read(block):
        sector, slot, _ = where(block, 1)
        return pltpu.make_async_copy(
            psi_ref.at[sector, slot], other_psi.at[block], read_sems.at[block]
        )

    def write(step):
        sector, slot, _ = where(step % blocks, step // blocks)
        return pltpu.make_async_copy(
            staged.at[step % depth], out_ref.at[sector, slot], write_sems.at[step % depth]
        )

    for block in range(blocks):
        read(block).start()
    quotient = jnp.sum(folds_ref[0:8, :]) / jnp.sum(folds_ref[8:16, :])
    quotient_ref[0] = quotient
    for step in range(2 * blocks):
        block, side = step % blocks, step // blocks
        if step >= depth:
            write(step - depth).wait()
        sector, slot, index = where(block, side)
        _, live, own_rows, partner_rows = block_facts(scalars, index, slot)
        mask = live_entries(jnp.where(live, own_rows, 0), partner_rows, width)
        if side:
            read(block).wait()
            values, sums = other_psi[block], other_ref[block]
        else:
            values, sums = live_psi[block], own_ref[block]
        scaled = quotient * jnp.where(mask, values.astype(jnp.float32), 0.0)
        staged[step % depth] = (sums.astype(jnp.float32) - scaled).astype(jnp.bfloat16)
        write(step).start()
    for step in range(2 * blocks - min(depth, 2 * blocks), 2 * blocks):
        write(step).wait()


def residual_call(scalars, folds, psi, live_psi, own, other):
    sectors, slots, states, width = psi.shape[:4]
    blocks = own.shape[0]
    depth = 4
    in_hbm = [pl.BlockSpec(memory_space=pltpu.HBM)]
    return pl.pallas_call(
        functools.partial(residual_kernel, sectors // 2, slots),
        in_specs=in_smem(len(scalars)) + resident(4) + in_hbm,
        out_specs=in_hbm + in_smem(1),
        out_shape=[
            jax.ShapeDtypeStruct(psi.shape, jnp.bfloat16),
            jax.ShapeDtypeStruct((1,), jnp.float32),
        ],
        scratch_shapes=[
            pltpu.VMEM((blocks, states, width, width), jnp.bfloat16),
            pltpu.VMEM((depth, states, width, width), jnp.bfloat16),
            pltpu.SemaphoreType.DMA((blocks,)),
            pltpu.SemaphoreType.DMA((depth,)),
        ],
        compiler_params=pltpu.CompilerParams(vmem_limit_bytes=41 * MIB),
        cost_estimate=pl.CostEstimate(
            flops=3 * psi.size, bytes_accessed=6 * psi.size, transcendentals=0
        ),
        name="residual",
    )(*scalars, folds, live_psi, own, other, psi)


def on_device(
    devices, rings, psi, left_env, right_env, local_ops, term_op, sector_rows, block_partner,
    block_count,
):
    sectors, slots, states, width = psi.shape[:4]
    terms = left_env.shape[1]
    half = sectors // 2
    me = lax.axis_index("term")
    ring = lax.axis_index("sec")
    core = me % 2
    meta = jnp.stack([ring * sectors, core, me, ring]).astype(jnp.int32)

    near_rows = lax.dynamic_slice_in_dim(sector_rows, ring * sectors, sectors)
    weight = block_count * (near_rows + width // 2)
    order = jnp.arange(sectors, dtype=jnp.int32)
    ahead = (weight[None, :] > weight[:, None]) | (
        (weight[None, :] == weight[:, None]) & (order[None, :] < order[:, None])
    )
    rank = jnp.sum(ahead.astype(jnp.int32), axis=1)
    index = ((rank ^ (rank >> 1)) & 1) * half + (rank >> 1)
    places = jnp.sum(jnp.where(index[None, :] == order[:, None], order[None, :], 0), axis=1)
    scalars = (meta, places, sector_rows, block_partner, block_count)

    def swap(value, bits, axis="term", size=devices):
        return lax.ppermute(value, axis, [(i, i ^ bits) for i in range(size)])

    def to_far_chips(near, received):
        both = stack_call(near, received)
        return both, [swap(both, bits) for bits in range(2, devices, 2)]

    chunks = [(at, 1) for at in range(terms)]
    ordered = jnp.roll(places, -core * half)
    parcels = [chunks[0], (chunks[0][1], terms - chunks[0][1])]
    mine, theirs, *shares = pack_call(
        parcels, ordered, term_op, local_ops, left_env, right_env
    )
    near_left = swap(theirs, 1)
    both_lefts, far_lefts = to_far_chips(mine, near_left)

    shards, rights = [], []
    swapped = [swap(share, 1, "sec", rings) for share in shares]
    line = rings == 4

    def gather():
        at = len(shards)
        if at == 0:
            pair = stack_call(shares[0], swapped[0])
        else:
            start, length = chunks[at]
            pair = stack_call(shares[1], swapped[1], (start - parcels[1][0], length))
        pieces = [pair]
        if line:
            pieces.append(lax.ppermute(pair, "sec", [(1, 2), (2, 1)]))
        bits = 2
        while bits < rings and not line:
            pieces = pieces + [swap(piece, bits, "sec", rings) for piece in pieces]
            bits *= 2
        shards.append(pieces)

    def choose(token):
        at = len(rights)
        afters = [token] + (rights[-1][2:] if rights else far_lefts)
        if 0 < at < len(chunks) - 1:
            afters.append(shards[at + 1][-1])
        pieces = shards[at]
        if line:
            pieces = pieces + [lax.ppermute(pieces[-1], "sec", [(1, 0), (2, 3)])]
        mine, other = choose_call(line, scalars, half, slots, pieces, afters)
        received = swap(other, 1)
        if at < len(chunks) - 1:
            both, far_rights = to_far_chips(mine, received)
        else:
            both = mine
            far_rights = [
                stack_call(swap(mine, bits), swap(other, bits + 1))
                for bits in range(2, devices, 2)
            ]
        rights.append([mine, received] + far_rights)
        return both

    products = {}
    shape = (half * slots, slots, states, width)
    far = tuple(range(2, devices))

    def go_left(sources, which, token, first=False, waits=()):
        items = [(source, *chunks[at]) for at in which for source in sources]
        near = [source for source in sources if source < 2]
        payloads = [(mine, near_left)[source] for source in near]
        if len(near) < len(sources):
            payloads += far_lefts
        renamed = [(sources.index(source), start, count) for source, start, count in items]
        outs = left_call(
            first, scalars, terms, renamed, shape, psi if first else live_psi, payloads,
            [token, *waits],
        )
        for at, out in zip([(at, source) for at in which for source in sources], outs):
            products[at] = out
        return outs[len(items) :]

    every = range(len(chunks))
    gather()
    token, live_psi, squares = go_left((0,), every, both_lefts, True)
    shards[0][-1], shares[1], swapped[1], _ = lax.optimization_barrier(
        (shards[0][-1], shares[1], swapped[1], token)
    )
    for chunk in chunks[1:]:
        gather()
    token, = go_left((1,), every[1:], token)
    token = choose(token)
    total = None
    for at, chunk in enumerate(chunks):
        last = at == len(chunks) - 1
        if len(rights) < len(chunks):
            token = choose(token)
        ahead = tuple(source for source in range(devices) if (at, source) in products)
        late = tuple(source for source in range(devices) if source not in ahead)
        payloads = ([near_left] if 1 in late else []) + (far_lefts if late else [])
        total, token = chunk_call(
            at == 0, last, terms, chunk, ahead, late, scalars, slots, live_psi,
            [products.pop((at, source)) for source in ahead], payloads,
            rights[at], total, token,
        )
        if at == len(chunks) - 3:
            token, = go_left(far, [len(chunks) - 1], token)

    other = swap(total, 1)
    folds = jnp.concatenate([token, squares], axis=0)
    parts = [folds] + [swap(folds, bits, "sec", rings) for bits in range(1, rings)]
    while len(parts) > 1:
        parts = [parts[at] + parts[at + 1] for at in range(0, len(parts), 2)]
    folds = parts[0]
    folds = folds + swap(folds, 1)
    residual, rayleigh = residual_call(scalars, folds, psi, live_psi, total, other)
    return residual, rayleigh


def solution(mesh):
    placed = (
        P(("groups", "sec"), None, None, None, None),
        P(("groups", "sec"), "term", None, None),
        P(("groups", "sec"), "term", None, None),
        P(),
        P("term"),
        P("groups"),
        P(("groups", "sec"), None),
        P(("groups", "sec")),
    )
    return jax.shard_map(
        functools.partial(on_device, mesh.shape["term"], mesh.shape["sec"]),
        mesh=mesh,
        in_specs=placed,
        out_specs=(P(("groups", "sec"), None, None, None, None), P("groups")),
        check_vma=False,
    )
```

```python
import functools

import jax
import jax.numpy as jnp
from jax import lax
from jax.experimental import pallas as pl
from jax.experimental.pallas import tpu as pltpu
from jax.sharding import PartitionSpec as P

TILE = 16
WIDE = 2
MIB = 1024 * 1024
SPARE = 3 * MIB // 2
HASTE = 256


def block_facts(scalars, index, slot):
    meta, places, sector_rows, partners, counts = scalars
    sector = places[index]
    live = slot < counts[sector]
    own_rows = sector_rows[meta[0] + sector]
    partner_rows = sector_rows[partners[sector, slot]]
    return sector, live, own_rows, partner_rows


def live_entries(own_rows, partner_rows, width):
    left = lax.broadcasted_iota(jnp.int32, (1, width, width), 1) < own_rows
    right = lax.broadcasted_iota(jnp.int32, (1, width, width), 2) < partner_rows
    return left & right


def folded(values):
    states, width = values.shape[0], values.shape[-1]
    return jnp.sum(values.reshape(states * width // 8, 8, width), axis=0)


def by_live_rows(own_rows, groups, work):
    few = 3 * groups // 4
    pl.when(own_rows <= few * TILE)(functools.partial(work, few))
    pl.when(own_rows > few * TILE)(functools.partial(work, groups))


def spread_operators(ops_ref, chosen, spread_ops, at, states):
    width, wide = ops_ref.shape[-1], states * TILE
    row_state = lax.broadcasted_iota(jnp.int32, (wide, states), 0) // TILE
    column = lax.broadcasted_iota(jnp.int32, (wide, states), 1)
    pick_rows = (row_state == column).astype(jnp.bfloat16)
    row = lax.broadcasted_iota(jnp.int32, (width, wide), 0)
    column_state = lax.broadcasted_iota(jnp.int32, (width, wide), 1) // TILE
    pick_columns = (row == column_state).astype(jnp.bfloat16)
    inner_row = lax.rem(lax.broadcasted_iota(jnp.int32, (wide, wide), 0), TILE)
    inner_column = lax.rem(lax.broadcasted_iota(jnp.int32, (wide, wide), 1), TILE)
    for term in chosen:
        operator = ops_ref[term * states : (term + 1) * states, :]
        rows = jnp.dot(pick_rows, operator, preferred_element_type=jnp.float32)
        full = jnp.dot(
            rows.astype(jnp.bfloat16), pick_columns, preferred_element_type=jnp.float32
        )
        spread_ops[at] = jnp.where(inner_row == inner_column, full, 0.0).astype(jnp.bfloat16)
        at += 1


def multiply_left(groups, lefts, live_psi, after_left):
    rows = groups * TILE
    states, width = live_psi.shape[0], live_psi.shape[-1]
    stacked = jnp.concatenate(lefts, axis=0)
    for pair in range(states // WIDE):
        columns = jnp.concatenate([live_psi[pair * WIDE + at] for at in range(WIDE)], axis=1)
        done = jnp.dot(stacked, columns, preferred_element_type=jnp.float32).astype(jnp.bfloat16)
        for term in range(len(lefts)):
            for at in range(WIDE):
                state = pair * WIDE + at
                after_left[term, :groups, state * TILE : (state + 1) * TILE, :] = done[
                    term * rows : (term + 1) * rows, at * width : (at + 1) * width
                ].reshape(groups, TILE, width)


def apply_operators(low, high, spread_ops, after_left, targets):
    width = after_left.shape[-1]
    for group in range(low, high, WIDE):
        for term, (target, lead) in enumerate(targets):
            columns = jnp.concatenate(
                [after_left[term, group + at] for at in range(WIDE)], axis=1
            )
            done = jnp.dot(
                spread_ops[term], columns, preferred_element_type=jnp.float32
            ).astype(jnp.bfloat16)
            for at in range(WIDE):
                target[(*lead, group + at)] = done[:, at * width : (at + 1) * width]


def each_live_block(half, slots, scalars, work):
    meta = scalars[0]

    def visit(block, carry):
        place, slot = block // slots, lax.rem(block, slots)
        sector, live, own_rows, partner_rows = block_facts(
            scalars, meta[1] * half + place, slot
        )
        pl.when(live)(functools.partial(work, block, place, sector, own_rows, partner_rows))
        return carry

    lax.fori_loop(0, half * slots, visit, 0)


def pack_kernel(chunks, half, terms, places, term_op, ops_ref, left_ref, right_ref, *rest):
    payloads, rest = rest[:2], rest[2:]
    shares, sems = rest[: len(chunks)], rest[len(chunks)]
    states, width = ops_ref.shape[1], left_ref.shape[-1]
    copied = half * terms * width
    for part, payload in enumerate(payloads):
        for place in range(half):
            pltpu.make_async_copy(
                left_ref.at[places[part * half + place]],
                payload.at[pl.ds(place * terms * width, terms * width)],
                sems.at[part],
            ).start()
    moves = []
    for at, (start, length) in enumerate(chunks):
        move = pltpu.make_async_copy(
            right_ref.at[:, pl.ds(start, length)], shares[at], sems.at[2 + at]
        )
        move.start()
        moves.append(move)
    for payload in payloads:
        for term in range(terms):
            rows = slice(copied + term * states, copied + (term + 1) * states)
            payload[rows, :] = jnp.zeros((states, width), jnp.bfloat16)
            payload[rows, :states] = ops_ref[term_op[term]]
    for part, payload in enumerate(payloads):
        whole = payload.at[pl.ds(0, copied)]
        pltpu.make_async_copy(whole, whole, sems.at[part]).wait()
    for move in moves:
        move.wait()


def pack_call(chunks, places, term_op, local_ops, left_env, right_env):
    sectors, terms, width = left_env.shape[:3]
    half, states = sectors // 2, local_ops.shape[1]
    payload = jax.ShapeDtypeStruct((terms * (half * width + states), width), jnp.bfloat16)
    shares = [
        jax.ShapeDtypeStruct((sectors, length, width, width), jnp.bfloat16)
        for start, length in chunks
    ]
    return pl.pallas_call(
        functools.partial(pack_kernel, chunks, half, terms),
        in_specs=in_smem(2) + resident(1) + [pl.BlockSpec(memory_space=pltpu.HBM)] * 2,
        out_specs=resident(2 + len(chunks)),
        out_shape=[payload, payload] + shares,
        scratch_shapes=[pltpu.SemaphoreType.DMA((2 + len(chunks),))],
        compiler_params=pltpu.CompilerParams(vmem_limit_bytes=58 * MIB),
        cost_estimate=pl.CostEstimate(
            flops=0, bytes_accessed=4 * left_env.size, transcendentals=0
        ),
        name="pack",
    )(places, term_op, local_ops, left_env.reshape(sectors, terms * width, width), right_env)


def source_views(payloads):
    views = []
    for payload in payloads:
        views += [payload] if len(payload.shape) == 2 else [payload.at[0], payload.at[1]]
    return views


def term_rows(view, place, held, term, rows):
    width = view.shape[-1]
    return view[pl.ds(pl.multiple_of((place * held + term) * width, width), rows), :]


def left_kernel(first, held, items, count, afters, half, slots, meta, places, sector_rows,
                partners, counts, *rest):
    scalars = (meta, places, sector_rows, partners, counts)
    psi_ref, rest = rest[afters], rest[afters + 1 :]
    payloads, rest = rest[:count], rest[count:]
    outs, rest = rest[: len(items)], rest[len(items) :]
    token_ref, rest = rest[0], rest[1:]
    if first:
        live_psi, square_ref, spread_ops, after_left, sems = rest
    else:
        live_psi = psi_ref
        spread_ops, after_left = rest
    states, width = live_psi.shape[1], live_psi.shape[-1]
    views = source_views(payloads)

    def fetch(block, sector):
        return pltpu.make_async_copy(
            psi_ref.at[sector, lax.rem(block, slots)], live_psi.at[block], sems.at[block]
        )

    if first:
        each_live_block(
            half, slots, scalars, lambda block, place, sector, *rows: fetch(block, sector).start()
        )
        square_ref[...] = jnp.zeros_like(square_ref)
    at = 0
    for source, start, terms in items:
        operators = views[source][half * held * width :, :]
        spread_operators(operators, range(start, start + terms), spread_ops, at, states)
        at += terms
    token_ref[...] = jnp.zeros_like(token_ref)

    def work(block, place, sector, own_rows, partner_rows):
        if first:
            fetch(block, sector).wait()
            mask = live_entries(own_rows, partner_rows, width)
            kept = jnp.where(mask, live_psi[block], jnp.zeros((), jnp.bfloat16))
            live_psi[block] = kept
            wide_psi = kept.astype(jnp.float32)
            square_ref[...] += folded(wide_psi * wide_psi)
        targets = [
            (outs[at], (block, term))
            for at, (source, start, terms) in enumerate(items)
            for term in range(terms)
        ]

        def multiply(groups):
            lefts = [
                term_rows(views[source], place, held, start + term, groups * TILE)
                for source, start, terms in items
                for term in range(terms)
            ]
            multiply_left(groups, lefts, live_psi.at[block], after_left)
            apply_operators(0, groups, spread_ops, after_left, targets)

        by_live_rows(own_rows, width // TILE, multiply)

    each_live_block(half, slots, scalars, work)


def resident(count):
    return [pl.BlockSpec(memory_space=pltpu.VMEM)] * count


def in_smem(count):
    return [pl.BlockSpec(memory_space=pltpu.SMEM)] * count


def left_call(first, scalars, held, items, shape, psi, payloads, afters):
    blocks, slots, states, width = shape
    groups, wide = width // TILE, states * TILE
    every = sum(terms for source, start, terms in items)
    fold_shape = jax.ShapeDtypeStruct((8, width), jnp.float32)
    out_shape = [
        jax.ShapeDtypeStruct((blocks, terms, groups, wide, width), jnp.bfloat16)
        for source, start, terms in items
    ] + [fold_shape]
    scratch = [
        pltpu.VMEM((every, wide, wide), jnp.bfloat16),
        pltpu.VMEM((every, groups, wide, width), jnp.bfloat16),
    ]
    if first:
        live_psi = jax.ShapeDtypeStruct((blocks, states, width, width), jnp.bfloat16)
        out_shape += [live_psi, fold_shape]
        scratch.append(pltpu.SemaphoreType.DMA((blocks,)))
    psi_spec = [pl.BlockSpec(memory_space=pltpu.HBM)] if first else resident(1)
    return pl.pallas_call(
        functools.partial(
            left_kernel, first, held, items, len(payloads), len(afters), blocks // slots, slots
        ),
        in_specs=in_smem(len(scalars))
        + [pl.BlockSpec(memory_space=pl.ANY)] * len(afters)
        + psi_spec
        + resident(len(payloads)),
        out_specs=resident(len(out_shape)),
        out_shape=out_shape,
        scratch_shapes=scratch,
        compiler_params=pltpu.CompilerParams(
            vmem_limit_bytes=max(
                28 * MIB if first else 0,
                SPARE + 2 * every * (wide * wide + groups * wide * width),
            )
        ),
        cost_estimate=pl.CostEstimate(
            flops=psi.size * every * (width + wide) // HASTE,
            bytes_accessed=psi.size // HASTE,
            transcendentals=0,
        ),
        name="left",
    )(*scalars, *afters, psi, *payloads)


def stack_kernel(start, near_ref, received_ref, both_ref):
    terms = both_ref.shape[2] if len(both_ref.shape) == 5 else None
    for side, ref in enumerate((near_ref, received_ref)):
        both_ref[side] = ref[...] if start is None else ref[:, start : start + terms]


def stack_call(near, received, chunk=None):
    start, terms = chunk or (None, None)
    shape = near.shape if chunk is None else (near.shape[0], terms) + near.shape[2:]
    return pl.pallas_call(
        functools.partial(stack_kernel, start),
        in_specs=resident(2),
        out_specs=resident(1)[0],
        out_shape=jax.ShapeDtypeStruct((2,) + shape, near.dtype),
        compiler_params=pltpu.CompilerParams(vmem_limit_bytes=SPARE),
        cost_estimate=pl.CostEstimate(flops=0, bytes_accessed=4096, transcendentals=0),
        name="stack",
    )(near, received)


def choose_kernel(line, count, afters, half, slots, meta, places, partners, *rest):
    rest = rest[afters:]
    pieces, (mine_ref, other_ref) = rest[:count], rest[count:]
    sectors = pieces[0].shape[1]
    for part, out_ref in enumerate((mine_ref, other_ref)):
        for block in range(half * slots):
            sector = places[(meta[1] ^ part) * half + block // slots]
            partner = partners[sector, block % slots]
            away = meta[3] ^ (partner // sectors)
            piece, side = away // 2, away & 1
            if line:
                inner = ((meta[3] + 1) & 2) // 2
                side = side ^ (piece & inner)
                piece = piece + (piece & (1 - inner))
            place = lax.rem(partner, sectors)
            for at in range(count):
                @pl.when(piece == at)
                def _(at=at, side=side, place=place, block=block, out_ref=out_ref):
                    out_ref[block] = pieces[at][side, place]


def choose_call(line, scalars, half, slots, pieces, afters):
    meta, places, _, partners, _ = scalars
    terms, width = pieces[0].shape[2:4]
    chosen = jax.ShapeDtypeStruct((half * slots, terms, width, width), jnp.bfloat16)
    return pl.pallas_call(
        functools.partial(choose_kernel, line, len(pieces), len(afters), half, slots),
        in_specs=in_smem(3)
        + [pl.BlockSpec(memory_space=pl.ANY)] * len(afters)
        + resident(len(pieces)),
        out_specs=resident(2),
        out_shape=[chosen, chosen],
        compiler_params=pltpu.CompilerParams(vmem_limit_bytes=SPARE),
        cost_estimate=pl.CostEstimate(flops=0, bytes_accessed=4096, transcendentals=0),
        name="choose",
    )(meta, places, partners, *afters, *pieces)


def chunk_kernel(first, last, held, chunk, ahead, late, count, half, slots,
                 meta, places, sector_rows, partners, counts, after_ref, psi_ref, *rest):
    start, terms = chunk
    early_refs, rest = rest[: len(ahead)], rest[len(ahead) :]
    payloads, rest = rest[:count], rest[count:]
    near_rights, rest = rest[:2], rest[2:]
    devices = len(ahead) + len(late)
    far_rights, rest = rest[: devices // 2 - 1], rest[devices // 2 - 1 :]
    if not first:
        sum_in, rest = rest[0], rest[1:]
    sum_out, fold_ref, *rest = rest
    if late:
        spread_ops, after_left, after_ops, *rest = rest
    states, width = psi_ref.shape[1], psi_ref.shape[-1]
    groups = width // TILE
    views = dict(zip(late, source_views(payloads)))
    rights = list(near_rights) + [right.at[side] for right in far_rights for side in (0, 1)]
    for at, source in enumerate(late):
        operators = views[source][half * held * width :, :]
        spread_operators(operators, range(start, start + terms), spread_ops, at * terms, states)
    fold_ref[...] = jnp.zeros_like(fold_ref)
    if last:
        sum_out[...] = jnp.zeros_like(sum_out)

    def work(block, place, sector, own_rows, partner_rows):
        total = rest[0] if last else sum_out.at[block]
        columns = [
            jnp.concatenate(
                [rights[pair + at][block, term] for at in range(2) for term in range(terms)],
                axis=0,
            )
            for pair in range(0, devices, 2)
        ]

        def operated(device, term, group):
            if device in ahead:
                return early_refs[ahead.index(device)][block, term, group]
            return after_ops[late.index(device) * terms + term, group]

        def multiply(live_groups):
            if late:
                lefts = [
                    term_rows(views[source], place, held, start + term, live_groups * TILE)
                    for source in late
                    for term in range(terms)
                ]
                multiply_left(live_groups, lefts, psi_ref.at[block], after_left)
            targets = [(after_ops, (term,)) for term in range(len(late) * terms)]
            for group in range(0, live_groups, WIDE):
                if late:
                    apply_operators(group, group + WIDE, spread_ops, after_left, targets)
                parts = []
                for pair in range(0, devices, 2):
                    rows = jnp.concatenate(
                        [
                            jnp.concatenate(
                                [
                                    operated(pair + at, term, group + side)
                                    for at in range(2)
                                    for term in range(terms)
                                ],
                                axis=1,
                            )
                            for side in range(WIDE)
                        ],
                        axis=0,
                    )
                    parts.append(
                        jnp.dot(rows, columns[pair // 2], preferred_element_type=jnp.float32)
                    )
                while len(parts) > 1:
                    parts = [parts[at] + parts[at + 1] for at in range(0, len(parts), 2)]
                done = parts[0].reshape(WIDE, states, TILE, width)
                for side in range(WIDE):
                    tile = slice((group + side) * TILE, (group + side + 1) * TILE)
                    if first:
                        total[:, tile, :] = done[side]
                    else:
                        total[:, tile, :] = sum_in[block, :, tile, :] + done[side]

        by_live_rows(own_rows, groups, multiply)
        if last:
            mask = live_entries(own_rows, partner_rows, width)
            kept = jnp.where(mask, total[...], 0.0)
            fold_ref[...] += folded(kept * psi_ref[block].astype(jnp.float32))
            sum_out[block] = kept.astype(jnp.bfloat16)

    each_live_block(half, slots, (meta, places, sector_rows, partners, counts), work)


def chunk_call(first, last, held, chunk, ahead, late, scalars, slots, psi, early, payloads,
               rights, total, after):
    blocks, states, width = psi.shape[:3]
    groups, wide = width // TILE, states * TILE
    start, terms = chunk
    operands = [after, psi, *early, *payloads, *rights]
    aliases = {}
    if not first:
        operands.append(total)
        if not last:
            aliases = {len(scalars) + len(operands) - 1: 0}
    sum_dtype = jnp.bfloat16 if last else jnp.float32
    every = len(late) * terms
    scratch = []
    if late:
        scratch += [
            pltpu.VMEM((every, wide, wide), jnp.bfloat16),
            pltpu.VMEM((every, groups, wide, width), jnp.bfloat16),
            pltpu.VMEM((every, groups, wide, width), jnp.bfloat16),
        ]
    if last:
        scratch.append(pltpu.VMEM((states, width, width), jnp.float32))
    work = psi.size * terms * ((len(ahead) + len(late)) * width + len(late) * (width + wide))
    return pl.pallas_call(
        functools.partial(
            chunk_kernel, first, last, held, chunk, ahead, late, len(payloads),
            blocks // slots, slots,
        ),
        in_specs=in_smem(len(scalars))
        + [pl.BlockSpec(memory_space=pl.ANY)]
        + resident(len(operands) - 1),
        out_specs=resident(2),
        out_shape=[
            jax.ShapeDtypeStruct(psi.shape, sum_dtype),
            jax.ShapeDtypeStruct((8, width), jnp.float32),
        ],
        scratch_shapes=scratch,
        input_output_aliases=aliases,
        compiler_params=pltpu.CompilerParams(
            vmem_limit_bytes=(len(ahead) + len(late)) * SPARE // 4
            + 2 * every * wide * (wide + 2 * groups * width)
            + 4 * int(last) * states * width * width
        ),
        cost_estimate=pl.CostEstimate(
            flops=work // HASTE, bytes_accessed=psi.size // HASTE, transcendentals=0
        ),
        name="chunk",
    )(*scalars, *operands)


def residual_kernel(half, slots, meta, places, sector_rows, partners, counts,
                    folds_ref, live_psi, own_ref, other_ref, psi_ref, out_ref, quotient_ref,
                    other_psi, staged, read_sems, write_sems):
    scalars = (meta, places, sector_rows, partners, counts)
    blocks, width = own_ref.shape[0], own_ref.shape[-1]
    depth = staged.shape[0]

    def where(block, side):
        index = (meta[1] ^ side) * half + block // slots
        return places[index], block % slots, index

    def read(block):
        sector, slot, _ = where(block, 1)
        return pltpu.make_async_copy(
            psi_ref.at[sector, slot], other_psi.at[block], read_sems.at[block]
        )

    def write(step):
        sector, slot, _ = where(step % blocks, step // blocks)
        return pltpu.make_async_copy(
            staged.at[step % depth], out_ref.at[sector, slot], write_sems.at[step % depth]
        )

    for block in range(blocks):
        read(block).start()
    quotient = jnp.sum(folds_ref[0:8, :]) / jnp.sum(folds_ref[8:16, :])
    quotient_ref[0] = quotient
    for step in range(2 * blocks):
        block, side = step % blocks, step // blocks
        if step >= depth:
            write(step - depth).wait()
        sector, slot, index = where(block, side)
        _, live, own_rows, partner_rows = block_facts(scalars, index, slot)
        mask = live_entries(jnp.where(live, own_rows, 0), partner_rows, width)
        if side:
            read(block).wait()
            values, sums = other_psi[block], other_ref[block]
        else:
            values, sums = live_psi[block], own_ref[block]
        scaled = quotient * jnp.where(mask, values.astype(jnp.float32), 0.0)
        staged[step % depth] = (sums.astype(jnp.float32) - scaled).astype(jnp.bfloat16)
        write(step).start()
    for step in range(2 * blocks - min(depth, 2 * blocks), 2 * blocks):
        write(step).wait()


def residual_call(scalars, folds, psi, live_psi, own, other):
    sectors, slots, states, width = psi.shape[:4]
    blocks = own.shape[0]
    depth = 4
    in_hbm = [pl.BlockSpec(memory_space=pltpu.HBM)]
    return pl.pallas_call(
        functools.partial(residual_kernel, sectors // 2, slots),
        in_specs=in_smem(len(scalars)) + resident(4) + in_hbm,
        out_specs=in_hbm + in_smem(1),
        out_shape=[
            jax.ShapeDtypeStruct(psi.shape, jnp.bfloat16),
            jax.ShapeDtypeStruct((1,), jnp.float32),
        ],
        scratch_shapes=[
            pltpu.VMEM((blocks, states, width, width), jnp.bfloat16),
            pltpu.VMEM((depth, states, width, width), jnp.bfloat16),
            pltpu.SemaphoreType.DMA((blocks,)),
            pltpu.SemaphoreType.DMA((depth,)),
        ],
        compiler_params=pltpu.CompilerParams(vmem_limit_bytes=41 * MIB),
        cost_estimate=pl.CostEstimate(
            flops=3 * psi.size, bytes_accessed=6 * psi.size, transcendentals=0
        ),
        name="residual",
    )(*scalars, folds, live_psi, own, other, psi)


def on_device(
    devices, rings, psi, left_env, right_env, local_ops, term_op, sector_rows, block_partner,
    block_count,
):
    sectors, slots, states, width = psi.shape[:4]
    terms = left_env.shape[1]
    half = sectors // 2
    me = lax.axis_index("term")
    ring = lax.axis_index("sec")
    core = me % 2
    meta = jnp.stack([ring * sectors, core, me, ring]).astype(jnp.int32)

    near_rows = lax.dynamic_slice_in_dim(sector_rows, ring * sectors, sectors)
    weight = block_count * (near_rows + width // 2)
    order = jnp.arange(sectors, dtype=jnp.int32)
    ahead = (weight[None, :] > weight[:, None]) | (
        (weight[None, :] == weight[:, None]) & (order[None, :] < order[:, None])
    )
    rank = jnp.sum(ahead.astype(jnp.int32), axis=1)
    index = ((rank ^ (rank >> 1)) & 1) * half + (rank >> 1)
    places = jnp.sum(jnp.where(index[None, :] == order[:, None], order[None, :], 0), axis=1)
    scalars = (meta, places, sector_rows, block_partner, block_count)

    def swap(value, bits, axis="term", size=devices):
        return lax.ppermute(value, axis, [(i, i ^ bits) for i in range(size)])

    def to_far_chips(near, received):
        both = stack_call(near, received)
        return both, [swap(both, bits) for bits in range(2, devices, 2)]

    chunks = [(at, 1) for at in range(terms)]
    ordered = jnp.roll(places, -core * half)
    parcels = [chunks[0], (chunks[0][1], terms - chunks[0][1])]
    mine, theirs, *shares = pack_call(
        parcels, ordered, term_op, local_ops, left_env, right_env
    )
    near_left = swap(theirs, 1)
    both_lefts, far_lefts = to_far_chips(mine, near_left)

    shards, rights = [], []
    swapped = [swap(share, 1, "sec", rings) for share in shares]
    line = rings == 4

    def gather():
        at = len(shards)
        if at == 0:
            pair = stack_call(shares[0], swapped[0])
        else:
            start, length = chunks[at]
            pair = stack_call(shares[1], swapped[1], (start - parcels[1][0], length))
        pieces = [pair]
        if line:
            pieces.append(lax.ppermute(pair, "sec", [(1, 2), (2, 1)]))
        bits = 2
        while bits < rings and not line:
            pieces = pieces + [swap(piece, bits, "sec", rings) for piece in pieces]
            bits *= 2
        shards.append(pieces)

    def choose(token):
        at = len(rights)
        afters = [token] + (rights[-1][2:] if rights else far_lefts)
        if 0 < at < len(chunks) - 1:
            afters.append(shards[at + 1][-1])
        pieces = shards[at]
        if line:
            pieces = pieces + [lax.ppermute(pieces[-1], "sec", [(1, 0), (2, 3)])]
        mine, other = choose_call(line, scalars, half, slots, pieces, afters)
        received = swap(other, 1)
        if at < len(chunks) - 1:
            both, far_rights = to_far_chips(mine, received)
        else:
            both = mine
            far_rights = [
                stack_call(swap(mine, bits), swap(other, bits + 1))
                for bits in range(2, devices, 2)
            ]
        rights.append([mine, received] + far_rights)
        return both

    products = {}
    shape = (half * slots, slots, states, width)
    far = tuple(range(2, devices))

    def go_left(sources, which, token, first=False, waits=()):
        items = [(source, *chunks[at]) for at in which for source in sources]
        near = [source for source in sources if source < 2]
        payloads = [(mine, near_left)[source] for source in near]
        if len(near) < len(sources):
            payloads += far_lefts
        renamed = [(sources.index(source), start, count) for source, start, count in items]
        outs = left_call(
            first, scalars, terms, renamed, shape, psi if first else live_psi, payloads,
            [token, *waits],
        )
        for at, out in zip([(at, source) for at in which for source in sources], outs):
            products[at] = out
        return outs[len(items) :]

    every = range(len(chunks))
    gather()
    token, live_psi, squares = go_left((0,), every, both_lefts, True)
    shards[0][-1], shares[1], swapped[1], _ = lax.optimization_barrier(
        (shards[0][-1], shares[1], swapped[1], token)
    )
    for chunk in chunks[1:]:
        gather()
    token, = go_left((1,), every[1:], token)
    token = choose(token)
    token, = go_left(far, [len(chunks) - 1], token)
    total = None
    for at, chunk in enumerate(chunks):
        last = at == len(chunks) - 1
        if len(rights) < len(chunks):
            token = choose(token)
        ahead = tuple(source for source in range(devices) if (at, source) in products)
        late = tuple(source for source in range(devices) if source not in ahead)
        payloads = ([near_left] if 1 in late else []) + (far_lefts if late else [])
        total, token = chunk_call(
            at == 0, last, terms, chunk, ahead, late, scalars, slots, live_psi,
            [products.pop((at, source)) for source in ahead], payloads,
            rights[at], total, token,
        )

    other = swap(total, 1)
    folds = jnp.concatenate([token, squares], axis=0)
    parts = [folds] + [swap(folds, bits, "sec", rings) for bits in range(1, rings)]
    while len(parts) > 1:
        parts = [parts[at] + parts[at + 1] for at in range(0, len(parts), 2)]
    folds = parts[0]
    folds = folds + swap(folds, 1)
    residual, rayleigh = residual_call(scalars, folds, psi, live_psi, total, other)
    return residual, rayleigh


def solution(mesh):
    placed = (
        P(("groups", "sec"), None, None, None, None),
        P(("groups", "sec"), "term", None, None),
        P(("groups", "sec"), "term", None, None),
        P(),
        P("term"),
        P("groups"),
        P(("groups", "sec"), None),
        P(("groups", "sec")),
    )
    return jax.shard_map(
        functools.partial(on_device, mesh.shape["term"], mesh.shape["sec"]),
        mesh=mesh,
        in_specs=placed,
        out_specs=(P(("groups", "sec"), None, None, None, None), P("groups")),
        check_vma=False,
    )
```

```python
import functools

import jax
import jax.numpy as jnp
from jax import lax
from jax.experimental import pallas as pl
from jax.experimental.pallas import tpu as pltpu
from jax.sharding import PartitionSpec as P

TILE = 16
WIDE = 2
MIB = 1024 * 1024
SPARE = 3 * MIB // 2
HASTE = 256


def block_facts(scalars, index, slot):
    meta, places, sector_rows, partners, counts = scalars
    sector = places[index]
    live = slot < counts[sector]
    own_rows = sector_rows[meta[0] + sector]
    partner_rows = sector_rows[partners[sector, slot]]
    return sector, live, own_rows, partner_rows


def live_entries(own_rows, partner_rows, width):
    left = lax.broadcasted_iota(jnp.int32, (1, width, width), 1) < own_rows
    right = lax.broadcasted_iota(jnp.int32, (1, width, width), 2) < partner_rows
    return left & right


def folded(values):
    states, width = values.shape[0], values.shape[-1]
    return jnp.sum(values.reshape(states * width // 8, 8, width), axis=0)


def by_live_rows(own_rows, groups, work):
    few = 3 * groups // 4
    pl.when(own_rows <= few * TILE)(functools.partial(work, few))
    pl.when(own_rows > few * TILE)(functools.partial(work, groups))


def spread_operators(ops_ref, chosen, spread_ops, at, states):
    width, wide = ops_ref.shape[-1], states * TILE
    row_state = lax.broadcasted_iota(jnp.int32, (wide, states), 0) // TILE
    column = lax.broadcasted_iota(jnp.int32, (wide, states), 1)
    pick_rows = (row_state == column).astype(jnp.bfloat16)
    row = lax.broadcasted_iota(jnp.int32, (width, wide), 0)
    column_state = lax.broadcasted_iota(jnp.int32, (width, wide), 1) // TILE
    pick_columns = (row == column_state).astype(jnp.bfloat16)
    inner_row = lax.rem(lax.broadcasted_iota(jnp.int32, (wide, wide), 0), TILE)
    inner_column = lax.rem(lax.broadcasted_iota(jnp.int32, (wide, wide), 1), TILE)
    for term in chosen:
        operator = ops_ref[term * states : (term + 1) * states, :]
        rows = jnp.dot(pick_rows, operator, preferred_element_type=jnp.float32)
        full = jnp.dot(
            rows.astype(jnp.bfloat16), pick_columns, preferred_element_type=jnp.float32
        )
        spread_ops[at] = jnp.where(inner_row == inner_column, full, 0.0).astype(jnp.bfloat16)
        at += 1


def multiply_left(groups, lefts, live_psi, after_left):
    rows = groups * TILE
    states, width = live_psi.shape[0], live_psi.shape[-1]
    stacked = jnp.concatenate(lefts, axis=0)
    for pair in range(states // WIDE):
        columns = jnp.concatenate([live_psi[pair * WIDE + at] for at in range(WIDE)], axis=1)
        done = jnp.dot(stacked, columns, preferred_element_type=jnp.float32).astype(jnp.bfloat16)
        for term in range(len(lefts)):
            for at in range(WIDE):
                state = pair * WIDE + at
                after_left[term, :groups, state * TILE : (state + 1) * TILE, :] = done[
                    term * rows : (term + 1) * rows, at * width : (at + 1) * width
                ].reshape(groups, TILE, width)


def apply_operators(low, high, spread_ops, after_left, targets):
    width = after_left.shape[-1]
    for group in range(low, high, WIDE):
        for term, (target, lead) in enumerate(targets):
            columns = jnp.concatenate(
                [after_left[term, group + at] for at in range(WIDE)], axis=1
            )
            done = jnp.dot(
                spread_ops[term], columns, preferred_element_type=jnp.float32
            ).astype(jnp.bfloat16)
            for at in range(WIDE):
                target[(*lead, group + at)] = done[:, at * width : (at + 1) * width]


def each_live_block(half, slots, scalars, work):
    meta = scalars[0]

    def visit(block, carry):
        place, slot = block // slots, lax.rem(block, slots)
        sector, live, own_rows, partner_rows = block_facts(
            scalars, meta[1] * half + place, slot
        )
        pl.when(live)(functools.partial(work, block, place, sector, own_rows, partner_rows))
        return carry

    lax.fori_loop(0, half * slots, visit, 0)


def pack_kernel(chunks, half, terms, places, term_op, ops_ref, left_ref, right_ref, *rest):
    payloads, rest = rest[:2], rest[2:]
    shares, sems = rest[: len(chunks)], rest[len(chunks)]
    states, width = ops_ref.shape[1], left_ref.shape[-1]
    copied = half * terms * width
    for part, payload in enumerate(payloads):
        for place in range(half):
            pltpu.make_async_copy(
                left_ref.at[places[part * half + place]],
                payload.at[pl.ds(place * terms * width, terms * width)],
                sems.at[part],
            ).start()
    moves = []
    for at, (start, length) in enumerate(chunks):
        move = pltpu.make_async_copy(
            right_ref.at[:, pl.ds(start, length)], shares[at], sems.at[2 + at]
        )
        move.start()
        moves.append(move)
    for payload in payloads:
        for term in range(terms):
            rows = slice(copied + term * states, copied + (term + 1) * states)
            payload[rows, :] = jnp.zeros((states, width), jnp.bfloat16)
            payload[rows, :states] = ops_ref[term_op[term]]
    for part, payload in enumerate(payloads):
        whole = payload.at[pl.ds(0, copied)]
        pltpu.make_async_copy(whole, whole, sems.at[part]).wait()
    for move in moves:
        move.wait()


def pack_call(chunks, places, term_op, local_ops, left_env, right_env):
    sectors, terms, width = left_env.shape[:3]
    half, states = sectors // 2, local_ops.shape[1]
    payload = jax.ShapeDtypeStruct((terms * (half * width + states), width), jnp.bfloat16)
    shares = [
        jax.ShapeDtypeStruct((sectors, length, width, width), jnp.bfloat16)
        for start, length in chunks
    ]
    return pl.pallas_call(
        functools.partial(pack_kernel, chunks, half, terms),
        in_specs=in_smem(2) + resident(1) + [pl.BlockSpec(memory_space=pltpu.HBM)] * 2,
        out_specs=resident(2 + len(chunks)),
        out_shape=[payload, payload] + shares,
        scratch_shapes=[pltpu.SemaphoreType.DMA((2 + len(chunks),))],
        compiler_params=pltpu.CompilerParams(vmem_limit_bytes=58 * MIB),
        cost_estimate=pl.CostEstimate(
            flops=0, bytes_accessed=4 * left_env.size, transcendentals=0
        ),
        name="pack",
    )(places, term_op, local_ops, left_env.reshape(sectors, terms * width, width), right_env)


def source_views(payloads):
    views = []
    for payload in payloads:
        views += [payload] if len(payload.shape) == 2 else [payload.at[0], payload.at[1]]
    return views


def term_rows(view, place, held, term, rows):
    width = view.shape[-1]
    return view[pl.ds(pl.multiple_of((place * held + term) * width, width), rows), :]


def left_kernel(first, held, items, count, afters, half, slots, meta, places, sector_rows,
                partners, counts, *rest):
    scalars = (meta, places, sector_rows, partners, counts)
    psi_ref, rest = rest[afters], rest[afters + 1 :]
    payloads, rest = rest[:count], rest[count:]
    outs, rest = rest[: len(items)], rest[len(items) :]
    token_ref, rest = rest[0], rest[1:]
    if first:
        live_psi, square_ref, spread_ops, after_left, sems = rest
    else:
        live_psi = psi_ref
        spread_ops, after_left = rest
    states, width = live_psi.shape[1], live_psi.shape[-1]
    views = source_views(payloads)

    def fetch(block, sector):
        return pltpu.make_async_copy(
            psi_ref.at[sector, lax.rem(block, slots)], live_psi.at[block], sems.at[block]
        )

    if first:
        each_live_block(
            half, slots, scalars, lambda block, place, sector, *rows: fetch(block, sector).start()
        )
        square_ref[...] = jnp.zeros_like(square_ref)
    at = 0
    for source, start, terms in items:
        operators = views[source][half * held * width :, :]
        spread_operators(operators, range(start, start + terms), spread_ops, at, states)
        at += terms
    token_ref[...] = jnp.zeros_like(token_ref)

    def work(block, place, sector, own_rows, partner_rows):
        if first:
            fetch(block, sector).wait()
            mask = live_entries(own_rows, partner_rows, width)
            kept = jnp.where(mask, live_psi[block], jnp.zeros((), jnp.bfloat16))
            live_psi[block] = kept
            wide_psi = kept.astype(jnp.float32)
            square_ref[...] += folded(wide_psi * wide_psi)
        targets = [
            (outs[at], (block, term))
            for at, (source, start, terms) in enumerate(items)
            for term in range(terms)
        ]

        def multiply(groups):
            lefts = [
                term_rows(views[source], place, held, start + term, groups * TILE)
                for source, start, terms in items
                for term in range(terms)
            ]
            multiply_left(groups, lefts, live_psi.at[block], after_left)
            apply_operators(0, groups, spread_ops, after_left, targets)

        by_live_rows(own_rows, width // TILE, multiply)

    each_live_block(half, slots, scalars, work)


def resident(count):
    return [pl.BlockSpec(memory_space=pltpu.VMEM)] * count


def in_smem(count):
    return [pl.BlockSpec(memory_space=pltpu.SMEM)] * count


def left_call(first, scalars, held, items, shape, psi, payloads, afters):
    blocks, slots, states, width = shape
    groups, wide = width // TILE, states * TILE
    every = sum(terms for source, start, terms in items)
    fold_shape = jax.ShapeDtypeStruct((8, width), jnp.float32)
    out_shape = [
        jax.ShapeDtypeStruct((blocks, terms, groups, wide, width), jnp.bfloat16)
        for source, start, terms in items
    ] + [fold_shape]
    scratch = [
        pltpu.VMEM((every, wide, wide), jnp.bfloat16),
        pltpu.VMEM((every, groups, wide, width), jnp.bfloat16),
    ]
    if first:
        live_psi = jax.ShapeDtypeStruct((blocks, states, width, width), jnp.bfloat16)
        out_shape += [live_psi, fold_shape]
        scratch.append(pltpu.SemaphoreType.DMA((blocks,)))
    psi_spec = [pl.BlockSpec(memory_space=pltpu.HBM)] if first else resident(1)
    return pl.pallas_call(
        functools.partial(
            left_kernel, first, held, items, len(payloads), len(afters), blocks // slots, slots
        ),
        in_specs=in_smem(len(scalars))
        + [pl.BlockSpec(memory_space=pl.ANY)] * len(afters)
        + psi_spec
        + resident(len(payloads)),
        out_specs=resident(len(out_shape)),
        out_shape=out_shape,
        scratch_shapes=scratch,
        compiler_params=pltpu.CompilerParams(
            vmem_limit_bytes=max(
                28 * MIB if first else 0,
                SPARE + 2 * every * (wide * wide + groups * wide * width),
            )
        ),
        cost_estimate=pl.CostEstimate(
            flops=psi.size * every * (width + wide) // HASTE,
            bytes_accessed=psi.size // HASTE,
            transcendentals=0,
        ),
        name="left",
    )(*scalars, *afters, psi, *payloads)


def stack_kernel(start, near_ref, received_ref, both_ref):
    terms = both_ref.shape[2] if len(both_ref.shape) == 5 else None
    for side, ref in enumerate((near_ref, received_ref)):
        both_ref[side] = ref[...] if start is None else ref[:, start : start + terms]


def stack_call(near, received, chunk=None):
    start, terms = chunk or (None, None)
    shape = near.shape if chunk is None else (near.shape[0], terms) + near.shape[2:]
    return pl.pallas_call(
        functools.partial(stack_kernel, start),
        in_specs=resident(2),
        out_specs=resident(1)[0],
        out_shape=jax.ShapeDtypeStruct((2,) + shape, near.dtype),
        compiler_params=pltpu.CompilerParams(vmem_limit_bytes=SPARE),
        cost_estimate=pl.CostEstimate(flops=0, bytes_accessed=4096, transcendentals=0),
        name="stack",
    )(near, received)


def choose_kernel(line, count, afters, half, slots, meta, places, partners, *rest):
    rest = rest[afters:]
    pieces, (mine_ref, other_ref) = rest[:count], rest[count:]
    sectors = pieces[0].shape[1]
    for part, out_ref in enumerate((mine_ref, other_ref)):
        for block in range(half * slots):
            sector = places[(meta[1] ^ part) * half + block // slots]
            partner = partners[sector, block % slots]
            away = meta[3] ^ (partner // sectors)
            piece, side = away // 2, away & 1
            if line:
                inner = ((meta[3] + 1) & 2) // 2
                side = side ^ (piece & inner)
                piece = piece + (piece & (1 - inner))
            place = lax.rem(partner, sectors)
            for at in range(count):
                @pl.when(piece == at)
                def _(at=at, side=side, place=place, block=block, out_ref=out_ref):
                    out_ref[block] = pieces[at][side, place]


def choose_call(line, scalars, half, slots, pieces, afters):
    meta, places, _, partners, _ = scalars
    terms, width = pieces[0].shape[2:4]
    chosen = jax.ShapeDtypeStruct((half * slots, terms, width, width), jnp.bfloat16)
    return pl.pallas_call(
        functools.partial(choose_kernel, line, len(pieces), len(afters), half, slots),
        in_specs=in_smem(3)
        + [pl.BlockSpec(memory_space=pl.ANY)] * len(afters)
        + resident(len(pieces)),
        out_specs=resident(2),
        out_shape=[chosen, chosen],
        compiler_params=pltpu.CompilerParams(vmem_limit_bytes=SPARE),
        cost_estimate=pl.CostEstimate(flops=0, bytes_accessed=4096, transcendentals=0),
        name="choose",
    )(meta, places, partners, *afters, *pieces)


def chunk_kernel(first, last, held, chunk, ahead, late, count, half, slots,
                 meta, places, sector_rows, partners, counts, after_ref, psi_ref, *rest):
    start, terms = chunk
    early_refs, rest = rest[: len(ahead)], rest[len(ahead) :]
    payloads, rest = rest[:count], rest[count:]
    near_rights, rest = rest[:2], rest[2:]
    devices = len(ahead) + len(late)
    far_rights, rest = rest[: devices // 2 - 1], rest[devices // 2 - 1 :]
    if not first:
        sum_in, rest = rest[0], rest[1:]
    sum_out, fold_ref, *rest = rest
    if late:
        spread_ops, after_left, after_ops, *rest = rest
    states, width = psi_ref.shape[1], psi_ref.shape[-1]
    groups = width // TILE
    views = dict(zip(late, source_views(payloads)))
    rights = list(near_rights) + [right.at[side] for right in far_rights for side in (0, 1)]
    for at, source in enumerate(late):
        operators = views[source][half * held * width :, :]
        spread_operators(operators, range(start, start + terms), spread_ops, at * terms, states)
    fold_ref[...] = jnp.zeros_like(fold_ref)
    if last:
        sum_out[...] = jnp.zeros_like(sum_out)

    def work(block, place, sector, own_rows, partner_rows):
        total = rest[0] if last else sum_out.at[block]
        columns = [
            jnp.concatenate(
                [rights[pair + at][block, term] for at in range(2) for term in range(terms)],
                axis=0,
            )
            for pair in range(0, devices, 2)
        ]

        def operated(device, term, group):
            if device in ahead:
                return early_refs[ahead.index(device)][block, term, group]
            return after_ops[late.index(device) * terms + term, group]

        def multiply(live_groups):
            if late:
                lefts = [
                    term_rows(views[source], place, held, start + term, live_groups * TILE)
                    for source in late
                    for term in range(terms)
                ]
                multiply_left(live_groups, lefts, psi_ref.at[block], after_left)
            targets = [(after_ops, (term,)) for term in range(len(late) * terms)]
            for group in range(0, live_groups, 2 * WIDE):
                sides = min(2 * WIDE, live_groups - group)
                if late:
                    apply_operators(group, group + sides, spread_ops, after_left, targets)
                parts = []
                for pair in range(0, devices, 2):
                    rows = jnp.concatenate(
                        [
                            jnp.concatenate(
                                [
                                    operated(pair + at, term, group + side)
                                    for at in range(2)
                                    for term in range(terms)
                                ],
                                axis=1,
                            )
                            for side in range(sides)
                        ],
                        axis=0,
                    )
                    parts.append(
                        jnp.dot(rows, columns[pair // 2], preferred_element_type=jnp.float32)
                    )
                while len(parts) > 1:
                    parts = [parts[at] + parts[at + 1] for at in range(0, len(parts), 2)]
                done = parts[0].reshape(sides, states, TILE, width)
                for side in range(sides):
                    tile = slice((group + side) * TILE, (group + side + 1) * TILE)
                    if first:
                        total[:, tile, :] = done[side]
                    else:
                        total[:, tile, :] = sum_in[block, :, tile, :] + done[side]

        by_live_rows(own_rows, groups, multiply)
        if last:
            mask = live_entries(own_rows, partner_rows, width)
            kept = jnp.where(mask, total[...], 0.0)
            fold_ref[...] += folded(kept * psi_ref[block].astype(jnp.float32))
            sum_out[block] = kept.astype(jnp.bfloat16)

    each_live_block(half, slots, (meta, places, sector_rows, partners, counts), work)


def chunk_call(first, last, held, chunk, ahead, late, scalars, slots, psi, early, payloads,
               rights, total, after):
    blocks, states, width = psi.shape[:3]
    groups, wide = width // TILE, states * TILE
    start, terms = chunk
    operands = [after, psi, *early, *payloads, *rights]
    aliases = {}
    if not first:
        operands.append(total)
        if not last:
            aliases = {len(scalars) + len(operands) - 1: 0}
    sum_dtype = jnp.bfloat16 if last else jnp.float32
    every = len(late) * terms
    scratch = []
    if late:
        scratch += [
            pltpu.VMEM((every, wide, wide), jnp.bfloat16),
            pltpu.VMEM((every, groups, wide, width), jnp.bfloat16),
            pltpu.VMEM((every, groups, wide, width), jnp.bfloat16),
        ]
    if last:
        scratch.append(pltpu.VMEM((states, width, width), jnp.float32))
    work = psi.size * terms * ((len(ahead) + len(late)) * width + len(late) * (width + wide))
    return pl.pallas_call(
        functools.partial(
            chunk_kernel, first, last, held, chunk, ahead, late, len(payloads),
            blocks // slots, slots,
        ),
        in_specs=in_smem(len(scalars))
        + [pl.BlockSpec(memory_space=pl.ANY)]
        + resident(len(operands) - 1),
        out_specs=resident(2),
        out_shape=[
            jax.ShapeDtypeStruct(psi.shape, sum_dtype),
            jax.ShapeDtypeStruct((8, width), jnp.float32),
        ],
        scratch_shapes=scratch,
        input_output_aliases=aliases,
        compiler_params=pltpu.CompilerParams(
            vmem_limit_bytes=(len(ahead) + len(late)) * SPARE // 4
            + 2 * every * wide * (wide + 2 * groups * width)
            + 4 * int(last) * states * width * width
        ),
        cost_estimate=pl.CostEstimate(
            flops=work // HASTE, bytes_accessed=psi.size // HASTE, transcendentals=0
        ),
        name="chunk",
    )(*scalars, *operands)


def residual_kernel(half, slots, meta, places, sector_rows, partners, counts,
                    folds_ref, live_psi, own_ref, other_ref, psi_ref, out_ref, quotient_ref,
                    other_psi, staged, read_sems, write_sems):
    scalars = (meta, places, sector_rows, partners, counts)
    blocks, width = own_ref.shape[0], own_ref.shape[-1]
    depth = staged.shape[0]

    def where(block, side):
        index = (meta[1] ^ side) * half + block // slots
        return places[index], block % slots, index

    def read(block):
        sector, slot, _ = where(block, 1)
        return pltpu.make_async_copy(
            psi_ref.at[sector, slot], other_psi.at[block], read_sems.at[block]
        )

    def write(step):
        sector, slot, _ = where(step % blocks, step // blocks)
        return pltpu.make_async_copy(
            staged.at[step % depth], out_ref.at[sector, slot], write_sems.at[step % depth]
        )

    for block in range(blocks):
        read(block).start()
    quotient = jnp.sum(folds_ref[0:8, :]) / jnp.sum(folds_ref[8:16, :])
    quotient_ref[0] = quotient
    for step in range(2 * blocks):
        block, side = step % blocks, step // blocks
        if step >= depth:
            write(step - depth).wait()
        sector, slot, index = where(block, side)
        _, live, own_rows, partner_rows = block_facts(scalars, index, slot)
        mask = live_entries(jnp.where(live, own_rows, 0), partner_rows, width)
        if side:
            read(block).wait()
            values, sums = other_psi[block], other_ref[block]
        else:
            values, sums = live_psi[block], own_ref[block]
        scaled = quotient * jnp.where(mask, values.astype(jnp.float32), 0.0)
        staged[step % depth] = (sums.astype(jnp.float32) - scaled).astype(jnp.bfloat16)
        write(step).start()
    for step in range(2 * blocks - min(depth, 2 * blocks), 2 * blocks):
        write(step).wait()


def residual_call(scalars, folds, psi, live_psi, own, other):
    sectors, slots, states, width = psi.shape[:4]
    blocks = own.shape[0]
    depth = 4
    in_hbm = [pl.BlockSpec(memory_space=pltpu.HBM)]
    return pl.pallas_call(
        functools.partial(residual_kernel, sectors // 2, slots),
        in_specs=in_smem(len(scalars)) + resident(4) + in_hbm,
        out_specs=in_hbm + in_smem(1),
        out_shape=[
            jax.ShapeDtypeStruct(psi.shape, jnp.bfloat16),
            jax.ShapeDtypeStruct((1,), jnp.float32),
        ],
        scratch_shapes=[
            pltpu.VMEM((blocks, states, width, width), jnp.bfloat16),
            pltpu.VMEM((depth, states, width, width), jnp.bfloat16),
            pltpu.SemaphoreType.DMA((blocks,)),
            pltpu.SemaphoreType.DMA((depth,)),
        ],
        compiler_params=pltpu.CompilerParams(vmem_limit_bytes=41 * MIB),
        cost_estimate=pl.CostEstimate(
            flops=3 * psi.size, bytes_accessed=6 * psi.size, transcendentals=0
        ),
        name="residual",
    )(*scalars, folds, live_psi, own, other, psi)


def on_device(
    devices, rings, psi, left_env, right_env, local_ops, term_op, sector_rows, block_partner,
    block_count,
):
    sectors, slots, states, width = psi.shape[:4]
    terms = left_env.shape[1]
    half = sectors // 2
    me = lax.axis_index("term")
    ring = lax.axis_index("sec")
    core = me % 2
    meta = jnp.stack([ring * sectors, core, me, ring]).astype(jnp.int32)

    near_rows = lax.dynamic_slice_in_dim(sector_rows, ring * sectors, sectors)
    weight = block_count * (near_rows + width // 2)
    order = jnp.arange(sectors, dtype=jnp.int32)
    ahead = (weight[None, :] > weight[:, None]) | (
        (weight[None, :] == weight[:, None]) & (order[None, :] < order[:, None])
    )
    rank = jnp.sum(ahead.astype(jnp.int32), axis=1)
    index = ((rank ^ (rank >> 1)) & 1) * half + (rank >> 1)
    places = jnp.sum(jnp.where(index[None, :] == order[:, None], order[None, :], 0), axis=1)
    scalars = (meta, places, sector_rows, block_partner, block_count)

    def swap(value, bits, axis="term", size=devices):
        return lax.ppermute(value, axis, [(i, i ^ bits) for i in range(size)])

    def to_far_chips(near, received):
        both = stack_call(near, received)
        return both, [swap(both, bits) for bits in range(2, devices, 2)]

    chunks = [(at, 1) for at in range(terms)]
    ordered = jnp.roll(places, -core * half)
    parcels = [chunks[0], (chunks[0][1], terms - chunks[0][1])]
    mine, theirs, *shares = pack_call(
        parcels, ordered, term_op, local_ops, left_env, right_env
    )
    near_left = swap(theirs, 1)
    both_lefts, far_lefts = to_far_chips(mine, near_left)

    shards, rights = [], []
    swapped = [swap(share, 1, "sec", rings) for share in shares]
    line = rings == 4

    def gather():
        at = len(shards)
        if at == 0:
            pair = stack_call(shares[0], swapped[0])
        else:
            start, length = chunks[at]
            pair = stack_call(shares[1], swapped[1], (start - parcels[1][0], length))
        pieces = [pair]
        if line:
            pieces.append(lax.ppermute(pair, "sec", [(1, 2), (2, 1)]))
        bits = 2
        while bits < rings and not line:
            pieces = pieces + [swap(piece, bits, "sec", rings) for piece in pieces]
            bits *= 2
        shards.append(pieces)

    def choose(token):
        at = len(rights)
        afters = [token] + (rights[-1][2:] if rights else far_lefts)
        if 0 < at < len(chunks) - 1:
            afters.append(shards[at + 1][-1])
        pieces = shards[at]
        if line:
            pieces = pieces + [lax.ppermute(pieces[-1], "sec", [(1, 0), (2, 3)])]
        mine, other = choose_call(line, scalars, half, slots, pieces, afters)
        received = swap(other, 1)
        if at < len(chunks) - 1:
            both, far_rights = to_far_chips(mine, received)
        else:
            both = mine
            far_rights = [
                stack_call(swap(mine, bits), swap(other, bits + 1))
                for bits in range(2, devices, 2)
            ]
        rights.append([mine, received] + far_rights)
        return both

    products = {}
    shape = (half * slots, slots, states, width)
    far = tuple(range(2, devices))

    def go_left(sources, which, token, first=False, waits=()):
        items = [(source, *chunks[at]) for at in which for source in sources]
        near = [source for source in sources if source < 2]
        payloads = [(mine, near_left)[source] for source in near]
        if len(near) < len(sources):
            payloads += far_lefts
        renamed = [(sources.index(source), start, count) for source, start, count in items]
        outs = left_call(
            first, scalars, terms, renamed, shape, psi if first else live_psi, payloads,
            [token, *waits],
        )
        for at, out in zip([(at, source) for at in which for source in sources], outs):
            products[at] = out
        return outs[len(items) :]

    every = range(len(chunks))
    gather()
    token, live_psi, squares = go_left((0,), every, both_lefts, True)
    shards[0][-1], shares[1], swapped[1], _ = lax.optimization_barrier(
        (shards[0][-1], shares[1], swapped[1], token)
    )
    for chunk in chunks[1:]:
        gather()
    token, = go_left((1,), every[1:], token)
    token = choose(token)
    token, = go_left(far, [len(chunks) - 1], token)
    total = None
    for at, chunk in enumerate(chunks):
        last = at == len(chunks) - 1
        if len(rights) < len(chunks):
            token = choose(token)
        ahead = tuple(source for source in range(devices) if (at, source) in products)
        late = tuple(source for source in range(devices) if source not in ahead)
        payloads = ([near_left] if 1 in late else []) + (far_lefts if late else [])
        total, token = chunk_call(
            at == 0, last, terms, chunk, ahead, late, scalars, slots, live_psi,
            [products.pop((at, source)) for source in ahead], payloads,
            rights[at], total, token,
        )

    other = swap(total, 1)
    folds = jnp.concatenate([token, squares], axis=0)
    parts = [folds] + [swap(folds, bits, "sec", rings) for bits in range(1, rings)]
    while len(parts) > 1:
        parts = [parts[at] + parts[at + 1] for at in range(0, len(parts), 2)]
    folds = parts[0]
    folds = folds + swap(folds, 1)
    residual, rayleigh = residual_call(scalars, folds, psi, live_psi, total, other)
    return residual, rayleigh


def solution(mesh):
    placed = (
        P(("groups", "sec"), None, None, None, None),
        P(("groups", "sec"), "term", None, None),
        P(("groups", "sec"), "term", None, None),
        P(),
        P("term"),
        P("groups"),
        P(("groups", "sec"), None),
        P(("groups", "sec")),
    )
    return jax.shard_map(
        functools.partial(on_device, mesh.shape["term"], mesh.shape["sec"]),
        mesh=mesh,
        in_specs=placed,
        out_specs=(P(("groups", "sec"), None, None, None, None), P("groups")),
        check_vma=False,
    )
```
